32 devices in a mesh: row: 8 (over y, x, core), col: 4 (over z).
Axes of the slice: x: 2, y: 2, z: 4, core: 2. Of those that a mesh axis runs over, the one named last changes fastest.
Arguments:
- inputs: bfloat16 [8192, 1536], P(('row', 'col')), may hold values from -6 to 6
- text_states: bfloat16 [8, 64, 1536], P('row', 'col'), may hold values from -6 to 6
- cotangent: float32 [8192, 1536], P(('row', 'col')), may hold values from -6 to 6
- norm_gains: float32 [2, 3, 1536], replicated, may hold values from 0.25 to 1.75
- norm_shifts: float32 [2, 3, 1536], replicated, may hold values from -3 to 3
- self_query: bfloat16 [2, 1536, 1536], P(None, 'row', 'col'), may hold values from -0.15625 to 0.15625
- self_key: bfloat16 [2, 1536, 1536], P(None, 'row', 'col'), may hold values from -0.15625 to 0.15625
- self_value: bfloat16 [2, 1536, 1536], P(None, 'row', 'col'), may hold values from -0.15625 to 0.15625
- self_out: bfloat16 [2, 1536, 1536], P(None, 'row', 'col'), may hold values from -1.75 to 1.75
- cross_query: bfloat16 [2, 1536, 1536], P(None, 'row', 'col'), may hold values from -0.15625 to 0.15625
- cross_key: bfloat16 [2, 1536, 1536], P(None, 'row', 'col'), may hold values from -0.15625 to 0.15625
- cross_value: bfloat16 [2, 1536, 1536], P(None, 'row', 'col'), may hold values from -0.15625 to 0.15625
- cross_out: bfloat16 [2, 1536, 1536], P(None, 'row', 'col'), may hold values from -0.4375 to 0.4375
- mlp_up: bfloat16 [2, 1536, 6144], P(None, 'row', 'col'), may hold values from -0.15625 to 0.15625
- mlp_down: bfloat16 [2, 1536, 6144], P(None, 'row', 'col'), may hold values from -0.078125 to 0.078125
Outputs:
- output: float32 [8192, 1536], P(('row', 'col'))
- input_grad: float32 [8192, 1536], P(('row', 'col'))
- text_grad: float32 [8, 64, 1536], P('row', 'col')
- norm_gains_grad: float32 [2, 3, 1536], replicated
- norm_shifts_grad: float32 [2, 2, 1536], replicated
- self_norm_shift_grad: float32 [2, 1536], replicated
- self_query_grad: float32 [2, 1536, 1536], P(None, 'row', 'col')
- self_key_grad: float32 [2, 1536, 1536], P(None, 'row', 'col')
- self_value_grad: float32 [2, 1536, 1536], P(None, 'row', 'col')
- self_out_grad: float32 [2, 1536, 1536], P(None, 'row', 'col')
- cross_query_grad: float32 [2, 1536, 1536], P(None, 'row', 'col')
- cross_key_grad: float32 [2, 1536, 1536], P(None, 'row', 'col')
- cross_value_grad: float32 [2, 1536, 1536], P(None, 'row', 'col')
- cross_out_grad: float32 [2, 1536, 1536], P(None, 'row', 'col')
- mlp_up_grad: float32 [2, 1536, 6144], P(None, 'row', 'col')
- mlp_down_grad: float32 [2, 1536, 6144], P(None, 'row', 'col')
The draws below stay inside these ranges and needn't reach their ends.
All inputs are finite; a program needn't handle non-finite values.
Results may differ from the reference program's by a relative error of at most 0.024.
Values may be sent and summed in bfloat16 or wider, within the bound.
No kernel may reach another device: no remote copies, remote signals or barrier semaphores. Data moves between devices by JAX's collectives and lax.ppermute only.
A program may use at most 320 MiB of HBM per device.

```python
import jax
import jax.numpy as jnp
from jax import lax

D = 1536
HEADS = 24
HEAD = 64
FF = 6144
TEXT = 64
CLIP_LEN = 1024
LAYERS = 2
CLIPS = 8
TOKENS = 8192


def shard_levels(own_key, extent, shards, low, largest):
    factor_of, own = 1.0, jax.random.fold_in(own_key, 6)
    for axis_at, shards_of in shards:
        steps = jnp.exp(jax.random.uniform(jax.random.fold_in(own, axis_at), (shards_of,), jnp.float32, low / len(shards), largest / len(shards)))
        factor_of = factor_of * jnp.repeat(steps, extent[axis_at] // shards_of).reshape([-1 if axis == axis_at else 1 for axis in range(len(extent))])
    return factor_of


def bell_draw(key, extent, deviation, reach, pieces=(), kind=jnp.bfloat16):
    values = jax.random.normal(key, extent, jnp.float32) * deviation
    if len(pieces) > 0:
        values = shard_levels(key, extent, pieces, -0.22, 0.18) * values
    return jnp.clip(values, min=-reach, max=reach).astype(kind)


def setup_inputs(seed: int = 0) -> dict:
    arg_keys = jax.random.split(jax.random.key(seed), 16)
    return {
        "inputs": bell_draw(arg_keys[0], (TOKENS, D), 1.0, 6.0, ((0, 32),)),
        "text_states": bell_draw(arg_keys[1], (CLIPS, TEXT, D), 1.0, 6.0, ((0, 8), (1, 4))),
        "cotangent": bell_draw(arg_keys[2], (TOKENS, D), 1.0, 6.0, ((0, 32),), jnp.float32),
        "norm_gains": jnp.clip(1.0 + 0.15 * jax.random.normal(arg_keys[3], (LAYERS, 3, D), jnp.float32), 0.25, 1.75),
        "norm_shifts": bell_draw(arg_keys[4], (LAYERS, 3, D), 0.5, 3.0, (), jnp.float32),
        "self_query": bell_draw(arg_keys[5], (LAYERS, D, D), D ** -0.5, 0.15625, ((1, 8), (2, 4))),
        "self_key": bell_draw(arg_keys[6], (LAYERS, D, D), D ** -0.5, 0.15625, ((1, 8), (2, 4))),
        "self_value": bell_draw(arg_keys[7], (LAYERS, D, D), D ** -0.5, 0.15625, ((1, 8), (2, 4))),
        "self_out": bell_draw(arg_keys[8], (LAYERS, D, D), (D * 8 // CLIP_LEN) ** -0.5, 1.75, ((1, 8), (2, 4))),
        "cross_query": bell_draw(arg_keys[9], (LAYERS, D, D), D ** -0.5, 0.15625, ((1, 8), (2, 4))),
        "cross_key": bell_draw(arg_keys[10], (LAYERS, D, D), D ** -0.5, 0.15625, ((1, 8), (2, 4))),
        "cross_value": bell_draw(arg_keys[11], (LAYERS, D, D), D ** -0.5, 0.15625, ((1, 8), (2, 4))),
        "cross_out": bell_draw(arg_keys[12], (LAYERS, D, D), (D * 8 // TEXT) ** -0.5, 0.4375, ((1, 8), (2, 4))),
        "mlp_up": bell_draw(arg_keys[13], (LAYERS, D, FF), D ** -0.5, 0.15625, ((1, 8), (2, 4))),
        "mlp_down": bell_draw(arg_keys[14], (LAYERS, D, FF), FF ** -0.5, 0.078125, ((1, 8), (2, 4))),
    }


@jax.custom_vjp
def low(v):
    return lax.optimization_barrier(v.astype(jnp.bfloat16)).astype(jnp.float32)

@jax.custom_vjp
def low_back(v):
    return v

def low_keep(v):
    return (low(v), None)

def low_pass(kept, grad):
    return (grad,)

def back_keep(v):
    return (v, None)

def back_low(kept, grad):
    return (low(grad),)
low.defvjp(low_keep, low_pass)
low_back.defvjp(back_keep, back_low)
HIGH = lax.Precision.HIGHEST
EPS = 1e-05
NEG = -1e+30
SCALE = 0.125

def matmul_high(left, right):
    return jnp.dot(left, right, precision=HIGH, preferred_element_type=jnp.float32)

def layer_norm(values_in, gain, shift):
    row_mean = lax.optimization_barrier(jnp.mean(values_in, axis=-1, keepdims=True))
    centered = values_in - row_mean
    variance = lax.optimization_barrier(jnp.mean(centered * centered, axis=-1, keepdims=True))
    return centered * lax.rsqrt(variance + EPS) * gain + shift

def softmax_rows(scores):
    row_max = lax.optimization_barrier(jnp.max(scores, axis=-1, keepdims=True))
    shifted = jnp.exp(scores - row_max)
    return shifted / lax.optimization_barrier(jnp.sum(shifted, axis=-1, keepdims=True))

def clip_attention(queries, keys_all, values_all, causal):
    scores = jnp.einsum('qhd,khd->hqk', queries, keys_all, precision=HIGH) * SCALE
    scores = low_back(scores)
    if causal:
        row_ids = lax.broadcasted_iota(jnp.int32, (queries.shape[0], keys_all.shape[0]), 0)
        key_ids = lax.broadcasted_iota(jnp.int32, (queries.shape[0], keys_all.shape[0]), 1)
        scores = jnp.where((key_ids <= row_ids)[None], scores, NEG)
    attn_probs = low(softmax_rows(scores))
    return jnp.einsum('hqk,khd->qhd', attn_probs, values_all, precision=HIGH)

def attention_all(queries, keys_all, values_all, key_rows, causal):

    def one_clip(clip_args):
        return clip_attention(clip_args[0], clip_args[1], clip_args[2], causal)
    shaped = (queries.reshape(-1, CLIP_LEN, HEADS, HEAD), keys_all.reshape(-1, key_rows, HEADS, HEAD), values_all.reshape(-1, key_rows, HEADS, HEAD))
    mapped = lax.map(jax.checkpoint(one_clip), shaped)
    return mapped.reshape(-1, D)

def forward(residual, text_rows, norm_gains, norm_shifts, self_query, self_key, self_value, self_out, cross_query, cross_key, cross_value, cross_out, mlp_up, mlp_down):
    for layer_index in range(LAYERS):
        normed = low(layer_norm(residual, norm_gains[layer_index, 0], norm_shifts[layer_index, 0]))
        queries = low(low_back(matmul_high(normed, self_query[layer_index])))
        keys_self = low(low_back(matmul_high(normed, self_key[layer_index])))
        values_self = low(low_back(matmul_high(normed, self_value[layer_index])))
        attn_out = low(low_back(attention_all(queries, keys_self, values_self, CLIP_LEN, True)))
        residual = residual + low_back(matmul_high(attn_out, self_out[layer_index].T))
        normed = low(layer_norm(residual, norm_gains[layer_index, 1], norm_shifts[layer_index, 1]))
        cross_queries = low(low_back(matmul_high(normed, cross_query[layer_index])))
        cross_keys = low(low_back(matmul_high(text_rows, cross_key[layer_index])))
        cross_values = low(low_back(matmul_high(text_rows, cross_value[layer_index])))
        cross_att = low(low_back(attention_all(cross_queries, cross_keys, cross_values, TEXT, False)))
        residual = residual + low_back(matmul_high(cross_att, cross_out[layer_index].T))
        normed = low(layer_norm(residual, norm_gains[layer_index, 2], norm_shifts[layer_index, 2]))
        hidden_pre = low_back(matmul_high(normed, mlp_up[layer_index]))
        hidden_act = low(jax.nn.gelu(hidden_pre, approximate=False))
        residual = residual + low_back(matmul_high(hidden_act, mlp_down[layer_index].T))
    return residual

def reference(inputs, text_states, cotangent, norm_gains, norm_shifts, self_query, self_key, self_value, self_out, cross_query, cross_key, cross_value, cross_out, mlp_up, mlp_down):
    primals = tuple((member.astype(jnp.float32) for member in (inputs, text_states.reshape(-1, D), norm_gains, norm_shifts, self_query, self_key, self_value, self_out, cross_query, cross_key, cross_value, cross_out, mlp_up, mlp_down)))
    output, pullback = jax.vjp(forward, *primals)
    grads = pullback(cotangent.astype(jnp.float32))
    return (output, grads[0], grads[1].reshape(text_states.shape), grads[2], grads[3][:, 1:], grads[3][:, 0], grads[4], grads[5], grads[6], grads[7], grads[8], grads[9], grads[10], grads[11], grads[12], grads[13])
```

```python
import functools

import jax
import jax.numpy as jnp
from jax import lax
from jax.experimental import pallas as pl
from jax.experimental.pallas import tpu as pltpu
from jax.sharding import PartitionSpec as P

HEAD = 64
CLIP_LEN = 1024
LAYERS = 2
SCALE = 0.125
EPS = 1e-05
NEG = -1e30
BF = jnp.bfloat16
F32 = jnp.float32
VMEM_LIMIT = 48 * 2**20
COST = CLIP_LEN * CLIP_LEN * 8


def product(left, right):
    return jnp.dot(left, right, preferred_element_type=F32)


def product_tn(left, right):
    return lax.dot_general(left, right, (((0,), (0,)), ((), ())), preferred_element_type=F32)


def product_nt(left, right):
    return lax.dot_general(left, right, (((1,), (1,)), ((), ())), preferred_element_type=F32)


def after(value, token):
    return lax.optimization_barrier((value, token))[0]


class Grid:
    def __init__(self, mesh):
        self.R = mesh.shape["row"]
        self.C = mesh.shape["col"]
        self.T = self.R // 2
        assert self.T == self.C
        self.groups = [[2 * i + core for i in range(self.T)] for core in range(2)]

    def at(self):
        row = lax.axis_index("row")
        self.i = row // 2
        self.core = row % 2
        self.z = lax.axis_index("col")

    def swap(self, value, d):
        return lax.ppermute(value, "row", [(r, r ^ (2 * d)) for r in range(self.R)])

    def core_swap(self, value):
        return lax.ppermute(value, "row", [(r, r ^ 1) for r in range(self.R)])

    def plane_a2a(self, value):
        return lax.all_to_all(value, "row", 0, 0, tiled=True, axis_index_groups=self.groups)

    def row_a2a(self, value):
        return lax.all_to_all(value, "row", 0, 0, tiled=True)

    def col_a2a(self, value):
        return lax.all_to_all(value, "col", 0, 0, tiled=True)

    def distances(self):
        return sorted(range(1, self.T), key=lambda d: (bin(d).count("1"), d))

    def gather(self, own):
        half = own.shape[0] // 2
        pieces = {0: own}
        for d in self.distances():
            high = 1 << (d.bit_length() - 1)
            low = d & -d
            if high == low:
                pieces[d] = self.swap(own, d)
            else:
                pieces[d] = jnp.concatenate(
                    [self.swap(pieces[d ^ high][:half], high), self.swap(pieces[d ^ low][half:], low)], axis=0
                )
        return [pieces[d] for d in range(self.T)]

    def scatter(self, terms):
        held = {}
        extra = {}
        half = None
        for d in reversed(self.distances()):
            term = terms[d]()
            half = term.shape[0] // 2
            for lower, upper in extra.get(d, []):
                term = term + jnp.concatenate([lower, upper], axis=0)
            sent = term.astype(BF)
            high = 1 << (d.bit_length() - 1)
            low = d & -d
            if high == low:
                held[d] = self.swap(sent, d).astype(F32)
            else:
                first = self.swap(sent[:half], high).astype(F32)
                second = self.swap(sent[half:], low).astype(F32)
                extra.setdefault(d ^ high, []).append((first, jnp.zeros_like(second)))
                extra.setdefault(d ^ low, []).append((jnp.zeros_like(first), second))
        total = terms[0]()
        for d in held:
            total = total + held[d]
        return total

    def natural(self, pieces):
        stacked = jnp.stack(pieces)
        return [lax.dynamic_index_in_dim(stacked, self.i ^ m, 0, keepdims=False) for m in range(self.T)]

    def tokens_in(self, block):
        rows, width = block.shape
        spread = self.plane_a2a(block.reshape(self.T, rows // self.T, width))
        return self.col_a2a(spread).reshape(rows, width)

    def tokens_out(self, block):
        rows, width = block.shape
        spread = self.col_a2a(block.reshape(self.C, rows // self.C, width))
        return self.plane_a2a(spread).reshape(rows, width)

    def total(self, value):
        for d in range(self.R.bit_length() - 1):
            value = value + lax.ppermute(value, "row", [(r, r ^ (1 << d)) for r in range(self.R)])
        for d in range(self.C.bit_length() - 1):
            value = value + lax.ppermute(value, "col", [(c, c ^ (1 << d)) for c in range(self.C)])
        return value

    def own_first(self, value):
        width = value.shape[-1]
        parts = value.reshape(value.shape[:-1] + (self.T, 2, width // self.R))
        even, odd = parts[..., 0, :], parts[..., 1, :]
        first = self.core == 0
        pair = [jnp.where(first, even, odd), jnp.where(first, odd, even)]
        return jnp.stack(pair, axis=-3).reshape(value.shape)

    def own_last(self, value):
        width = value.shape[-1]
        parts = value.reshape(value.shape[:-1] + (2, self.T, width // self.R))
        own, other = parts[..., 0, :, :], parts[..., 1, :, :]
        first = self.core == 0
        pair = [jnp.where(first, own, other), jnp.where(first, other, own)]
        return jnp.stack(pair, axis=-2).reshape(value.shape)


def gelu_parts(u):
    cdf = 0.5 * (1.0 + lax.erf(u * (0.5**0.5)))
    pdf = jnp.exp(-0.5 * u * u) * (0.5 / jnp.pi) ** 0.5
    return u * cdf, cdf + u * pdf


def norm_forward(residual, gain, shift):
    row_mean = jnp.mean(residual, axis=1, keepdims=True)
    centered = residual - row_mean
    variance = jnp.mean(centered * centered, axis=1, keepdims=True)
    inv_std = lax.rsqrt(variance + EPS)
    normed = centered * inv_std
    return (normed, inv_std, (normed * gain + shift).astype(BF))


def norm_backward(grad_out, normed, inv_std, gain):
    scaled = grad_out * gain
    row_mean = jnp.mean(scaled, axis=1, keepdims=True)
    row_along = jnp.mean(scaled * normed, axis=1, keepdims=True)
    grad_in = inv_std * (scaled - row_mean - normed * row_along)
    return (grad_in, jnp.sum(grad_out * normed, axis=0), jnp.sum(grad_out, axis=0))


def to_clip(grid, i, source, target):
    rows = CLIP_LEN // grid.T
    small = rows // grid.C
    for d in range(grid.T):
        for k in range(grid.C):
            start = pl.multiple_of((i ^ d) * small + k * rows, small)
            target[pl.ds(start, small), :] = source[d * rows + k * small : d * rows + (k + 1) * small, :]


def from_clip(grid, i, block, k, target, lanes):
    rows = CLIP_LEN // grid.T
    small = rows // grid.C
    for d in range(grid.T):
        start = pl.multiple_of((i ^ d) * small, small)
        target[d * rows + k * small : d * rows + (k + 1) * small, lanes] = block[pl.ds(start, small), :]


def causal_block(scores_t, size):
    keys = lax.broadcasted_iota(jnp.int32, (size, size), 0)
    asks = lax.broadcasted_iota(jnp.int32, (size, size), 1)
    last = scores_t.shape[0] - size
    edge = jnp.where(keys <= asks, scores_t[last:], NEG)
    return edge if last == 0 else jnp.concatenate([scores_t[:last], edge], axis=0)


def dot_nt(left, right):
    return lax.dot_general(left, right, (((1,), (1,)), ((), ())), preferred_element_type=F32)


def dot_nn(left, right):
    return lax.dot_general(left, right, (((1,), (0,)), ((), ())), preferred_element_type=F32)


def flip(value):
    return value.astype(F32).T


def self_forward_kernel(grid, units, width, i_ref, x_ref, out_ref, sums_ref, clip, block):
    i = i_ref[0]
    size = CLIP_LEN // grid.C
    to_clip(grid, i, x_ref, clip)
    for u in range(units):
        base = u * 3 * width
        heads = range(width // HEAD)
        keys = [clip[:, base + width + h * HEAD : base + width + (h + 1) * HEAD] for h in heads]
        values_t = [
            flip(clip[:, base + 2 * width + h * HEAD : base + 2 * width + (h + 1) * HEAD]).astype(BF) for h in heads
        ]
        for k in range(grid.C):
            low, high = k * size, (k + 1) * size
            outs = []
            for h in heads:
                asks = clip[low:high, base + h * HEAD : base + (h + 1) * HEAD] * BF(SCALE)
                scores = causal_block(dot_nt(keys[h][:high], asks), size)
                top = jnp.max(scores, axis=0, keepdims=True)
                weight = jnp.exp(scores - top)
                total = jnp.sum(weight, axis=0, keepdims=True)
                outs.append(dot_nn(values_t[h][:, :high], weight.astype(BF)) / total)
                sums_ref[u, h : h + 1, low:high] = top + jnp.log(total)
            both = outs[0] if len(outs) == 1 else jnp.concatenate(outs, axis=0)
            block[...] = both.T.astype(BF)
            from_clip(grid, i, block, k, out_ref, slice(u * width, (u + 1) * width))


def self_backward_kernel(grid, units, width, i_ref, x_ref, da_ref, sums_ref, out_ref, clip, da_clip, block, acc):
    i = i_ref[0]
    size = CLIP_LEN // grid.C
    to_clip(grid, i, x_ref, clip)
    to_clip(grid, i, da_ref, da_clip)
    for u in range(units):
        base = u * 3 * width
        heads = range(width // HEAD)
        lanes = lambda which, h: slice(base + which * width + h * HEAD, base + which * width + (h + 1) * HEAD)
        keys = [clip[:, lanes(1, h)] for h in heads]
        values = [clip[:, lanes(2, h)] for h in heads]
        keys_t = [flip(keys[h]).astype(BF) for h in heads]
        for k in reversed(range(grid.C)):
            low, high = k * size, (k + 1) * size
            dq = []
            for h in heads:
                asks = clip[low:high, lanes(0, h)] * BF(SCALE)
                da = da_clip[low:high, u * width + h * HEAD : u * width + (h + 1) * HEAD]
                scores = causal_block(dot_nt(keys[h][:high], asks), size)
                probs = jnp.exp(scores - sums_ref[u, h : h + 1, low:high])
                d_probs = dot_nt(values[h][:high], da)
                inner = jnp.sum(probs * d_probs, axis=0, keepdims=True)
                d_scores = (probs * (d_probs - inner)).astype(BF)
                dk = dot_nn(d_scores, asks)
                dv = dot_nn(probs.astype(BF), da)
                at_k, at_v = slice(h * HEAD, (h + 1) * HEAD), slice(width + h * HEAD, width + (h + 1) * HEAD)
                if k == grid.C - 1:
                    acc[:, at_k] = dk
                    acc[:, at_v] = dv
                else:
                    acc[:high, at_k] += dk
                    acc[:high, at_v] += dv
                dq.append(dot_nn(keys_t[h][:, :high], d_scores) * SCALE)
            both = dq[0] if len(dq) == 1 else jnp.concatenate(dq, axis=0)
            block[:, :width] = both.T.astype(BF)
            block[:, width:] = acc[low:high, :].astype(BF)
            from_clip(grid, i, block, k, out_ref, slice(base, base + 3 * width))


def self_specs(grid, units, width):
    per_step = 1 if width % 128 == 0 else units
    steps = units // per_step

    def spec(lanes):
        return pl.BlockSpec((CLIP_LEN, per_step * lanes), lambda n, i: (0, n))

    sums = pl.BlockSpec((per_step, 8, CLIP_LEN), lambda n, i: (n, 0, 0))
    return steps, per_step, spec, sums


def self_attention(grid, x, units, width):
    steps, per_step, spec, sums = self_specs(grid, units, width)
    size = CLIP_LEN // grid.C
    return pl.pallas_call(
        functools.partial(self_forward_kernel, grid, per_step, width),
        grid_spec=pltpu.PrefetchScalarGridSpec(
            num_scalar_prefetch=1,
            grid=(steps,),
            in_specs=[spec(3 * width)],
            out_specs=[spec(width), sums],
            scratch_shapes=[
                pltpu.VMEM((CLIP_LEN, per_step * 3 * width), BF),
                pltpu.VMEM((size, width), BF),
            ],
        ),
        out_shape=[
            jax.ShapeDtypeStruct((CLIP_LEN, units * width), BF),
            jax.ShapeDtypeStruct((units, 8, CLIP_LEN), F32),
        ],
        compiler_params=pltpu.CompilerParams(vmem_limit_bytes=VMEM_LIMIT),
        cost_estimate=pl.CostEstimate(
            flops=COST * units * width, bytes_accessed=CLIP_LEN * units * width * 8, transcendentals=0
        ),
        name="self_attention",
    )(grid.i.reshape(1), x)


def self_attention_grad(grid, x, da, sums_in, units, width):
    steps, per_step, spec, sums = self_specs(grid, units, width)
    size = CLIP_LEN // grid.C
    return pl.pallas_call(
        functools.partial(self_backward_kernel, grid, per_step, width),
        grid_spec=pltpu.PrefetchScalarGridSpec(
            num_scalar_prefetch=1,
            grid=(steps,),
            in_specs=[spec(3 * width), spec(width), sums],
            out_specs=spec(3 * width),
            scratch_shapes=[
                pltpu.VMEM((CLIP_LEN, per_step * 3 * width), BF),
                pltpu.VMEM((CLIP_LEN, per_step * width), BF),
                pltpu.VMEM((size, 3 * width), BF),
                pltpu.VMEM((CLIP_LEN, 2 * width), F32),
            ],
        ),
        out_shape=jax.ShapeDtypeStruct((CLIP_LEN, units * 3 * width), BF),
        compiler_params=pltpu.CompilerParams(vmem_limit_bytes=VMEM_LIMIT),
        cost_estimate=pl.CostEstimate(
            flops=3 * COST * units * width, bytes_accessed=CLIP_LEN * units * width * 16, transcendentals=0
        ),
        name="self_attention_grad",
    )(grid.i.reshape(1), x, da, sums_in)


def cross_scores(keys, asks):
    scores = dot_nt(keys, asks)
    top = jnp.max(scores, axis=0, keepdims=True)
    weight = jnp.exp(scores - top)
    return weight / jnp.sum(weight, axis=0, keepdims=True)


def cross_forward_kernel(q_ref, k_ref, v_ref, out_ref):
    for low in range(0, q_ref.shape[1], 2 * HEAD):
        pair = []
        for at in (slice(low, low + HEAD), slice(low + HEAD, low + 2 * HEAD)):
            probs = cross_scores(k_ref[:, at], q_ref[:, at] * BF(SCALE)).astype(BF)
            pair.append(dot_nn(flip(v_ref[:, at]).astype(BF), probs))
        out_ref[:, low : low + 2 * HEAD] = jnp.concatenate(pair, axis=0).T.astype(BF)


def cross_backward_kernel(q_ref, k_ref, v_ref, dc_ref, dq_ref, dk_ref, dv_ref):
    for low in range(0, q_ref.shape[1], 2 * HEAD):
        pair, dk, dv = [], [], []
        for at in (slice(low, low + HEAD), slice(low + HEAD, low + 2 * HEAD)):
            asks = q_ref[:, at] * BF(SCALE)
            probs = cross_scores(k_ref[:, at], asks)
            d_probs = dot_nt(v_ref[:, at], dc_ref[:, at])
            inner = jnp.sum(probs * d_probs, axis=0, keepdims=True)
            d_scores = (probs * (d_probs - inner)).astype(BF)
            dk.append(dot_nn(d_scores, asks))
            dv.append(dot_nn(probs.astype(BF), dc_ref[:, at]))
            pair.append(dot_nn(flip(k_ref[:, at]).astype(BF), d_scores) * SCALE)
        at = slice(low, low + 2 * HEAD)
        dq_ref[:, at] = jnp.concatenate(pair, axis=0).T.astype(BF)
        dk_ref[:, at] = jnp.concatenate(dk, axis=1)
        dv_ref[:, at] = jnp.concatenate(dv, axis=1)


def cross_call(kernel, name, arrays, outs):
    width = arrays[0].shape[1]
    lanes = 512 if width % 512 == 0 else width

    def spec(rows):
        return pl.BlockSpec((rows, lanes), lambda n: (0, n))

    return pl.pallas_call(
        kernel,
        grid=(width // lanes,),
        in_specs=[spec(a.shape[0]) for a in arrays],
        out_specs=[spec(rows) for rows, _ in outs],
        out_shape=[jax.ShapeDtypeStruct((rows, width), kind) for rows, kind in outs],
        compiler_params=pltpu.CompilerParams(vmem_limit_bytes=VMEM_LIMIT),
        cost_estimate=pl.CostEstimate(
            flops=arrays[0].shape[0] * arrays[1].shape[0] * width * 20, bytes_accessed=2**22, transcendentals=0
        ),
        name=name,
    )(*arrays)


def cross_attention(queries, keys, values):
    return cross_call(cross_forward_kernel, "cross_attention", [queries, keys, values], [(queries.shape[0], BF)])[0]


def cross_attention_grad(queries, keys, values, grad_out):
    outs = [(queries.shape[0], BF), (keys.shape[0], F32), (keys.shape[0], F32)]
    return cross_call(cross_backward_kernel, "cross_attention_grad", [queries, keys, values, grad_out], outs)


def head_units(grid, width):
    heads = width // HEAD
    per_unit = -(-heads // grid.T)
    assert heads % per_unit == 0
    return heads // per_unit, per_unit * HEAD


def self_weights(grid, mats, token):
    rows, width = mats[0].shape
    count = len(mats)
    units, wide = head_units(grid, width)
    slots = jnp.stack(mats).reshape(count, rows, units, wide).transpose(2, 0, 1, 3)
    slots = jnp.concatenate([slots, jnp.zeros((grid.T - units, count, rows, wide), BF)], axis=0)
    order = [lax.dynamic_index_in_dim(slots, (s - grid.z - 1) % grid.T, 0, keepdims=False) for s in range(grid.T)]
    moved = grid.plane_a2a(jnp.stack(order))
    moved = after(moved.transpose(1, 0, 2, 3).reshape(count, grid.T * rows, wide), token)
    token = lax.all_gather(moved, "col", axis=0)
    half = jnp.stack(
        [lax.dynamic_index_in_dim(token, (grid.i - 1 - m) % grid.T, 0, keepdims=False) for m in range(units)]
    )
    other = grid.core_swap(half)

    def columns(part):
        low = part[:, :3].transpose(2, 0, 1, 3).reshape(grid.T * rows, units * 3 * wide)
        return low, part[:, 3].transpose(1, 0, 2).reshape(grid.T * rows, units * wide)

    own_in, own_out = columns(half)
    other_in, other_out = columns(other)
    return (joined([own_in, other_in]), joined([own_out, other_out])), token


def core_sum(grid, low, axis=0):
    half = low.shape[axis] // 2
    keep = lax.slice_in_dim(low, 0, half, axis=axis)
    send = lax.slice_in_dim(low, half, 2 * half, axis=axis)
    return (keep.astype(F32) + grid.core_swap(send).astype(F32)).astype(BF)


def self_weights_grad(grid, low, rows, width):
    units, wide = head_units(grid, width)
    half = core_sum(grid, low, 1)
    half = jnp.concatenate([half, jnp.zeros((grid.C - units,) + half.shape[1:], BF)], axis=0)
    slots = jnp.stack(
        [lax.dynamic_index_in_dim(half, (grid.i - c - 1) % grid.T, 0, keepdims=False) for c in range(grid.C)]
    )
    summed = lax.psum_scatter(slots, "col", scatter_dimension=0)
    moved = grid.plane_a2a(summed.reshape(grid.T, rows, 4 * wide))
    mine = [
        lax.dynamic_index_in_dim(moved, (grid.z + 1 + m) % grid.T, 0, keepdims=False) for m in range(units)
    ]
    return [
        jnp.concatenate([part[:, n * wide : (n + 1) * wide] for part in mine], axis=1).astype(F32) for n in range(4)
    ]


def hidden_weights(grid, mats, token):
    rows, width = mats[0].shape
    count = len(mats)
    wide = width // grid.T
    slots = jnp.stack(mats).reshape(count, rows, grid.T, wide).transpose(2, 0, 1, 3)
    moved = grid.plane_a2a(after(slots, token))
    moved = moved.transpose(1, 0, 2, 3).reshape(count, grid.T * rows, wide)
    token = lax.all_gather(moved, "col", axis=0)
    other = grid.core_swap(token)

    def columns(part, n):
        return part[:, n].transpose(1, 0, 2).reshape(grid.T * rows, grid.C * wide)

    return [joined([columns(token, n), columns(other, n)]) for n in range(count)], token


def hidden_weights_grad(grid, low, rows, width):
    half = core_sum(grid, low, 1)
    summed = lax.psum_scatter(half, "col", scatter_dimension=0)
    moved = grid.plane_a2a(summed.reshape(grid.T, rows, width // grid.T))
    return moved.transpose(1, 0, 2).reshape(rows, width).astype(F32)


def cross_weights(grid, mats, token):
    rows, width = mats[0].shape
    count = len(mats)
    token = lax.all_gather(after(jnp.stack(mats), token), "col", axis=0)
    own = token.transpose(1, 2, 0, 3).reshape(count * rows, grid.C * width)
    half = jnp.stack(grid.natural(grid.gather(own)))
    half = half.reshape(grid.T, count, rows, grid.C * width).transpose(1, 0, 2, 3)
    half = half.reshape(count, grid.T * rows, grid.C * width)
    other = grid.core_swap(half)
    return [joined([half[n], other[n]]) for n in range(count)], token


def cross_weights_grad(grid, lows, rows, width):
    count = len(lows)
    halves = [core_sum(grid, low).reshape(grid.T, rows, grid.C * width) for low in lows]

    def term(d):
        parts = [lax.dynamic_index_in_dim(half, grid.i ^ d, 0, keepdims=False) for half in halves]
        return lambda: joined(parts).astype(F32)

    own = grid.scatter([term(d) for d in range(grid.T)]).astype(BF)
    own = own.reshape(count, rows, grid.C, width).transpose(2, 0, 1, 3)
    summed = lax.psum_scatter(own, "col", scatter_dimension=0).astype(F32)
    return [summed[n] for n in range(count)]


def text_columns(grid, text):
    _, own, width = text.shape
    parts = text.reshape(own, grid.R, width // grid.R).transpose(1, 0, 2)
    parts = grid.row_a2a(parts)
    pieces = [parts] + [
        lax.ppermute(parts, "col", [(c, c ^ d) for c in range(grid.C)]) for d in range(1, grid.C)
    ]
    stacked = jnp.stack(pieces)
    order = [lax.dynamic_index_in_dim(stacked, grid.z ^ c, 0, keepdims=False) for c in range(grid.C)]
    return jnp.stack(order, axis=1).reshape(-1, width // grid.R)


def text_forward(grid, columns, mats):
    count, rows, width = mats.shape
    own = columns.shape[0] // (grid.R * grid.C)
    part = product(columns, mats.transpose(1, 0, 2).reshape(rows, count * width)).astype(BF)
    part = part.reshape(grid.T, 2, grid.C, own, count * width).transpose(2, 1, 0, 3, 4)
    part = part.reshape(grid.R, grid.T * own, count * width)
    moved = grid.row_a2a(part).astype(F32)
    summed = jnp.sum(moved, axis=0).astype(BF).reshape(grid.T, own, count * width)
    moved = grid.col_a2a(summed)
    mine = moved.reshape(grid.C, own, count, width).transpose(1, 2, 0, 3)
    mine = mine.reshape(own, count * grid.C * width)
    full = jnp.concatenate(grid.gather(mine), axis=0)
    return full.reshape(-1, count, grid.C * width)


def text_backward(grid, grads, width):
    states = grads.shape[0]
    own = states // grid.T
    pieces = grads.reshape(grid.T, own, -1)
    mine = grid.scatter([lambda d=d: pieces[d] for d in range(grid.T)]).astype(BF)
    mine = mine.reshape(own, -1, grid.C, width).transpose(2, 0, 1, 3)
    moved = grid.col_a2a(mine)
    other = grid.core_swap(moved)
    pair = jnp.stack(
        [jnp.where(grid.core == 0, moved, other), jnp.where(grid.core == 0, other, moved)], axis=1
    )
    shape = pair.shape
    flat = pair.reshape(shape[0] * 2, -1)
    full = jnp.stack(grid.natural(grid.gather(flat)), axis=1)
    return full.reshape(-1, shape[3], width)


def text_out(grid, part):
    own = part.shape[0] // (grid.R * grid.C)
    cols = part.shape[1]
    parts = part.astype(BF).reshape(grid.R, grid.C, own, cols).transpose(1, 0, 2, 3)
    moved = grid.col_a2a(parts).astype(F32)
    summed = jnp.sum(moved, axis=0).astype(BF)
    moved = grid.row_a2a(summed)
    return moved.transpose(1, 0, 2).reshape(1, own, grid.R * cols).astype(F32)


def joined(pieces):
    return jnp.concatenate(pieces, axis=0)


def rows_of(grid, value, d):
    count = value.shape[0] // grid.T
    return value[d * count : (d + 1) * count]


def layer_forward(grid, residual, weights, text_pair, gains, shifts, units, wide):
    (w_qkv, w_out), w_cross, w_hidden = weights
    normed_one, inv_one, low_one = norm_forward(residual, gains[0], shifts[0])
    full_one = joined(grid.gather(low_one))
    qkv = product(full_one, w_qkv).astype(BF)
    attn_low, sums_self = self_attention(grid, qkv, units, wide)
    residual = residual + grid.scatter(
        [lambda d=d: product_nt(rows_of(grid, attn_low, d), w_out) for d in range(grid.T)]
    )
    normed_two, inv_two, low_two = norm_forward(residual, gains[1], shifts[1])
    cross_queries = product(low_two, w_cross[0]).astype(BF)
    cross_low = cross_attention(cross_queries, text_pair[0], text_pair[1])
    residual = residual + product_nt(cross_low, w_cross[1])
    normed_three, inv_three, low_three = norm_forward(residual, gains[2], shifts[2])
    full_three = joined(grid.gather(low_three))
    hidden, slope = gelu_parts(product(full_three, w_hidden[0]))
    hidden_low = hidden.astype(BF)
    hidden_slope = slope.astype(BF)
    residual = residual + grid.scatter(
        [lambda d=d: product_nt(rows_of(grid, hidden_low, d), w_hidden[1]) for d in range(grid.T)]
    )
    stored = dict(
        normed_one=normed_one,
        inv_one=inv_one,
        full_one=full_one,
        qkv=qkv,
        attn_low=attn_low,
        sums_self=sums_self,
        normed_two=normed_two,
        inv_two=inv_two,
        low_two=low_two,
        cross_queries=cross_queries,
        cross_low=cross_low,
        normed_three=normed_three,
        inv_three=inv_three,
        full_three=full_three,
        hidden_low=hidden_low,
        hidden_slope=hidden_slope,
    )
    return residual, stored


def weight_product(left, right, blocks):
    parts = right.reshape(right.shape[0], blocks, -1)
    return lax.dot_general(left, parts, (((0,), (0,)), ((), ())), preferred_element_type=F32).astype(BF).transpose(1, 0, 2)


def layer_backward(grid, gradient, weights, text_pair, gains, stored, units, wide):
    (w_qkv, w_out), w_cross, w_hidden = weights
    dy_three = joined(grid.gather(gradient.astype(BF)))
    d_pre = (product(dy_three, w_hidden[1]) * stored["hidden_slope"].astype(F32)).astype(BF)
    grad_normed = grid.scatter(
        [lambda d=d: product_nt(rows_of(grid, d_pre, d), w_hidden[0]) for d in range(grid.T)]
    )
    hidden_grads = [
        weight_product(stored["full_three"], d_pre, grid.C),
        weight_product(dy_three, stored["hidden_low"], grid.C),
    ]
    grad_res, gain_three, shift_three = norm_backward(
        grad_normed, stored["normed_three"], stored["inv_three"], gains[2]
    )
    gradient = gradient + grad_res
    dy_two = gradient.astype(BF)
    d_cross = product(dy_two, w_cross[1]).astype(BF)
    d_cquery, d_ckey, d_cvalue = cross_attention_grad(
        stored["cross_queries"], text_pair[0], text_pair[1], d_cross
    )
    grad_normed = product_nt(d_cquery, w_cross[0])
    cross_grads = [
        product_tn(stored["low_two"], d_cquery).astype(BF),
        product_tn(dy_two, stored["cross_low"]).astype(BF),
    ]
    text_grads = jnp.concatenate([d_ckey, d_cvalue], axis=1)
    grad_res, gain_two, shift_two = norm_backward(
        grad_normed, stored["normed_two"], stored["inv_two"], gains[1]
    )
    gradient = gradient + grad_res
    dy_one = joined(grid.gather(gradient.astype(BF)))
    d_attn = product(dy_one, w_out).astype(BF)
    d_qkv = self_attention_grad(grid, stored["qkv"], d_attn, stored["sums_self"], units, wide)
    grad_normed = grid.scatter(
        [lambda d=d: product_nt(rows_of(grid, d_qkv, d), w_qkv) for d in range(grid.T)]
    )
    self_grads = jnp.concatenate(
        [
            weight_product(stored["full_one"], d_qkv, units),
            weight_product(dy_one, stored["attn_low"], units),
        ],
        axis=2,
    )
    grad_res, gain_one, shift_one = norm_backward(
        grad_normed, stored["normed_one"], stored["inv_one"], gains[0]
    )
    gradient = gradient + grad_res
    norms = jnp.stack([gain_one, gain_two, gain_three, shift_one, shift_two, shift_three])
    return gradient, hidden_grads, cross_grads, self_grads, text_grads, norms


def shards(
    grid,
    inputs,
    text_states,
    cotangent,
    norm_gains,
    norm_shifts,
    self_query,
    self_key,
    self_value,
    self_out,
    cross_query,
    cross_key,
    cross_value,
    cross_out,
    mlp_up,
    mlp_down,
):
    grid.at()
    rows, width = self_query.shape[1:]
    hidden_width = mlp_up.shape[2]
    units, wide = head_units(grid, width)
    weights = []
    token = jnp.zeros((), BF)
    gains, shifts = grid.own_first(norm_gains), grid.own_first(norm_shifts)
    residual = grid.own_first(grid.tokens_in(inputs)).astype(F32)
    for n in range(LAYERS):
        w_self, token = self_weights(grid, [self_query[n], self_key[n], self_value[n], self_out[n]], token)
        w_cross, token = cross_weights(grid, [cross_query[n], cross_out[n]], token)
        w_hidden, token = hidden_weights(grid, [mlp_up[n], mlp_down[n]], token)
        weights.append((w_self, w_cross, w_hidden))
    text_cols = text_columns(grid, text_states)
    text_mats = jnp.stack([mat for n in range(LAYERS) for mat in (cross_key[n], cross_value[n])])
    text_all = text_forward(grid, text_cols, text_mats)
    text_pairs = [(text_all[:, 2 * n], text_all[:, 2 * n + 1]) for n in range(LAYERS)]
    stored = []
    for n in range(LAYERS):
        residual, kept = layer_forward(
            grid, residual, weights[n], text_pairs[n], gains[n], shifts[n], units, wide
        )
        stored.append(kept)
    output = grid.tokens_out(grid.own_last(residual.astype(BF))).astype(F32)
    gradient = grid.own_first(grid.tokens_in(cotangent.astype(BF))).astype(F32)
    hidden_out = [None] * LAYERS
    cross_out_grads = [None] * LAYERS
    self_out_grads = [None] * LAYERS
    text_weights = [None] * LAYERS
    norms = [None] * LAYERS
    text_part = 0.0
    for n in range(LAYERS - 1, -1, -1):
        gradient, hidden_grads, cross_grads, self_grads, text_grads, norms[n] = layer_backward(
            grid, gradient, weights[n], text_pairs[n], gains[n], stored[n], units, wide
        )
        hidden_out[n] = [hidden_weights_grad(grid, low, rows, hidden_width) for low in hidden_grads]
        cross_out_grads[n] = cross_weights_grad(grid, cross_grads, rows, width)
        self_out_grads[n] = self_weights_grad(grid, self_grads, rows, width)
        text_full = text_backward(grid, text_grads, width)
        text_weights[n] = [product_tn(text_cols, text_full[:, side]) for side in range(2)]
        text_part = (
            text_part
            + product_nt(text_full[:, 0], cross_key[n])
            + product_nt(text_full[:, 1], cross_value[n])
        )
    input_grad = grid.tokens_out(grid.own_last(gradient.astype(BF))).astype(F32)
    text_grad = text_out(grid, text_part)
    totals = grid.total(grid.own_last(jnp.stack(norms)))
    gains_sum, shifts_sum = totals[:, :3], totals[:, 3:]

    def both(values, slot):
        return jnp.stack([values[n][slot] for n in range(LAYERS)])

    return (
        output,
        input_grad,
        text_grad,
        gains_sum,
        shifts_sum[:, 1:],
        shifts_sum[:, 0],
        both(self_out_grads, 0),
        both(self_out_grads, 1),
        both(self_out_grads, 2),
        both(self_out_grads, 3),
        both(cross_out_grads, 0),
        both(text_weights, 0),
        both(text_weights, 1),
        both(cross_out_grads, 1),
        both(hidden_out, 0),
        both(hidden_out, 1),
    )


def solution(mesh):
    grid = Grid(mesh)
    tokens = P(("row", "col"), None)
    text = P("row", "col", None)
    block = P(None, "row", "col")
    in_specs = (tokens, text, tokens, P(), P()) + (block,) * 10
    out_specs = (tokens, tokens, text, P(), P(), P()) + (block,) * 10

    def run(*args):
        return shards(grid, *args)

    return jax.shard_map(run, mesh=mesh, in_specs=in_specs, out_specs=out_specs, check_vma=False)
```

```python
import functools

import jax
import jax.numpy as jnp
from jax import lax
from jax.experimental import pallas as pl
from jax.experimental.pallas import tpu as pltpu
from jax.sharding import PartitionSpec as P

HEAD = 64
CLIP_LEN = 1024
LAYERS = 2
SCALE = 0.125
EPS = 1e-05
NEG = -1e30
BF = jnp.bfloat16
F32 = jnp.float32
VMEM_LIMIT = 48 * 2**20
COST = CLIP_LEN * CLIP_LEN * 8


def product(left, right):
    return jnp.dot(left, right, preferred_element_type=F32)


def product_tn(left, right):
    return lax.dot_general(left, right, (((0,), (0,)), ((), ())), preferred_element_type=F32)


def product_nt(left, right):
    return lax.dot_general(left, right, (((1,), (1,)), ((), ())), preferred_element_type=F32)


def after(value, token):
    return lax.optimization_barrier((value, token))[0]


def tied(values, others):
    leaves, tree = jax.tree.flatten(values)
    arrays = [leaf for leaf in leaves if not isinstance(leaf, int)]
    others = [leaf for leaf in jax.tree.leaves(others) if not isinstance(leaf, int)]
    done = iter(lax.optimization_barrier((arrays, others))[0])
    return jax.tree.unflatten(tree, [leaf if isinstance(leaf, int) else next(done) for leaf in leaves])


def meet(values, fill):
    return tied((values, fill), [])


def joined(pieces):
    return pieces[0] if len(pieces) == 1 else jnp.concatenate(pieces, axis=0)


def flat(pieces):
    return [array for piece in pieces for array in piece]


class Grid:
    def __init__(self, mesh):
        self.R = mesh.shape["row"]
        self.C = mesh.shape["col"]
        self.T = self.R // 2
        assert self.T == self.C
        self.groups = [[2 * i + core for i in range(self.T)] for core in range(2)]

    def at(self):
        row = lax.axis_index("row")
        self.i = row // 2
        self.core = row % 2
        self.z = lax.axis_index("col")

    def swap(self, value, d):
        return lax.ppermute(value, "row", [(r, r ^ (2 * d)) for r in range(self.R)])

    def core_swap(self, value):
        return lax.ppermute(value, "row", [(r, r ^ 1) for r in range(self.R)])

    def plane_a2a(self, value):
        return lax.all_to_all(value, "row", 0, 0, tiled=True, axis_index_groups=self.groups)

    def row_a2a(self, value):
        return lax.all_to_all(value, "row", 0, 0, tiled=True)

    def col_a2a(self, value):
        return lax.all_to_all(value, "col", 0, 0, tiled=True)

    def distances(self):
        return sorted(range(1, self.T), key=lambda d: (bin(d).count("1"), d))

    def order(self):
        return [0] + self.distances()

    def gather_begin(self, own):
        return [own] + [self.swap(own, d) for d in self.distances() if d & (d - 1) == 0]

    def gather_end(self, near):
        half = near[0].shape[0] // 2
        pieces = {d: [piece] for d, piece in zip([0] + [d for d in self.distances() if d & (d - 1) == 0], near)}

        def part(d, upper):
            if len(pieces[d]) == 2:
                return pieces[d][upper]
            return pieces[d][0][half:] if upper else pieces[d][0][:half]

        for d in self.distances():
            high = 1 << (d.bit_length() - 1)
            low = d & -d
            if high != low:
                pieces[d] = [self.swap(part(d ^ high, 0), high), self.swap(part(d ^ low, 1), low)]
        return [pieces[d] for d in self.order()]

    def gather(self, own):
        return self.gather_end(self.gather_begin(own))

    def scatter_begin(self, top):
        d = self.order()[-1]
        high = 1 << (d.bit_length() - 1)
        low = d & -d
        return [(d ^ high, 0, self.swap(top[0], high)), (d ^ low, 1, self.swap(top[1], low))]

    def scatter_end(self, state, rest, fill=()):
        held = []
        order = self.order()
        state = list(state)
        for n in reversed(range(1, self.T - 1)):
            d = order[n]
            high = 1 << (d.bit_length() - 1)
            low = d & -d
            half = rest[n].shape[0] // 2
            parts = [rest[n][:half], rest[n][half:]]
            for goal, upper, value in state:
                if goal == d:
                    parts[upper] = parts[upper] + value.astype(F32)
            parts = [part.astype(BF) for part in parts]
            if high == low:
                held.append(self.swap(joined(parts), d))
            else:
                state += [(d ^ high, 0, self.swap(parts[0], high)), (d ^ low, 1, self.swap(parts[1], low))]
        total = rest[0]
        held, fill = meet(held, fill)
        for value in held:
            total = total + value.astype(F32)
        return total, fill

    def scatter(self, top, rest, fill=()):
        return self.scatter_end(self.scatter_begin(top), rest, fill)

    def natural(self, pieces):
        by_distance = [None] * self.T
        for d, piece in zip(self.order(), pieces):
            by_distance[d] = joined(piece)
        return self.picked(by_distance, [self.i ^ m for m in range(self.T)])

    def picked(self, parts, indices):
        stacked = jnp.stack(parts)
        return [lax.dynamic_index_in_dim(stacked, index, 0, keepdims=False) for index in indices]

    def col_swap(self, value, d):
        if d == 0:
            return value
        return lax.ppermute(value, "col", [(c, c ^ d) for c in range(self.C)])

    def plane_swap(self, value, d):
        return self.swap(value, d) if d else value

    def tokens_in(self, block, mid=None):
        rows, width = block.shape
        parts = block.reshape(self.T, rows // self.T, width)
        sent = [lax.dynamic_index_in_dim(parts, self.i ^ d, 0, keepdims=False) for d in range(self.T)]
        got = [self.plane_swap(sent[d], d) for d in range(self.T)]
        got = got if mid is None else tied(got, mid)
        sent = self.picked(got, [self.i ^ self.z ^ e for e in range(self.C)])
        return joined([self.col_swap(sent[e], e) for e in range(self.C)])

    def tokens_out_begin(self, block):
        small = block.shape[0] // self.C
        return [self.col_swap(block[e * small : (e + 1) * small], e) for e in range(self.C)]

    def tokens_out_end(self, got):
        sent = self.picked(got, [self.i ^ self.z ^ d for d in range(self.T)])
        got = [self.plane_swap(sent[d], d) for d in range(self.T)]
        return joined(self.picked(got, [self.i ^ m for m in range(self.T)]))

    def tokens_out(self, block):
        return self.tokens_out_end(self.tokens_out_begin(block))

    def total(self, value):
        for d in range(self.R.bit_length() - 1):
            value = value + lax.ppermute(value, "row", [(r, r ^ (1 << d)) for r in range(self.R)])
        for d in range(self.C.bit_length() - 1):
            value = value + lax.ppermute(value, "col", [(c, c ^ (1 << d)) for c in range(self.C)])
        return value


def gelu_parts(u):
    cdf = 0.5 * (1.0 + lax.erf(u * (0.5**0.5)))
    pdf = jnp.exp(-0.5 * u * u) * (0.5 / jnp.pi) ** 0.5
    return u * cdf, cdf + u * pdf


def norm_forward(residual, gain, shift):
    row_mean = jnp.mean(residual, axis=1, keepdims=True)
    centered = residual - row_mean
    variance = jnp.mean(centered * centered, axis=1, keepdims=True)
    inv_std = lax.rsqrt(variance + EPS)
    normed = centered * inv_std
    return (normed, inv_std, (normed * gain + shift).astype(BF))


def norm_backward(grad_out, normed, inv_std, gain):
    scaled = grad_out * gain
    row_mean = jnp.mean(scaled, axis=1, keepdims=True)
    row_along = jnp.mean(scaled * normed, axis=1, keepdims=True)
    grad_in = inv_std * (scaled - row_mean - normed * row_along)
    return (grad_in, jnp.sum(grad_out * normed, axis=0), jnp.sum(grad_out, axis=0))


def to_clip(grid, at_ref, source, target):
    rows = CLIP_LEN // grid.T
    small = rows // grid.C
    for n, d in enumerate(grid.order()):
        for e in range(grid.C):
            start = pl.multiple_of((at_ref[0] ^ d) * small + (at_ref[1] ^ e) * rows, small)
            low = n * rows + e * small
            target[pl.ds(start, small), :] = source[low : low + small, :]


def from_clip(grid, at_ref, block, k, target):
    rows = CLIP_LEN // grid.T
    small = rows // grid.C
    for n, d in enumerate(grid.order()):
        start = pl.multiple_of((at_ref[0] ^ d) * small, small)
        goal = pl.multiple_of(n * rows + (at_ref[1] ^ k) * small, small)
        target[pl.ds(goal, small), :] = block[pl.ds(start, small), :]


def causal_block(scores_t, size):
    keys = lax.broadcasted_iota(jnp.int32, (size, size), 0)
    asks = lax.broadcasted_iota(jnp.int32, (size, size), 1)
    last = scores_t.shape[0] - size
    edge = jnp.where(keys <= asks, scores_t[last:], NEG)
    return edge if last == 0 else jnp.concatenate([scores_t[:last], edge], axis=0)


def dot_nt(left, right):
    return lax.dot_general(left, right, (((1,), (1,)), ((), ())), preferred_element_type=F32)


def dot_nn(left, right):
    return lax.dot_general(left, right, (((1,), (0,)), ((), ())), preferred_element_type=F32)


def flip(value):
    return value.astype(F32).T


def self_forward_kernel(grid, width, at_ref, x_ref, out_ref, sums_ref, clip, block):
    size = CLIP_LEN // grid.C
    to_clip(grid, at_ref, x_ref, clip)
    heads = range(width // HEAD)

    def lanes(which, h):
        return slice(which * width + h * HEAD, which * width + (h + 1) * HEAD)

    keys = [clip[:, lanes(1, h)] for h in heads]
    values_t = [flip(clip[:, lanes(2, h)]).astype(BF) for h in heads]
    for k in range(grid.C):
        low, high = k * size, (k + 1) * size
        outs = []
        for h in heads:
            asks = clip[low:high, lanes(0, h)] * BF(SCALE)
            scores = causal_block(dot_nt(keys[h][:high], asks), size)
            top = jnp.max(scores, axis=0, keepdims=True)
            weight = jnp.exp(scores - top)
            total = jnp.sum(weight, axis=0, keepdims=True)
            outs.append(dot_nn(values_t[h][:, :high], weight.astype(BF)) / total)
            sums_ref[h : h + 1, low:high] = top + jnp.log(total)
        both = outs[0] if len(outs) == 1 else jnp.concatenate(outs, axis=0)
        block[...] = both.T.astype(BF)
        from_clip(grid, at_ref, block, k, out_ref)


def self_backward_kernel(grid, width, at_ref, x_ref, da_ref, sums_ref, out_ref, clip, da_clip, block, acc):
    size = CLIP_LEN // grid.C
    to_clip(grid, at_ref, x_ref, clip)
    to_clip(grid, at_ref, da_ref, da_clip)
    heads = range(width // HEAD)

    def lanes(which, h):
        return slice(which * width + h * HEAD, which * width + (h + 1) * HEAD)

    keys = [clip[:, lanes(1, h)] for h in heads]
    values = [clip[:, lanes(2, h)] for h in heads]
    keys_t = [flip(keys[h]).astype(BF) for h in heads]
    for k in reversed(range(grid.C)):
        low, high = k * size, (k + 1) * size
        dq = []
        for h in heads:
            asks = clip[low:high, lanes(0, h)] * BF(SCALE)
            da = da_clip[low:high, lanes(0, h)]
            scores = causal_block(dot_nt(keys[h][:high], asks), size)
            probs = jnp.exp(scores - sums_ref[h : h + 1, low:high])
            d_probs = dot_nt(values[h][:high], da)
            inner = jnp.sum(probs * d_probs, axis=0, keepdims=True)
            d_scores = (probs * (d_probs - inner)).astype(BF)
            dk = dot_nn(d_scores, asks)
            dv = dot_nn(probs.astype(BF), da)
            if k == grid.C - 1:
                acc[:, lanes(0, h)] = dk
                acc[:, lanes(1, h)] = dv
            else:
                acc[:high, lanes(0, h)] += dk
                acc[:high, lanes(1, h)] += dv
            dq.append(dot_nn(keys_t[h][:, :high], d_scores) * SCALE)
        both = dq[0] if len(dq) == 1 else jnp.concatenate(dq, axis=0)
        block[:, :width] = both.T.astype(BF)
        block[:, width:] = acc[low:high, :].astype(BF)
        from_clip(grid, at_ref, block, k, out_ref)


def unit_spec(rows, lanes):
    return pl.BlockSpec((None, rows, lanes), lambda n, *at: (n, 0, 0))


def self_attention(grid, x):
    units, _, width = x.shape
    width //= 3
    size = CLIP_LEN // grid.C
    return pl.pallas_call(
        functools.partial(self_forward_kernel, grid, width),
        grid_spec=pltpu.PrefetchScalarGridSpec(
            num_scalar_prefetch=1,
            grid=(units,),
            in_specs=[unit_spec(CLIP_LEN, 3 * width)],
            out_specs=[unit_spec(CLIP_LEN, width), unit_spec(8, CLIP_LEN)],
            scratch_shapes=[pltpu.VMEM((CLIP_LEN, 3 * width), BF), pltpu.VMEM((size, width), BF)],
        ),
        out_shape=[
            jax.ShapeDtypeStruct((units, CLIP_LEN, width), BF),
            jax.ShapeDtypeStruct((units, 8, CLIP_LEN), F32),
        ],
        compiler_params=pltpu.CompilerParams(vmem_limit_bytes=VMEM_LIMIT),
        cost_estimate=pl.CostEstimate(
            flops=COST * units * width, bytes_accessed=CLIP_LEN * units * width * 8, transcendentals=0
        ),
        name="self_attention",
    )(jnp.stack([grid.i, grid.z]), x)


def self_attention_grad(grid, x, da, sums):
    units, _, width = da.shape
    size = CLIP_LEN // grid.C
    return pl.pallas_call(
        functools.partial(self_backward_kernel, grid, width),
        grid_spec=pltpu.PrefetchScalarGridSpec(
            num_scalar_prefetch=1,
            grid=(units,),
            in_specs=[unit_spec(CLIP_LEN, 3 * width), unit_spec(CLIP_LEN, width), unit_spec(8, CLIP_LEN)],
            out_specs=unit_spec(CLIP_LEN, 3 * width),
            scratch_shapes=[
                pltpu.VMEM((CLIP_LEN, 3 * width), BF),
                pltpu.VMEM((CLIP_LEN, width), BF),
                pltpu.VMEM((size, 3 * width), BF),
                pltpu.VMEM((CLIP_LEN, 2 * width), F32),
            ],
        ),
        out_shape=jax.ShapeDtypeStruct((units, CLIP_LEN, 3 * width), BF),
        compiler_params=pltpu.CompilerParams(vmem_limit_bytes=VMEM_LIMIT),
        cost_estimate=pl.CostEstimate(
            flops=3 * COST * units * width, bytes_accessed=CLIP_LEN * units * width * 16, transcendentals=0
        ),
        name="self_attention_grad",
    )(jnp.stack([grid.i, grid.z]), x, da, sums)


def reorder_kernel(spans, core_ref, x_ref, out_ref):
    for core in range(2):

        @pl.when(core_ref[0] == core)
        def _(core=core):
            out_ref[...] = jnp.concatenate([x_ref[:, low : low + size] for low, size in spans[core]], axis=1)


def reorder(grid, x, back):
    rows, width = x.shape
    size = width // grid.R
    half = width // 2
    if back:
        spans = [[((r % 2 != core) * half + r // 2 * size, size) for r in range(grid.R)] for core in range(2)]
    else:
        spans = [[((2 * i + (core + n) % 2) * size, size) for n in range(2) for i in range(grid.T)] for core in range(2)]
    return pl.pallas_call(
        functools.partial(reorder_kernel, spans),
        grid_spec=pltpu.PrefetchScalarGridSpec(
            num_scalar_prefetch=1,
            grid=(1,),
            in_specs=[pl.BlockSpec((rows, width), lambda n, core: (0, 0))],
            out_specs=pl.BlockSpec((rows, width), lambda n, core: (0, 0)),
        ),
        out_shape=jax.ShapeDtypeStruct((rows, width), x.dtype),
        name="reorder",
    )(grid.core.reshape(1), x)


def own_first(grid, x):
    return reorder(grid, x, False)


def own_last(grid, x):
    return reorder(grid, x, True)


def lanes_of(ref, mats):
    parts = [ref[m] for m in mats]
    return parts[0] if len(parts) == 1 else jnp.concatenate(parts, axis=1)


def columns_kernel(mats, count, kind, *refs):
    pieces, (own_ref, other_ref), rest = refs[:count], refs[count : count + 2], refs[count + 2 :]
    own, other = lanes_of(own_ref, mats), lanes_of(other_ref, mats)
    half = own.shape[0]
    low = 0
    for piece in pieces:
        high = low + piece.shape[0]
        out = dot_nn(piece[:, :half], own) + dot_nn(piece[:, half:], other)
        if kind == "gelu":
            value, slope = gelu_parts(out)
            rest[0][low:high] = value.astype(BF)
            rest[1][low:high] = slope.astype(BF)
        elif kind == "slope":
            rest[1][low:high] = (out * rest[0][low:high].astype(F32)).astype(BF)
        else:
            rest[0][low:high] = out.astype(BF)
        low = high


def whole(array):
    return pl.BlockSpec(array.shape, lambda n: (0,) * array.ndim)


def act_spec(rows, lanes):
    return pl.BlockSpec((None, rows, lanes), lambda n: (n, 0, 0))


def columns_product(pieces, weights, mats, kind="plain", slope=None):
    own, other = weights
    blocks, _, half, wide = own.shape
    lanes = len(mats) * wide
    rows = sum(p.shape[0] for p in pieces)
    extra = [] if slope is None else [slope]
    outs = 2 if kind == "gelu" else 1
    shape = jax.ShapeDtypeStruct((blocks, rows, lanes), BF)
    first, picked = (mats[0], 1) if len(mats) == 1 else (0, own.shape[1])
    spec = pl.BlockSpec((None, picked) + own.shape[2:], lambda n: (n, first, 0, 0))
    result = pl.pallas_call(
        functools.partial(columns_kernel, (0,) if len(mats) == 1 else mats, len(pieces), kind),
        grid=(blocks,),
        in_specs=[whole(p) for p in pieces] + [spec, spec] + [act_spec(rows, lanes)] * len(extra),
        out_specs=[act_spec(rows, lanes)] * outs,
        out_shape=[shape] * outs,
        compiler_params=pltpu.CompilerParams(vmem_limit_bytes=VMEM_LIMIT),
        cost_estimate=pl.CostEstimate(flops=4 * half * rows * lanes * blocks, bytes_accessed=4 * half * lanes * blocks, transcendentals=0),
        name="columns_" + kind,
    )(*pieces, own, other, *extra)
    return result if outs > 1 else result[0]


def rows_kernel(mats, low, high, act_ref, own_ref, other_ref, *outs):
    blocks = act_ref.shape[0]
    acts = [act_ref[n, low:high] for n in range(blocks)]
    half = own_ref.shape[2]
    for cols, ref in ((slice(0, half), own_ref), (slice(half, 2 * half), other_ref)):
        parts = [lanes_of(ref.at[n], mats) for n in range(blocks)]
        if parts[0].shape[1] < 256:
            total = dot_nt(jnp.concatenate(acts, axis=1), jnp.concatenate(parts, axis=1))
        else:
            total = dot_nt(acts[0], parts[0])
            for act, part in zip(acts[1:], parts[1:]):
                total = total + dot_nt(act, part)
        at = 0
        for out in outs:
            out[:, cols] = total[at : at + out.shape[0]].astype(out.dtype)
            at += out.shape[0]


def rows_product(act, weights, mats, low, high, shapes):
    own, other = weights
    blocks, _, half, _ = own.shape
    lanes = act.shape[2]
    first, count = (mats[0], 1) if len(mats) == 1 else (0, own.shape[1])
    spec = pl.BlockSpec((blocks, count) + own.shape[2:], lambda n: (0, first, 0, 0))
    return pl.pallas_call(
        functools.partial(rows_kernel, (0,) if len(mats) == 1 else mats, low, high),
        grid=(1,),
        in_specs=[whole(act), spec, spec],
        out_specs=[whole(s) for s in shapes],
        out_shape=shapes,
        compiler_params=pltpu.CompilerParams(vmem_limit_bytes=VMEM_LIMIT),
        cost_estimate=pl.CostEstimate(
            flops=4 * half * (high - low) * lanes * blocks, bytes_accessed=4 * half * lanes * blocks, transcendentals=0
        ),
        name="rows",
    )(act, own, other)


def rows_top(grid, act, weights, mats):
    rows = act.shape[1] // grid.T
    shapes = [jax.ShapeDtypeStruct((rows // 2, 2 * weights[0].shape[2]), BF)] * 2
    return list(rows_product(act, weights, mats, rows * (grid.T - 1), rows * grid.T, shapes))


def rows_rest(grid, act, weights, mats):
    rows = act.shape[1] // grid.T
    shapes = [jax.ShapeDtypeStruct((rows, 2 * weights[0].shape[2]), F32)] * (grid.T - 1)
    return list(rows_product(act, weights, mats, 0, rows * (grid.T - 1), shapes))


def rows_terms(grid, act, weights, mats):
    top = rows_top(grid, act, weights, mats)
    return top, rows_rest(grid, after(act, top), weights, mats)


def grads_kernel(count, *refs):
    pieces, y_ref, keep_ref, send_ref, turned = refs[:count], refs[count], refs[count + 1], refs[count + 2], refs[count + 3]
    half = keep_ref.shape[0]

    @pl.when(pl.program_id(0) == 0)
    def _():
        low = 0
        for piece in pieces:
            high = low + piece.shape[0]
            turned[:, low:high] = piece[...].T
            low = high

    y = y_ref[...]
    keep_ref[...] = dot_nn(turned[:half], y).astype(BF)
    send_ref[...] = dot_nn(turned[half:], y).astype(BF)


def weight_grads(pieces, y):
    blocks, rows, lanes = y.shape
    width = pieces[0].shape[1]
    half = width // 2
    shape = jax.ShapeDtypeStruct((blocks, half, lanes), BF)
    return pl.pallas_call(
        functools.partial(grads_kernel, len(pieces)),
        grid=(blocks,),
        in_specs=[whole(p) for p in pieces] + [act_spec(rows, lanes)],
        out_specs=[act_spec(half, lanes)] * 2,
        out_shape=[shape] * 2,
        scratch_shapes=[pltpu.VMEM((width, rows), BF)],
        compiler_params=pltpu.CompilerParams(vmem_limit_bytes=VMEM_LIMIT),
        cost_estimate=pl.CostEstimate(flops=4 * half * rows * lanes * blocks, bytes_accessed=4 * half * lanes * blocks, transcendentals=0),
        name="weight_grads",
    )(*pieces, y)


def cross_scores(keys, asks):
    scores = dot_nt(keys, asks)
    top = jnp.max(scores, axis=0, keepdims=True)
    weight = jnp.exp(scores - top)
    return weight / jnp.sum(weight, axis=0, keepdims=True)


def cross_forward_kernel(q_ref, k_ref, v_ref, out_ref):
    for low in range(0, q_ref.shape[1], 2 * HEAD):
        pair = []
        for at in (slice(low, low + HEAD), slice(low + HEAD, low + 2 * HEAD)):
            probs = cross_scores(k_ref[:, at], q_ref[:, at] * BF(SCALE)).astype(BF)
            pair.append(dot_nn(flip(v_ref[:, at]).astype(BF), probs))
        out_ref[:, low : low + 2 * HEAD] = jnp.concatenate(pair, axis=0).T.astype(BF)


def cross_backward_kernel(q_ref, k_ref, v_ref, dc_ref, dq_ref, dk_ref, dv_ref):
    for low in range(0, q_ref.shape[1], 2 * HEAD):
        pair, dk, dv = [], [], []
        for at in (slice(low, low + HEAD), slice(low + HEAD, low + 2 * HEAD)):
            asks = q_ref[:, at] * BF(SCALE)
            probs = cross_scores(k_ref[:, at], asks)
            d_probs = dot_nt(v_ref[:, at], dc_ref[:, at])
            inner = jnp.sum(probs * d_probs, axis=0, keepdims=True)
            d_scores = (probs * (d_probs - inner)).astype(BF)
            dk.append(dot_nn(d_scores, asks))
            dv.append(dot_nn(probs.astype(BF), dc_ref[:, at]))
            pair.append(dot_nn(flip(k_ref[:, at]).astype(BF), d_scores) * SCALE)
        at = slice(low, low + 2 * HEAD)
        dq_ref[:, at] = jnp.concatenate(pair, axis=0).T.astype(BF)
        dk_ref[:, at] = jnp.concatenate(dk, axis=1)
        dv_ref[:, at] = jnp.concatenate(dv, axis=1)


def cross_call(kernel, name, arrays, outs):
    width = arrays[0].shape[1]
    lanes = 512 if width % 512 == 0 else width

    def spec(rows):
        return pl.BlockSpec((rows, lanes), lambda n: (0, n))

    return pl.pallas_call(
        kernel,
        grid=(width // lanes,),
        in_specs=[spec(a.shape[0]) for a in arrays],
        out_specs=[spec(rows) for rows, _ in outs],
        out_shape=[jax.ShapeDtypeStruct((rows, width), kind) for rows, kind in outs],
        compiler_params=pltpu.CompilerParams(vmem_limit_bytes=VMEM_LIMIT),
        cost_estimate=pl.CostEstimate(
            flops=arrays[0].shape[0] * arrays[1].shape[0] * width * 20, bytes_accessed=2**22, transcendentals=0
        ),
        name=name,
    )(*arrays)


def cross_attention(queries, keys, values):
    return cross_call(cross_forward_kernel, "cross_attention", [queries, keys, values], [(queries.shape[0], BF)])[0]


def cross_attention_grad(queries, keys, values, grad_out):
    outs = [(queries.shape[0], BF), (keys.shape[0], F32), (keys.shape[0], F32)]
    return cross_call(cross_backward_kernel, "cross_attention_grad", [queries, keys, values, grad_out], outs)


def head_units(grid, width):
    heads = width // HEAD
    per_unit = -(-heads // grid.T)
    assert heads % per_unit == 0
    return heads // per_unit, per_unit * HEAD


def self_slots(grid, mats):
    units, wide = head_units(grid, mats[0].shape[1])
    both = jnp.stack(mats)
    lows = [jnp.minimum((s - grid.z - 1) % grid.T, units - 1) * wide for s in range(grid.T)]
    return jnp.stack([lax.dynamic_slice_in_dim(both, low, wide, axis=2) for low in lows])


def by_matrix(moved):
    sources, count, rows, wide = moved.shape
    return moved.transpose(1, 0, 2, 3).reshape(count, sources * rows, wide)


def self_weights(grid, slots, units):
    half = jnp.stack(
        [lax.dynamic_index_in_dim(slots, (grid.i - 1 - m) % grid.T, 0, keepdims=False) for m in range(units)]
    )
    return half, grid.core_swap(half)


def core_sum(grid, keep, send, mid):
    got = tied(grid.core_swap(send), mid)
    return (keep.astype(F32) + got.astype(F32)).astype(BF)


def self_grad_slots(grid, pairs, mid):
    half = jnp.concatenate([core_sum(grid, *pair, mid) for pair in pairs], axis=2)
    half = jnp.concatenate([half, jnp.zeros((grid.C - half.shape[0],) + half.shape[1:], BF)], axis=0)
    return jnp.stack(
        [lax.dynamic_index_in_dim(half, (grid.i - c - 1) % grid.T, 0, keepdims=False) for c in range(grid.C)]
    )


def self_grad_blocks(grid, moved, units):
    wide = moved.shape[2] // 4
    mine = [lax.dynamic_index_in_dim(moved, (grid.z + 1 + m) % grid.T, 0, keepdims=False) for m in range(units)]
    return [
        jnp.concatenate([part[:, n * wide : (n + 1) * wide] for part in mine], axis=1).astype(F32) for n in range(4)
    ]


def hidden_slots(grid, mats):
    rows, width = mats[0].shape
    count = len(mats)
    return jnp.stack(mats).reshape(count, rows, grid.T, width // grid.T).transpose(2, 0, 1, 3)


def hidden_gathered(moved, n, token):
    sources, _, rows, wide = moved.shape
    return lax.all_gather(after(moved[:, n].reshape(1, sources * rows, wide), token), "col", axis=0)


def with_other(grid, own):
    return own, grid.core_swap(own)


def hidden_grad_slots(grid, pairs, mid):
    return jnp.concatenate([core_sum(grid, *pair, mid) for pair in pairs], axis=2)


def col_sum(slots):
    return lax.psum_scatter(slots, "col", scatter_dimension=0)


def hidden_grad_blocks(grid, moved, count):
    rows, wide = moved.shape[1], moved.shape[2] // count
    return [
        moved[:, :, n * wide : (n + 1) * wide].transpose(1, 0, 2).reshape(rows, -1).astype(F32) for n in range(count)
    ]


def cross_columns(grid, blocks):
    _, count, rows, width = blocks.shape
    return blocks.transpose(1, 2, 0, 3).reshape(count * rows, grid.C * width)


def cross_weights(grid, pieces, count):
    half = jnp.stack(grid.natural(pieces))
    width = half.shape[2]
    half = half.reshape(grid.T, count, -1, width).transpose(1, 0, 2, 3).reshape(count, -1, width)
    other = grid.core_swap(half)
    return [joined([half[n], other[n]]) for n in range(count)]


def cross_core_sum(grid, lows, mid):
    edge = lows[0].shape[0] // 2
    return [core_sum(grid, low[:edge], low[edge:], mid) for low in lows]


def cross_terms(grid, halves, rows, width):
    halves = [half.reshape(grid.T, rows, grid.C * width) for half in halves]

    def term(d):
        return joined([lax.dynamic_index_in_dim(half, grid.i ^ d, 0, keepdims=False) for half in halves])

    order = grid.order()
    top = term(order[-1])
    size = top.shape[0] // 2
    return [top[:size], top[size:]], [term(d).astype(F32) for d in order[:-1]]


def cross_blocks(grid, own, rows, width):
    return own.astype(BF).reshape(-1, rows, grid.C, width).transpose(2, 0, 1, 3)


def text_columns(grid, text):
    _, own, width = text.shape
    parts = text.reshape(own, grid.R, width // grid.R).transpose(1, 0, 2)
    parts = grid.row_a2a(parts)
    pieces = [parts] + [
        lax.ppermute(parts, "col", [(c, c ^ d) for c in range(grid.C)]) for d in range(1, grid.C)
    ]
    stacked = jnp.stack(pieces)
    order = [lax.dynamic_index_in_dim(stacked, grid.z ^ c, 0, keepdims=False) for c in range(grid.C)]
    return jnp.stack(order, axis=1).reshape(-1, width // grid.R)


def text_parts(grid, columns, mats):
    count, rows, width = mats.shape
    own = columns.shape[0] // (grid.R * grid.C)
    part = product(columns, mats.transpose(1, 0, 2).reshape(rows, count * width)).astype(BF)
    part = part.reshape(grid.T, 2, grid.C, own, count * width).transpose(2, 1, 0, 3, 4)
    return grid.row_a2a(part.reshape(grid.R, grid.T * own, count * width))


def text_shared(grid, moved):
    own = moved.shape[1] // grid.T
    summed = jnp.sum(moved.astype(F32), axis=0).astype(BF).reshape(grid.T, own, moved.shape[2])
    sent = grid.picked(list(summed), [grid.z ^ e for e in range(grid.C)])
    return [grid.col_swap(sent[e], e) for e in range(grid.C)]


def text_states_of(grid, got, count):
    own, width = got[0].shape[0], got[0].shape[1] // count
    blocks = jnp.stack(grid.picked(got, [grid.z ^ c for c in range(grid.C)]))
    mine = blocks.reshape(grid.C, own, count, width).transpose(1, 2, 0, 3)
    mine = mine.reshape(own, count * grid.C * width)
    full = joined(flat(grid.gather(mine)))
    return full.reshape(-1, count, grid.C * width)


def text_begin(grid, grads):
    own = grads.shape[0] // grid.T
    pieces = grads.reshape(grid.T, own, -1)
    top = pieces[grid.T - 1].astype(BF)
    return grid.scatter_begin([top[: own // 2], top[own // 2 :]]), [pieces[n] for n in range(grid.T - 1)]


def text_backward(grid, mine, width):
    own = mine.shape[0]
    mine = mine.reshape(own, -1, grid.C, width).transpose(2, 0, 1, 3)
    moved = grid.col_a2a(mine)
    other = grid.core_swap(moved)
    pair = jnp.stack(
        [jnp.where(grid.core == 0, moved, other), jnp.where(grid.core == 0, other, moved)], axis=1
    )
    shape = pair.shape
    flat = pair.reshape(shape[0] * 2, -1)
    full = jnp.stack(grid.natural(grid.gather(flat)), axis=1)
    return full.reshape(-1, shape[3], width)


def text_out(grid, part):
    own = part.shape[0] // (grid.R * grid.C)
    cols = part.shape[1]
    parts = part.astype(BF).reshape(grid.R, grid.C, own, cols).transpose(1, 0, 2, 3)
    moved = grid.col_a2a(parts).astype(F32)
    summed = jnp.sum(moved, axis=0).astype(BF)
    moved = grid.row_a2a(summed)
    return moved.transpose(1, 0, 2).reshape(1, own, grid.R * cols).astype(F32)


def shards(
    grid,
    inputs,
    text_states,
    cotangent,
    norm_gains,
    norm_shifts,
    self_query,
    self_key,
    self_value,
    self_out,
    cross_query,
    cross_key,
    cross_value,
    cross_out,
    mlp_up,
    mlp_down,
):
    grid.at()
    last = LAYERS - 1
    rows, width = self_query.shape[1:]
    units, _ = head_units(grid, width)

    self_parts = [self_slots(grid, [w[n] for w in (self_query, self_key, self_value, self_out)]) for n in range(LAYERS)]
    hidden_parts = [hidden_slots(grid, [mlp_up[n], mlp_down[n]]) for n in range(LAYERS)]
    self_moved = [None] * LAYERS
    hidden_moved = [None] * LAYERS
    self_full = [None] * LAYERS
    self_moved[0] = grid.plane_a2a(self_parts[0])
    sent = by_matrix(self_moved[0])
    cross_parts = [jnp.stack([cross_query[n], cross_out[n]]) for n in range(LAYERS)]
    tokens = grid.tokens_in(jnp.concatenate([inputs, cotangent.astype(BF)], axis=1))
    tokens, sent = meet(tokens, sent)
    text_cols = text_columns(grid, after(text_states, tokens))
    gradient = tokens[:, inputs.shape[1] :]
    tokens = tokens[:, : inputs.shape[1]]
    self_full[0] = lax.all_gather(sent, "col", axis=0)
    residual = own_first(grid, tokens).astype(F32)
    norm_rows = after(jnp.concatenate([norm_gains, norm_shifts], axis=1), tokens)
    norm_rows = own_first(grid, norm_rows.reshape(-1, norm_rows.shape[2])).reshape(norm_rows.shape)
    gains, shifts = norm_rows[:, :3], norm_rows[:, 3:]
    text_mats = jnp.stack([mat for n in range(LAYERS) for mat in (cross_key[n], cross_value[n])])

    kept = [dict() for _ in range(LAYERS)]
    w_self = [None] * LAYERS
    w_cross = [None] * LAYERS
    w_hidden = [None] * LAYERS
    for n in range(LAYERS):
        k = kept[n]
        k["normed_one"], k["inv_one"], low_one = norm_forward(residual, gains[n, 0], shifts[n, 0])
        near_one = grid.gather_begin(low_one)
        if n == 0:
            hidden_moved[0] = grid.plane_a2a(after(hidden_parts[0], near_one))
            text_moved = text_parts(grid, after(text_cols, near_one), text_mats)
        full_one = flat(grid.gather_end(near_one))
        if n == 0:
            (self_full[0], full_one), (text_sent, hidden_moved[0]) = meet(
                (self_full[0], full_one), (text_shared(grid, text_moved), hidden_moved[0])
            )
            cross_full = lax.all_gather(after(cross_parts[0], sent), "col", axis=0)
        else:
            self_full[n] = after(self_full[n], residual)
        k["full_one"] = full_one
        w_self[n] = self_weights(grid, self_full[n], units)
        k["qkv"] = columns_product(full_one, w_self[n], (0, 1, 2))
        k["attn_low"], k["sums_self"] = self_attention(grid, k["qkv"])
        if n > 0:
            next_near = grid.gather_begin(cross_columns(grid, after(cross_full, full_one)))
            k["attn_low"], next_near = meet(k["attn_low"], next_near)
            w_cross[n] = cross_weights(grid, grid.gather_end(next_near), 2)
        up_full = hidden_gathered(hidden_moved[n], 0, full_one)
        down_full = hidden_gathered(hidden_moved[n], 1, k["qkv"])
        top, rest = rows_terms(grid, k["attn_low"], w_self[n], (3,))
        fill = []
        if n == 0:
            next_near = grid.gather_begin(cross_columns(grid, after(cross_full, k["qkv"])))
            rest, next_near = meet(rest, next_near)
            w_cross[0] = cross_weights(grid, grid.gather_end(next_near), 2)
        if n == 0:
            text_all = text_states_of(grid, tied(text_sent, top), 2 * LAYERS)
        added, _ = grid.scatter(top, rest)
        residual = residual + added
        w_up = with_other(grid, after(up_full, residual))
        before_cross = residual
        k["text"] = [text_all[:, 2 * n + side] for side in range(2)]
        k["normed_two"], k["inv_two"], k["low_two"] = norm_forward(residual, gains[n, 1], shifts[n, 1])
        k["cross_queries"] = product(k["low_two"], w_cross[n][0]).astype(BF)
        k["cross_low"] = cross_attention(k["cross_queries"], *k["text"])
        residual = residual + product_nt(k["cross_low"], w_cross[n][1])
        k["normed_three"], k["inv_three"], low_three = norm_forward(residual, gains[n, 2], shifts[n, 2])
        if n < last:
            sent = by_matrix(grid.plane_a2a(after(self_parts[n + 1], before_cross)))
            low_three, sent = meet(low_three, sent)
            self_full[n + 1] = lax.all_gather(sent, "col", axis=0)
            cross_full = lax.all_gather(after(cross_parts[n + 1], sent), "col", axis=0)
        if n == last:
            low_three, next_near = meet(low_three, grid.gather_begin(after(gradient, before_cross)))
        k["full_three"] = flat(grid.gather(low_three))
        if n < last:
            hidden_moved[n + 1] = grid.plane_a2a(after(hidden_parts[n + 1], low_three))
            k["full_three"], hidden_moved[n + 1] = meet(k["full_three"], hidden_moved[n + 1])
        k["hidden_low"], k["hidden_slope"] = columns_product(k["full_three"], w_up, (0,), "gelu")
        w_hidden[n] = (w_up, with_other(grid, after(down_full, k["hidden_low"])))
        if n < last:
            top, rest = rows_terms(grid, k["hidden_low"], w_hidden[n][1], (0,))
            gradient = own_first(grid, after(gradient, rest)) if n == 0 else gradient
            added, gradient = grid.scatter(top, rest, gradient)
            residual = residual + added
        else:
            dy_three = flat(grid.gather_end(next_near))
            gradient = gradient.astype(F32)

    before_last = residual
    hidden_sums = [None] * LAYERS
    self_sums = [None] * LAYERS
    cross_sums = [None] * LAYERS
    text_grads = [None] * LAYERS
    norms = [None] * LAYERS
    fill = []
    for n in range(last, -1, -1):
        k = kept[n]
        w_up, w_down = w_hidden[n]
        if n < last:
            sent, slots = meet(gradient.astype(BF), self_slots_grad)
            self_sums[n + 1] = col_sum(slots)
            dy_three, hidden_sums[n + 1] = meet(flat(grid.gather(sent)), hidden_sums[n + 1])
        if n == last:
            late_top, late_rest = rows_terms(grid, k["hidden_low"], w_down, (0,))
            late_state = grid.scatter_begin(late_top)
            dy_three, late_rest = meet(dy_three, late_rest)
        d_pre = columns_product(dy_three, w_down, (0,), "slope", k["hidden_slope"])
        top, rest = rows_terms(grid, d_pre, w_up, (0,))
        state = grid.scatter_begin(top)
        if n < last:
            own, _ = grid.scatter_end(tied(cross_state, dy_three), cross_last)
            own = cross_blocks(grid, own, rows, width)
            (state, rest), own = meet((state, rest), own)
            cross_late = own
        hidden_pairs = [
            weight_grads(after(k["full_three"], state), d_pre),
            weight_grads(after(dy_three, state), k["hidden_low"]),
        ]
        if n == last:
            late_state = tied(late_state, rest)
        grad_normed, hidden_pairs = grid.scatter_end(state, rest, hidden_pairs)
        grad_res, gain_three, shift_three = norm_backward(grad_normed, k["normed_three"], k["inv_three"], gains[n, 2])
        gradient = gradient + grad_res
        before_cross = gradient
        if n == last:
            late_sum, _ = grid.scatter_end(tied(late_state, gradient), late_rest)
        dy_two = gradient.astype(BF)
        d_cross = product(dy_two, w_cross[n][1]).astype(BF)
        d_cquery, d_ckey, d_cvalue = cross_attention_grad(k["cross_queries"], *k["text"], d_cross)
        grad_normed = product_nt(d_cquery, w_cross[n][0])
        text_grads[n] = jnp.concatenate([d_ckey, d_cvalue], axis=1)
        grad_res, gain_two, shift_two = norm_backward(grad_normed, k["normed_two"], k["inv_two"], gains[n, 1])
        gradient = gradient + grad_res
        sent = gradient.astype(BF)
        cross_lows = [
            product_tn(after(k["low_two"], sent), d_cquery).astype(BF),
            product_tn(after(dy_two, sent), k["cross_low"]).astype(BF),
        ]
        cross_halves = cross_core_sum(grid, cross_lows, sent)
        cross_top, cross_rest = cross_terms(grid, cross_halves, rows, width)
        fill = [cross_top]
        if n == last:
            sent, late_sum = meet(sent, late_sum)
            output = own_last(grid, (before_last + late_sum).astype(BF))
            fill += [output, hidden_grad_slots(grid, hidden_pairs, sent)]
        else:
            sent, hidden_slots_grad = meet(sent, hidden_grad_slots(grid, hidden_pairs, grad_normed))
            hidden_sums[n] = col_sum(hidden_slots_grad)
            cross_sums[n + 1] = col_sum(after(cross_late, hidden_slots_grad))
            fill.append(self_sums[n + 1])
        dy_one, fill = meet(flat(grid.gather(sent)), fill)
        cross_top = fill[0]
        if n == last:
            output = grid.tokens_out_begin(fill[1])
            hidden_sums[n] = col_sum(fill[2])
        else:
            self_sums[n + 1] = fill[1]
        d_attn = columns_product(dy_one, w_self[n], (3,))
        d_qkv = self_attention_grad(grid, k["qkv"], d_attn, k["sums_self"])
        cross_state, cross_last = grid.scatter_begin(after(cross_top, dy_one)), cross_rest
        if n == 0:
            text_state, text_rest = text_begin(grid, after(jnp.concatenate(text_grads, axis=1), dy_one))
            d_qkv, text_state = meet(d_qkv, text_state)
        if n == last:
            d_qkv, output = meet(d_qkv, output)
            output = grid.tokens_out_end(output)
        d_qkv, cross_state = meet(d_qkv, cross_state)
        if n > 0:
            top, rest = rows_terms(grid, d_qkv, w_self[n], (0, 1, 2))
            state = grid.scatter_begin(top)
            qkv_pair = weight_grads(after(k["full_one"], state), d_qkv)
            out_pair = weight_grads(after(dy_one, state), k["attn_low"])
            fill = [qkv_pair, out_pair, output]
        else:
            qkv_pair = weight_grads(k["full_one"], d_qkv)
            out_pair = weight_grads(dy_one, after(k["attn_low"], d_qkv))
            text_mine = grid.scatter_end(text_state, text_rest)[0].astype(BF)
            out_pair, text_mine = meet(out_pair, text_mine)
            top = rows_top(grid, after(d_qkv, [qkv_pair, out_pair]), w_self[n], (0, 1, 2))
            state = grid.scatter_begin(top)
            top, slots = meet(top, self_grad_slots(grid, [qkv_pair, out_pair], out_pair))
            self_sums[0] = col_sum(slots)
            rest = rows_rest(grid, after(d_qkv, top), w_self[n], (0, 1, 2))
            own, _ = grid.scatter_end(tied(cross_state, rest), cross_last)
            cross_sums[n] = col_sum(after(cross_blocks(grid, own, rows, width), self_sums[0]))
            fill = []
        grad_normed, fill = grid.scatter_end(state, rest, fill)
        if n > 0:
            qkv_pair, out_pair, output = fill
            self_slots_grad = self_grad_slots(grid, [qkv_pair, out_pair], grad_normed)
        grad_res, gain_one, shift_one = norm_backward(grad_normed, k["normed_one"], k["inv_one"], gains[n, 0])
        gradient = gradient + grad_res
        norms[n] = jnp.stack([gain_one, gain_two, gain_three, shift_one, shift_two, shift_three])

    cross_out_grads = [value.astype(F32) for value in cross_sums]
    input_grad = grid.tokens_out_begin(own_last(grid, gradient.astype(BF)))
    text_full = text_backward(grid, after(text_mine, rest), width)
    text_weights = [[product_tn(text_cols, text_full[:, 2 * n + side]) for side in range(2)] for n in range(LAYERS)]
    text_part = 0.0
    for n in range(LAYERS):
        for side, mats in enumerate((cross_key, cross_value)):
            text_part = text_part + product_nt(text_full[:, 2 * n + side], mats[n])
    text_grad = text_out(grid, text_part)
    early = [hidden_sums[n] for n in range(1, LAYERS)] + [self_sums[n] for n in range(1, LAYERS)]
    widths = [value.shape[1] for value in early]
    moved = jnp.concatenate([value.reshape(grid.T, rows, value.shape[1]) for value in early], axis=2)
    moved = grid.plane_a2a(after(moved, grad_normed))
    input_grad, moved = meet(input_grad, moved)
    input_grad = grid.tokens_out_end(input_grad).astype(F32)
    parts = [moved[:, :, sum(widths[:m]) : sum(widths[: m + 1])] for m in range(len(early))]
    first = [grid.plane_a2a(value[0].reshape(grid.T, rows, value[0].shape[1])) for value in (hidden_sums, self_sums)]
    hidden_out = [hidden_grad_blocks(grid, part, 2) for part in [first[0]] + parts[: LAYERS - 1]]
    self_out_grads = [self_grad_blocks(grid, part, units) for part in [first[1]] + parts[LAYERS - 1 :]]
    totals = grid.total(own_last(grid, jnp.concatenate(norms, axis=0))).reshape(LAYERS, 6, -1)
    gains_sum, shifts_sum = totals[:, :3], totals[:, 3:]

    def both(values, slot):
        return jnp.stack([values[n][slot] for n in range(LAYERS)])

    return (
        output.astype(F32),
        input_grad,
        text_grad,
        gains_sum,
        shifts_sum[:, 1:],
        shifts_sum[:, 0],
        both(self_out_grads, 0),
        both(self_out_grads, 1),
        both(self_out_grads, 2),
        both(self_out_grads, 3),
        both(cross_out_grads, 0),
        both(text_weights, 0),
        both(text_weights, 1),
        both(cross_out_grads, 1),
        both(hidden_out, 0),
        both(hidden_out, 1),
    )


def solution(mesh):
    grid = Grid(mesh)
    tokens = P(("row", "col"), None)
    text = P("row", "col", None)
    block = P(None, "row", "col")
    in_specs = (tokens, text, tokens, P(), P()) + (block,) * 10
    out_specs = (tokens, tokens, text, P(), P(), P()) + (block,) * 10

    def run(*args):
        return shards(grid, *args)

    return jax.shard_map(run, mesh=mesh, in_specs=in_specs, out_specs=out_specs, check_vma=False)
```

```python
import functools

import jax
import jax.numpy as jnp
from jax import lax
from jax.experimental import pallas as pl
from jax.experimental.pallas import tpu as pltpu
from jax.sharding import PartitionSpec as P

HEAD = 64
CLIP_LEN = 1024
LAYERS = 2
SCALE = 0.125
EPS = 1e-05
NEG = -1e30
BF = jnp.bfloat16
F32 = jnp.float32
VMEM_LIMIT = 48 * 2**20
COST = CLIP_LEN * CLIP_LEN * 8


def product(left, right):
    return jnp.dot(left, right, preferred_element_type=F32)


def product_tn(left, right):
    return lax.dot_general(left, right, (((0,), (0,)), ((), ())), preferred_element_type=F32)


def product_nt(left, right):
    return lax.dot_general(left, right, (((1,), (1,)), ((), ())), preferred_element_type=F32)


def after(value, token):
    return lax.optimization_barrier((value, token))[0]


def tied(values, others):
    leaves, tree = jax.tree.flatten(values)
    arrays = [leaf for leaf in leaves if not isinstance(leaf, int)]
    others = [leaf for leaf in jax.tree.leaves(others) if not isinstance(leaf, int)]
    done = iter(lax.optimization_barrier((arrays, others))[0])
    return jax.tree.unflatten(tree, [leaf if isinstance(leaf, int) else next(done) for leaf in leaves])


def meet(values, fill):
    return tied((values, fill), [])


def joined(pieces):
    return pieces[0] if len(pieces) == 1 else jnp.concatenate(pieces, axis=0)


def flat(pieces):
    return [array for piece in pieces for array in piece]


class Grid:
    def __init__(self, mesh):
        self.R = mesh.shape["row"]
        self.C = mesh.shape["col"]
        self.T = self.R // 2
        assert self.T == self.C
        self.groups = [[2 * i + core for i in range(self.T)] for core in range(2)]

    def at(self):
        row = lax.axis_index("row")
        self.i = row // 2
        self.core = row % 2
        self.z = lax.axis_index("col")

    def swap(self, value, d):
        return lax.ppermute(value, "row", [(r, r ^ (2 * d)) for r in range(self.R)])

    def core_swap(self, value):
        return lax.ppermute(value, "row", [(r, r ^ 1) for r in range(self.R)])

    def plane_a2a(self, value):
        return lax.all_to_all(value, "row", 0, 0, tiled=True, axis_index_groups=self.groups)

    def row_a2a(self, value):
        return lax.all_to_all(value, "row", 0, 0, tiled=True)

    def col_a2a(self, value):
        return lax.all_to_all(value, "col", 0, 0, tiled=True)

    def distances(self):
        return sorted(range(1, self.T), key=lambda d: (bin(d).count("1"), d))

    def order(self):
        return [0] + self.distances()

    def gather_begin(self, own):
        return [own] + [self.swap(own, d) for d in self.distances() if d & (d - 1) == 0]

    def gather_end(self, near):
        half = near[0].shape[0] // 2
        pieces = {d: [piece] for d, piece in zip([0] + [d for d in self.distances() if d & (d - 1) == 0], near)}

        def part(d, upper):
            if len(pieces[d]) == 2:
                return pieces[d][upper]
            return pieces[d][0][half:] if upper else pieces[d][0][:half]

        for d in self.distances():
            high = 1 << (d.bit_length() - 1)
            low = d & -d
            if high != low:
                pieces[d] = [self.swap(part(d ^ high, 0), high), self.swap(part(d ^ low, 1), low)]
        return [pieces[d] for d in self.order()]

    def gather(self, own):
        return self.gather_end(self.gather_begin(own))

    def scatter_begin(self, top):
        d = self.order()[-1]
        high = 1 << (d.bit_length() - 1)
        low = d & -d
        return [(d ^ high, 0, self.swap(top[0], high)), (d ^ low, 1, self.swap(top[1], low))]

    def scatter_end(self, state, rest, fill=()):
        held = []
        order = self.order()
        state = list(state)
        for n in reversed(range(1, self.T - 1)):
            d = order[n]
            high = 1 << (d.bit_length() - 1)
            low = d & -d
            half = rest[n].shape[0] // 2
            parts = [rest[n][:half], rest[n][half:]]
            for goal, upper, value in state:
                if goal == d:
                    parts[upper] = parts[upper] + value.astype(F32)
            parts = [part.astype(BF) for part in parts]
            if high == low:
                held.append(self.swap(joined(parts), d))
            else:
                state += [(d ^ high, 0, self.swap(parts[0], high)), (d ^ low, 1, self.swap(parts[1], low))]
        total = rest[0]
        held, fill = meet(held, fill)
        for value in held:
            total = total + value.astype(F32)
        return total, fill

    def scatter(self, top, rest, fill=()):
        return self.scatter_end(self.scatter_begin(top), rest, fill)

    def natural(self, pieces):
        by_distance = [None] * self.T
        for d, piece in zip(self.order(), pieces):
            by_distance[d] = joined(piece)
        return self.picked(by_distance, [self.i ^ m for m in range(self.T)])

    def picked(self, parts, indices):
        stacked = jnp.stack(parts)
        return [lax.dynamic_index_in_dim(stacked, index, 0, keepdims=False) for index in indices]

    def col_swap(self, value, d):
        if d == 0:
            return value
        return lax.ppermute(value, "col", [(c, c ^ d) for c in range(self.C)])

    def plane_swap(self, value, d):
        return self.swap(value, d) if d else value

    def tokens_in(self, block, mid=None):
        rows, width = block.shape
        parts = block.reshape(self.T, rows // self.T, width)
        sent = [lax.dynamic_index_in_dim(parts, self.i ^ d, 0, keepdims=False) for d in range(self.T)]
        got = [self.plane_swap(sent[d], d) for d in range(self.T)]
        got = got if mid is None else tied(got, mid)
        sent = self.picked(got, [self.i ^ self.z ^ e for e in range(self.C)])
        return joined([self.col_swap(sent[e], e) for e in range(self.C)])

    def tokens_out_begin(self, block):
        small = block.shape[0] // self.C
        return [self.col_swap(block[e * small : (e + 1) * small], e) for e in range(self.C)]

    def tokens_out_end(self, got):
        sent = self.picked(got, [self.i ^ self.z ^ d for d in range(self.T)])
        got = [self.plane_swap(sent[d], d) for d in range(self.T)]
        return joined(self.picked(got, [self.i ^ m for m in range(self.T)]))

    def tokens_out(self, block):
        return self.tokens_out_end(self.tokens_out_begin(block))

    def total(self, value):
        for d in range(self.R.bit_length() - 1):
            value = value + lax.ppermute(value, "row", [(r, r ^ (1 << d)) for r in range(self.R)])
        for d in range(self.C.bit_length() - 1):
            value = value + lax.ppermute(value, "col", [(c, c ^ (1 << d)) for c in range(self.C)])
        return value


def gelu_parts(u):
    cdf = 0.5 * (1.0 + lax.erf(u * (0.5**0.5)))
    pdf = jnp.exp(-0.5 * u * u) * (0.5 / jnp.pi) ** 0.5
    return u * cdf, cdf + u * pdf


def norm_forward(residual, gain, shift):
    row_mean = jnp.mean(residual, axis=1, keepdims=True)
    centered = residual - row_mean
    variance = jnp.mean(centered * centered, axis=1, keepdims=True)
    inv_std = lax.rsqrt(variance + EPS)
    normed = centered * inv_std
    return (normed, inv_std, (normed * gain + shift).astype(BF))


def norm_backward(grad_out, normed, inv_std, gain):
    scaled = grad_out * gain
    row_mean = jnp.mean(scaled, axis=1, keepdims=True)
    row_along = jnp.mean(scaled * normed, axis=1, keepdims=True)
    grad_in = inv_std * (scaled - row_mean - normed * row_along)
    return (grad_in, jnp.sum(grad_out * normed, axis=0), jnp.sum(grad_out, axis=0))


def to_clip(grid, at_ref, source, target):
    rows = CLIP_LEN // grid.T
    small = rows // grid.C
    for n, d in enumerate(grid.order()):
        for e in range(grid.C):
            start = pl.multiple_of((at_ref[0] ^ d) * small + (at_ref[1] ^ e) * rows, small)
            low = n * rows + e * small
            target[pl.ds(start, small), :] = source[low : low + small, :]


def from_clip(grid, at_ref, block, k, target):
    rows = CLIP_LEN // grid.T
    small = rows // grid.C
    for n, d in enumerate(grid.order()):
        start = pl.multiple_of((at_ref[0] ^ d) * small, small)
        goal = pl.multiple_of(n * rows + (at_ref[1] ^ k) * small, small)
        target[pl.ds(goal, small), :] = block[pl.ds(start, small), :]


def causal_block(scores_t, size):
    keys = lax.broadcasted_iota(jnp.int32, (size, size), 0)
    asks = lax.broadcasted_iota(jnp.int32, (size, size), 1)
    last = scores_t.shape[0] - size
    edge = jnp.where(keys <= asks, scores_t[last:], NEG)
    return edge if last == 0 else jnp.concatenate([scores_t[:last], edge], axis=0)


def dot_nt(left, right):
    return lax.dot_general(left, right, (((1,), (1,)), ((), ())), preferred_element_type=F32)


def dot_nn(left, right):
    return lax.dot_general(left, right, (((1,), (0,)), ((), ())), preferred_element_type=F32)


def flip(value):
    return value.astype(F32).T


def self_forward_kernel(grid, width, at_ref, x_ref, out_ref, sums_ref, clip, block):
    size = CLIP_LEN // grid.C
    to_clip(grid, at_ref, x_ref, clip)
    heads = range(width // HEAD)

    def lanes(which, h):
        return slice(which * width + h * HEAD, which * width + (h + 1) * HEAD)

    keys = [clip[:, lanes(1, h)] for h in heads]
    values_t = [flip(clip[:, lanes(2, h)]).astype(BF) for h in heads]
    for k in range(grid.C):
        low, high = k * size, (k + 1) * size
        outs = []
        for h in heads:
            asks = clip[low:high, lanes(0, h)] * BF(SCALE)
            scores = causal_block(dot_nt(keys[h][:high], asks), size)
            top = jnp.max(scores, axis=0, keepdims=True)
            weight = jnp.exp(scores - top)
            total = jnp.sum(weight, axis=0, keepdims=True)
            outs.append(dot_nn(values_t[h][:, :high], weight.astype(BF)) / total)
            sums_ref[h : h + 1, low:high] = top + jnp.log(total)
        both = outs[0] if len(outs) == 1 else jnp.concatenate(outs, axis=0)
        block[...] = both.T.astype(BF)
        from_clip(grid, at_ref, block, k, out_ref)


def self_backward_kernel(grid, width, at_ref, x_ref, da_ref, sums_ref, out_ref, clip, da_clip, block, acc):
    size = CLIP_LEN // grid.C
    to_clip(grid, at_ref, x_ref, clip)
    to_clip(grid, at_ref, da_ref, da_clip)
    heads = range(width // HEAD)

    def lanes(which, h):
        return slice(which * width + h * HEAD, which * width + (h + 1) * HEAD)

    keys = [clip[:, lanes(1, h)] for h in heads]
    values = [clip[:, lanes(2, h)] for h in heads]
    keys_t = [flip(keys[h]).astype(BF) for h in heads]
    for k in reversed(range(grid.C)):
        low, high = k * size, (k + 1) * size
        dq = []
        for h in heads:
            asks = clip[low:high, lanes(0, h)] * BF(SCALE)
            da = da_clip[low:high, lanes(0, h)]
            scores = causal_block(dot_nt(keys[h][:high], asks), size)
            probs = jnp.exp(scores - sums_ref[h : h + 1, low:high])
            d_probs = dot_nt(values[h][:high], da)
            inner = jnp.sum(probs * d_probs, axis=0, keepdims=True)
            d_scores = (probs * (d_probs - inner)).astype(BF)
            dk = dot_nn(d_scores, asks)
            dv = dot_nn(probs.astype(BF), da)
            if k == grid.C - 1:
                acc[:, lanes(0, h)] = dk
                acc[:, lanes(1, h)] = dv
            else:
                acc[:high, lanes(0, h)] += dk
                acc[:high, lanes(1, h)] += dv
            dq.append(dot_nn(keys_t[h][:, :high], d_scores) * SCALE)
        both = dq[0] if len(dq) == 1 else jnp.concatenate(dq, axis=0)
        block[:, :width] = both.T.astype(BF)
        block[:, width:] = acc[low:high, :].astype(BF)
        from_clip(grid, at_ref, block, k, out_ref)


def unit_spec(rows, lanes):
    return pl.BlockSpec((None, rows, lanes), lambda n, *at: (n, 0, 0))


def self_attention(grid, x):
    units, _, width = x.shape
    width //= 3
    size = CLIP_LEN // grid.C
    return pl.pallas_call(
        functools.partial(self_forward_kernel, grid, width),
        grid_spec=pltpu.PrefetchScalarGridSpec(
            num_scalar_prefetch=1,
            grid=(units,),
            in_specs=[unit_spec(CLIP_LEN, 3 * width)],
            out_specs=[unit_spec(CLIP_LEN, width), unit_spec(8, CLIP_LEN)],
            scratch_shapes=[pltpu.VMEM((CLIP_LEN, 3 * width), BF), pltpu.VMEM((size, width), BF)],
        ),
        out_shape=[
            jax.ShapeDtypeStruct((units, CLIP_LEN, width), BF),
            jax.ShapeDtypeStruct((units, 8, CLIP_LEN), F32),
        ],
        compiler_params=pltpu.CompilerParams(vmem_limit_bytes=VMEM_LIMIT),
        cost_estimate=pl.CostEstimate(
            flops=COST * units * width, bytes_accessed=CLIP_LEN * units * width * 8, transcendentals=0
        ),
        name="self_attention",
    )(jnp.stack([grid.i, grid.z]), x)


def self_attention_grad(grid, x, da, sums):
    units, _, width = da.shape
    size = CLIP_LEN // grid.C
    return pl.pallas_call(
        functools.partial(self_backward_kernel, grid, width),
        grid_spec=pltpu.PrefetchScalarGridSpec(
            num_scalar_prefetch=1,
            grid=(units,),
            in_specs=[unit_spec(CLIP_LEN, 3 * width), unit_spec(CLIP_LEN, width), unit_spec(8, CLIP_LEN)],
            out_specs=unit_spec(CLIP_LEN, 3 * width),
            scratch_shapes=[
                pltpu.VMEM((CLIP_LEN, 3 * width), BF),
                pltpu.VMEM((CLIP_LEN, width), BF),
                pltpu.VMEM((size, 3 * width), BF),
                pltpu.VMEM((CLIP_LEN, 2 * width), F32),
            ],
        ),
        out_shape=jax.ShapeDtypeStruct((units, CLIP_LEN, 3 * width), BF),
        compiler_params=pltpu.CompilerParams(vmem_limit_bytes=VMEM_LIMIT),
        cost_estimate=pl.CostEstimate(
            flops=3 * COST * units * width, bytes_accessed=CLIP_LEN * units * width * 16, transcendentals=0
        ),
        name="self_attention_grad",
    )(jnp.stack([grid.i, grid.z]), x, da, sums)


def reorder_kernel(spans, core_ref, x_ref, out_ref):
    for core in range(2):

        @pl.when(core_ref[0] == core)
        def _(core=core):
            out_ref[...] = jnp.concatenate([x_ref[:, low : low + size] for low, size in spans[core]], axis=1)


def reorder(grid, x, back):
    rows, width = x.shape
    size = width // grid.R
    half = width // 2
    if back:
        spans = [[((r % 2 != core) * half + r // 2 * size, size) for r in range(grid.R)] for core in range(2)]
    else:
        spans = [[((2 * i + (core + n) % 2) * size, size) for n in range(2) for i in range(grid.T)] for core in range(2)]
    return pl.pallas_call(
        functools.partial(reorder_kernel, spans),
        grid_spec=pltpu.PrefetchScalarGridSpec(
            num_scalar_prefetch=1,
            grid=(1,),
            in_specs=[pl.BlockSpec((rows, width), lambda n, core: (0, 0))],
            out_specs=pl.BlockSpec((rows, width), lambda n, core: (0, 0)),
        ),
        out_shape=jax.ShapeDtypeStruct((rows, width), x.dtype),
        name="reorder",
    )(grid.core.reshape(1), x)


def own_first(grid, x):
    return reorder(grid, x, False)


def own_last(grid, x):
    return reorder(grid, x, True)


def lanes_of(ref, mats):
    parts = [ref[m] for m in mats]
    return parts[0] if len(parts) == 1 else jnp.concatenate(parts, axis=1)


def columns_kernel(mats, count, kind, *refs):
    pieces, (own_ref, other_ref), rest = refs[:count], refs[count : count + 2], refs[count + 2 :]
    own, other = lanes_of(own_ref, mats), lanes_of(other_ref, mats)
    half = own.shape[0]
    low = 0
    for piece in pieces:
        high = low + piece.shape[0]
        out = dot_nn(piece[:, :half], own) + dot_nn(piece[:, half:], other)
        if kind == "gelu":
            value, slope = gelu_parts(out)
            rest[0][low:high] = value.astype(BF)
            rest[1][low:high] = slope.astype(BF)
        elif kind == "slope":
            rest[1][low:high] = (out * rest[0][low:high].astype(F32)).astype(BF)
        else:
            rest[0][low:high] = out.astype(BF)
        low = high


def whole(array):
    return pl.BlockSpec(array.shape, lambda n: (0,) * array.ndim)


def act_spec(rows, lanes):
    return pl.BlockSpec((None, rows, lanes), lambda n: (n, 0, 0))


def columns_product(pieces, weights, mats, kind="plain", slope=None):
    own, other = weights
    blocks, _, half, wide = own.shape
    lanes = len(mats) * wide
    rows = sum(p.shape[0] for p in pieces)
    extra = [] if slope is None else [slope]
    outs = 2 if kind == "gelu" else 1
    shape = jax.ShapeDtypeStruct((blocks, rows, lanes), BF)
    first, picked = (mats[0], 1) if len(mats) == 1 else (0, own.shape[1])
    spec = pl.BlockSpec((None, picked) + own.shape[2:], lambda n: (n, first, 0, 0))
    result = pl.pallas_call(
        functools.partial(columns_kernel, (0,) if len(mats) == 1 else mats, len(pieces), kind),
        grid=(blocks,),
        in_specs=[whole(p) for p in pieces] + [spec, spec] + [act_spec(rows, lanes)] * len(extra),
        out_specs=[act_spec(rows, lanes)] * outs,
        out_shape=[shape] * outs,
        compiler_params=pltpu.CompilerParams(vmem_limit_bytes=VMEM_LIMIT),
        cost_estimate=pl.CostEstimate(flops=4 * half * rows * lanes * blocks, bytes_accessed=4 * half * lanes * blocks, transcendentals=0),
        name="columns_" + kind,
    )(*pieces, own, other, *extra)
    return result if outs > 1 else result[0]


def rows_kernel(mats, low, high, act_ref, own_ref, other_ref, *outs):
    blocks = act_ref.shape[0]
    acts = [act_ref[n, low:high] for n in range(blocks)]
    half = own_ref.shape[2]
    for cols, ref in ((slice(0, half), own_ref), (slice(half, 2 * half), other_ref)):
        parts = [lanes_of(ref.at[n], mats) for n in range(blocks)]
        if parts[0].shape[1] < 256:
            total = dot_nt(jnp.concatenate(acts, axis=1), jnp.concatenate(parts, axis=1))
        else:
            total = dot_nt(acts[0], parts[0])
            for act, part in zip(acts[1:], parts[1:]):
                total = total + dot_nt(act, part)
        at = 0
        for out in outs:
            out[:, cols] = total[at : at + out.shape[0]].astype(out.dtype)
            at += out.shape[0]


def rows_product(act, weights, mats, low, high, shapes):
    own, other = weights
    blocks, _, half, _ = own.shape
    lanes = act.shape[2]
    first, count = (mats[0], 1) if len(mats) == 1 else (0, own.shape[1])
    spec = pl.BlockSpec((blocks, count) + own.shape[2:], lambda n: (0, first, 0, 0))
    return pl.pallas_call(
        functools.partial(rows_kernel, (0,) if len(mats) == 1 else mats, low, high),
        grid=(1,),
        in_specs=[whole(act), spec, spec],
        out_specs=[whole(s) for s in shapes],
        out_shape=shapes,
        compiler_params=pltpu.CompilerParams(vmem_limit_bytes=VMEM_LIMIT),
        cost_estimate=pl.CostEstimate(
            flops=4 * half * (high - low) * lanes * blocks, bytes_accessed=4 * half * lanes * blocks, transcendentals=0
        ),
        name="rows",
    )(act, own, other)


def rows_top(grid, act, weights, mats):
    rows = act.shape[1] // grid.T
    shapes = [jax.ShapeDtypeStruct((rows // 2, 2 * weights[0].shape[2]), BF)] * 2
    return list(rows_product(act, weights, mats, rows * (grid.T - 1), rows * grid.T, shapes))


def rows_rest(grid, act, weights, mats):
    rows = act.shape[1] // grid.T
    shapes = [jax.ShapeDtypeStruct((rows, 2 * weights[0].shape[2]), F32)] * (grid.T - 1)
    return list(rows_product(act, weights, mats, 0, rows * (grid.T - 1), shapes))


def rows_terms(grid, act, weights, mats):
    top = rows_top(grid, act, weights, mats)
    return top, rows_rest(grid, after(act, top), weights, mats)


def grads_kernel(count, *refs):
    pieces, y_ref, keep_ref, send_ref, turned = refs[:count], refs[count], refs[count + 1], refs[count + 2], refs[count + 3]
    half = keep_ref.shape[0]

    @pl.when(pl.program_id(0) == 0)
    def _():
        low = 0
        for piece in pieces:
            high = low + piece.shape[0]
            turned[:, low:high] = piece[...].T
            low = high

    y = y_ref[...]
    keep_ref[...] = dot_nn(turned[:half], y).astype(BF)
    send_ref[...] = dot_nn(turned[half:], y).astype(BF)


def weight_grads(pieces, y):
    blocks, rows, lanes = y.shape
    width = pieces[0].shape[1]
    half = width // 2
    shape = jax.ShapeDtypeStruct((blocks, half, lanes), BF)
    return pl.pallas_call(
        functools.partial(grads_kernel, len(pieces)),
        grid=(blocks,),
        in_specs=[whole(p) for p in pieces] + [act_spec(rows, lanes)],
        out_specs=[act_spec(half, lanes)] * 2,
        out_shape=[shape] * 2,
        scratch_shapes=[pltpu.VMEM((width, rows), BF)],
        compiler_params=pltpu.CompilerParams(vmem_limit_bytes=VMEM_LIMIT),
        cost_estimate=pl.CostEstimate(flops=4 * half * rows * lanes * blocks, bytes_accessed=4 * half * lanes * blocks, transcendentals=0),
        name="weight_grads",
    )(*pieces, y)


def cross_scores(keys, asks):
    scores = dot_nt(keys, asks)
    top = jnp.max(scores, axis=0, keepdims=True)
    weight = jnp.exp(scores - top)
    return weight / jnp.sum(weight, axis=0, keepdims=True)


def cross_forward_kernel(q_ref, k_ref, v_ref, out_ref):
    for low in range(0, q_ref.shape[1], 2 * HEAD):
        pair = []
        for at in (slice(low, low + HEAD), slice(low + HEAD, low + 2 * HEAD)):
            probs = cross_scores(k_ref[:, at], q_ref[:, at] * BF(SCALE)).astype(BF)
            pair.append(dot_nn(flip(v_ref[:, at]).astype(BF), probs))
        out_ref[:, low : low + 2 * HEAD] = jnp.concatenate(pair, axis=0).T.astype(BF)


def cross_backward_kernel(q_ref, k_ref, v_ref, dc_ref, dq_ref, dk_ref, dv_ref):
    for low in range(0, q_ref.shape[1], 2 * HEAD):
        pair, dk, dv = [], [], []
        for at in (slice(low, low + HEAD), slice(low + HEAD, low + 2 * HEAD)):
            asks = q_ref[:, at] * BF(SCALE)
            probs = cross_scores(k_ref[:, at], asks)
            d_probs = dot_nt(v_ref[:, at], dc_ref[:, at])
            inner = jnp.sum(probs * d_probs, axis=0, keepdims=True)
            d_scores = (probs * (d_probs - inner)).astype(BF)
            dk.append(dot_nn(d_scores, asks))
            dv.append(dot_nn(probs.astype(BF), dc_ref[:, at]))
            pair.append(dot_nn(flip(k_ref[:, at]).astype(BF), d_scores) * SCALE)
        at = slice(low, low + 2 * HEAD)
        dq_ref[:, at] = jnp.concatenate(pair, axis=0).T.astype(BF)
        dk_ref[:, at] = jnp.concatenate(dk, axis=1)
        dv_ref[:, at] = jnp.concatenate(dv, axis=1)


def cross_call(kernel, name, arrays, outs):
    width = arrays[0].shape[1]
    lanes = 512 if width % 512 == 0 else width

    def spec(rows):
        return pl.BlockSpec((rows, lanes), lambda n: (0, n))

    return pl.pallas_call(
        kernel,
        grid=(width // lanes,),
        in_specs=[spec(a.shape[0]) for a in arrays],
        out_specs=[spec(rows) for rows, _ in outs],
        out_shape=[jax.ShapeDtypeStruct((rows, width), kind) for rows, kind in outs],
        compiler_params=pltpu.CompilerParams(vmem_limit_bytes=VMEM_LIMIT),
        cost_estimate=pl.CostEstimate(
            flops=arrays[0].shape[0] * arrays[1].shape[0] * width * 20, bytes_accessed=2**22, transcendentals=0
        ),
        name=name,
    )(*arrays)


def cross_attention(queries, keys, values):
    return cross_call(cross_forward_kernel, "cross_attention", [queries, keys, values], [(queries.shape[0], BF)])[0]


def cross_attention_grad(queries, keys, values, grad_out):
    outs = [(queries.shape[0], BF), (keys.shape[0], F32), (keys.shape[0], F32)]
    return cross_call(cross_backward_kernel, "cross_attention_grad", [queries, keys, values, grad_out], outs)


def head_units(grid, width):
    heads = width // HEAD
    per_unit = -(-heads // grid.T)
    assert heads % per_unit == 0
    return heads // per_unit, per_unit * HEAD


def self_slots(grid, mats):
    units, wide = head_units(grid, mats[0].shape[1])
    both = jnp.stack(mats)
    lows = [jnp.minimum((s - grid.z - 1) % grid.T, units - 1) * wide for s in range(grid.T)]
    return jnp.stack([lax.dynamic_slice_in_dim(both, low, wide, axis=2) for low in lows])


def by_matrix(moved):
    sources, count, rows, wide = moved.shape
    return moved.transpose(1, 0, 2, 3).reshape(count, sources * rows, wide)


def self_weights(grid, slots, units):
    half = jnp.stack(
        [lax.dynamic_index_in_dim(slots, (grid.i - 1 - m) % grid.T, 0, keepdims=False) for m in range(units)]
    )
    return half, grid.core_swap(half)


def core_sum(grid, keep, send, mid):
    got = tied(grid.core_swap(send), mid)
    return (keep.astype(F32) + got.astype(F32)).astype(BF)


def self_grad_slots(grid, pairs, mid):
    half = jnp.concatenate([core_sum(grid, *pair, mid) for pair in pairs], axis=2)
    half = jnp.concatenate([half, jnp.zeros((grid.C - half.shape[0],) + half.shape[1:], BF)], axis=0)
    return jnp.stack(
        [lax.dynamic_index_in_dim(half, (grid.i - c - 1) % grid.T, 0, keepdims=False) for c in range(grid.C)]
    )


def self_grad_blocks(grid, moved, units):
    wide = moved.shape[2] // 4
    mine = [lax.dynamic_index_in_dim(moved, (grid.z + 1 + m) % grid.T, 0, keepdims=False) for m in range(units)]
    return [
        jnp.concatenate([part[:, n * wide : (n + 1) * wide] for part in mine], axis=1).astype(F32) for n in range(4)
    ]


def hidden_slots(grid, mats):
    rows, width = mats[0].shape
    count = len(mats)
    return jnp.stack(mats).reshape(count, rows, grid.T, width // grid.T).transpose(2, 0, 1, 3)


def hidden_gathered(moved, n, token):
    sources, _, rows, wide = moved.shape
    return lax.all_gather(after(moved[:, n].reshape(1, sources * rows, wide), token), "col", axis=0)


def with_other(grid, own):
    return own, grid.core_swap(own)


def hidden_grad_slots(grid, pairs, mid):
    return jnp.concatenate([core_sum(grid, *pair, mid) for pair in pairs], axis=2)


def col_sum(slots):
    return lax.psum_scatter(slots, "col", scatter_dimension=0)


def hidden_grad_blocks(grid, moved, count):
    rows, wide = moved.shape[1], moved.shape[2] // count
    return [
        moved[:, :, n * wide : (n + 1) * wide].transpose(1, 0, 2).reshape(rows, -1).astype(F32) for n in range(count)
    ]


def cross_columns(grid, blocks):
    _, count, rows, width = blocks.shape
    return blocks.transpose(1, 2, 0, 3).reshape(count * rows, grid.C * width)


def cross_weights(grid, pieces, count):
    half = jnp.stack(grid.natural(pieces))
    width = half.shape[2]
    half = half.reshape(grid.T, count, -1, width).transpose(1, 0, 2, 3).reshape(count, -1, width)
    other = grid.core_swap(half)
    return [joined([half[n], other[n]]) for n in range(count)]


def cross_core_sum(grid, lows, mid):
    edge = lows[0].shape[0] // 2
    return [core_sum(grid, low[:edge], low[edge:], mid) for low in lows]


def cross_terms(grid, halves, rows, width):
    halves = [half.reshape(grid.T, rows, grid.C * width) for half in halves]

    def term(d):
        return joined([lax.dynamic_index_in_dim(half, grid.i ^ d, 0, keepdims=False) for half in halves])

    order = grid.order()
    top = term(order[-1])
    size = top.shape[0] // 2
    return [top[:size], top[size:]], [term(d).astype(F32) for d in order[:-1]]


def cross_blocks(grid, own, rows, width):
    return own.astype(BF).reshape(-1, rows, grid.C, width).transpose(2, 0, 1, 3)


def text_columns(grid, text):
    _, own, width = text.shape
    parts = text.reshape(own, grid.R, width // grid.R).transpose(1, 0, 2)
    parts = grid.row_a2a(parts)
    pieces = [parts] + [
        lax.ppermute(parts, "col", [(c, c ^ d) for c in range(grid.C)]) for d in range(1, grid.C)
    ]
    stacked = jnp.stack(pieces)
    order = [lax.dynamic_index_in_dim(stacked, grid.z ^ c, 0, keepdims=False) for c in range(grid.C)]
    return jnp.stack(order, axis=1).reshape(-1, width // grid.R)


def text_parts(grid, columns, mats):
    count, rows, width = mats.shape
    own = columns.shape[0] // (grid.R * grid.C)
    part = product(columns, mats.transpose(1, 0, 2).reshape(rows, count * width)).astype(BF)
    part = part.reshape(grid.T, 2, grid.C, own, count * width).transpose(2, 1, 0, 3, 4)
    return grid.row_a2a(part.reshape(grid.R, grid.T * own, count * width))


def text_shared(grid, moved):
    own = moved.shape[1] // grid.T
    summed = jnp.sum(moved.astype(F32), axis=0).astype(BF).reshape(grid.T, own, moved.shape[2])
    sent = grid.picked(list(summed), [grid.z ^ e for e in range(grid.C)])
    return [grid.col_swap(sent[e], e) for e in range(grid.C)]


def text_states_of(grid, got, count):
    own, width = got[0].shape[0], got[0].shape[1] // count
    blocks = jnp.stack(grid.picked(got, [grid.z ^ c for c in range(grid.C)]))
    mine = blocks.reshape(grid.C, own, count, width).transpose(1, 2, 0, 3)
    mine = mine.reshape(own, count * grid.C * width)
    full = joined(flat(grid.gather(mine)))
    return full.reshape(-1, count, grid.C * width)


def text_begin(grid, grads):
    own = grads.shape[0] // grid.T
    pieces = grads.reshape(grid.T, own, -1)
    top = pieces[grid.T - 1].astype(BF)
    return grid.scatter_begin([top[: own // 2], top[own // 2 :]]), [pieces[n] for n in range(grid.T - 1)]


def text_backward(grid, mine, width):
    own = mine.shape[0]
    mine = mine.reshape(own, -1, grid.C, width).transpose(2, 0, 1, 3)
    moved = grid.col_a2a(mine)
    other = grid.core_swap(moved)
    pair = jnp.stack(
        [jnp.where(grid.core == 0, moved, other), jnp.where(grid.core == 0, other, moved)], axis=1
    )
    shape = pair.shape
    flat = pair.reshape(shape[0] * 2, -1)
    full = jnp.stack(grid.natural(grid.gather(flat)), axis=1)
    return full.reshape(-1, shape[3], width)


def text_out(grid, part):
    own = part.shape[0] // (grid.R * grid.C)
    cols = part.shape[1]
    parts = part.astype(BF).reshape(grid.R, grid.C, own, cols).transpose(1, 0, 2, 3)
    moved = grid.col_a2a(parts).astype(F32)
    summed = jnp.sum(moved, axis=0).astype(BF)
    moved = grid.row_a2a(summed)
    return moved.transpose(1, 0, 2).reshape(1, own, grid.R * cols).astype(F32)


def shards(
    grid,
    inputs,
    text_states,
    cotangent,
    norm_gains,
    norm_shifts,
    self_query,
    self_key,
    self_value,
    self_out,
    cross_query,
    cross_key,
    cross_value,
    cross_out,
    mlp_up,
    mlp_down,
):
    grid.at()
    last = LAYERS - 1
    rows, width = self_query.shape[1:]
    units, _ = head_units(grid, width)

    self_parts = [self_slots(grid, [w[n] for w in (self_query, self_key, self_value, self_out)]) for n in range(LAYERS)]
    hidden_parts = [hidden_slots(grid, [mlp_up[n], mlp_down[n]]) for n in range(LAYERS)]
    self_moved = [None] * LAYERS
    hidden_moved = [None] * LAYERS
    self_full = [None] * LAYERS
    self_moved[0] = grid.plane_a2a(self_parts[0])
    sent = by_matrix(self_moved[0])
    cross_parts = [jnp.stack([cross_query[n], cross_out[n]]) for n in range(LAYERS)]
    tokens = grid.tokens_in(jnp.concatenate([inputs, cotangent.astype(BF)], axis=1))
    tokens, sent = meet(tokens, sent)
    text_cols = text_columns(grid, after(text_states, tokens))
    gradient = tokens[:, inputs.shape[1] :]
    tokens = tokens[:, : inputs.shape[1]]
    self_full[0] = lax.all_gather(sent, "col", axis=0)
    residual = own_first(grid, tokens).astype(F32)
    norm_rows = after(jnp.concatenate([norm_gains, norm_shifts], axis=1), tokens)
    norm_rows = own_first(grid, norm_rows.reshape(-1, norm_rows.shape[2])).reshape(norm_rows.shape)
    gains, shifts = norm_rows[:, :3], norm_rows[:, 3:]
    text_mats = jnp.stack([mat for n in range(LAYERS) for mat in (cross_key[n], cross_value[n])])

    kept = [dict() for _ in range(LAYERS)]
    w_self = [None] * LAYERS
    w_cross = [None] * LAYERS
    w_hidden = [None] * LAYERS
    for n in range(LAYERS):
        k = kept[n]
        k["normed_one"], k["inv_one"], low_one = norm_forward(residual, gains[n, 0], shifts[n, 0])
        near_one = grid.gather_begin(low_one)
        if n == 0:
            hidden_moved[0] = grid.plane_a2a(after(hidden_parts[0], near_one))
            text_moved = text_parts(grid, after(text_cols, near_one), text_mats)
        full_one = flat(grid.gather_end(near_one))
        if n == 0:
            (self_full[0], full_one), (text_sent, hidden_moved[0]) = meet(
                (self_full[0], full_one), (text_shared(grid, text_moved), hidden_moved[0])
            )
            cross_full = lax.all_gather(after(cross_parts[0], sent), "col", axis=0)
        else:
            self_full[n] = after(self_full[n], residual)
        k["full_one"] = full_one
        w_self[n] = self_weights(grid, self_full[n], units)
        k["qkv"] = columns_product(full_one, w_self[n], (0, 1, 2))
        k["attn_low"], k["sums_self"] = self_attention(grid, k["qkv"])
        if n > 0:
            next_near = grid.gather_begin(cross_columns(grid, after(cross_full, full_one)))
            k["attn_low"], next_near = meet(k["attn_low"], next_near)
            w_cross[n] = cross_weights(grid, grid.gather_end(next_near), 2)
        up_full = hidden_gathered(hidden_moved[n], 0, full_one if n == 0 else hidden_moved[n])
        down_full = hidden_gathered(hidden_moved[n], 1, k["qkv"])
        top, rest = rows_terms(grid, k["attn_low"], w_self[n], (3,))
        fill = []
        if n == 0:
            next_near = grid.gather_begin(cross_columns(grid, after(cross_full, k["qkv"])))
            rest, next_near = meet(rest, next_near)
            w_cross[0] = cross_weights(grid, grid.gather_end(next_near), 2)
        if n == 0:
            text_all = text_states_of(grid, tied(text_sent, top), 2 * LAYERS)
        added, _ = grid.scatter(top, rest)
        residual = residual + added
        w_up = with_other(grid, after(up_full, residual))
        before_cross = residual
        k["text"] = [text_all[:, 2 * n + side] for side in range(2)]
        k["normed_two"], k["inv_two"], k["low_two"] = norm_forward(residual, gains[n, 1], shifts[n, 1])
        k["cross_queries"] = product(k["low_two"], w_cross[n][0]).astype(BF)
        k["cross_low"] = cross_attention(k["cross_queries"], *k["text"])
        residual = residual + product_nt(k["cross_low"], w_cross[n][1])
        k["normed_three"], k["inv_three"], low_three = norm_forward(residual, gains[n, 2], shifts[n, 2])
        if n < last:
            w_down = with_other(grid, after(down_full, before_cross))
            w_down, low_three = meet(w_down, low_three)
            sent = by_matrix(grid.plane_a2a(after(self_parts[n + 1], before_cross)))
            low_three, sent = meet(low_three, sent)
            self_full[n + 1] = lax.all_gather(sent, "col", axis=0)
            cross_full = lax.all_gather(after(cross_parts[n + 1], sent), "col", axis=0)
        if n == last:
            low_three, next_near = meet(low_three, grid.gather_begin(after(gradient, before_cross)))
        k["full_three"] = flat(grid.gather(low_three))
        if n < last:
            hidden_moved[n + 1] = grid.plane_a2a(after(hidden_parts[n + 1], low_three))
            k["full_three"], hidden_moved[n + 1] = meet(k["full_three"], hidden_moved[n + 1])
        k["hidden_low"], k["hidden_slope"] = columns_product(k["full_three"], w_up, (0,), "gelu")
        if n == last:
            w_down = with_other(grid, after(down_full, k["hidden_low"]))
        w_hidden[n] = (w_up, w_down)
        if n < last:
            top, rest = rows_terms(grid, k["hidden_low"], w_hidden[n][1], (0,))
            gradient = own_first(grid, after(gradient, rest)) if n == 0 else gradient
            added, gradient = grid.scatter(top, rest, gradient)
            residual = residual + added
        else:
            dy_three = flat(grid.gather_end(next_near))
            gradient = gradient.astype(F32)

    before_last = residual
    hidden_sums = [None] * LAYERS
    self_sums = [None] * LAYERS
    cross_sums = [None] * LAYERS
    text_grads = [None] * LAYERS
    norms = [None] * LAYERS
    fill = []
    for n in range(last, -1, -1):
        k = kept[n]
        w_up, w_down = w_hidden[n]
        if n < last:
            sent, slots = meet(gradient.astype(BF), self_slots_grad)
            self_sums[n + 1] = col_sum(slots)
            cross_terms_late = cross_terms(grid, cross_core_sum(grid, cross_lows, sent), rows, width)
            dy_three, cross_terms_late = meet(flat(grid.gather(sent)), cross_terms_late)
        if n == last:
            late_top, late_rest = rows_terms(grid, k["hidden_low"], w_down, (0,))
            late_state = grid.scatter_begin(late_top)
            dy_three, late_rest = meet(dy_three, late_rest)
        d_pre = columns_product(dy_three, w_down, (0,), "slope", k["hidden_slope"])
        top, rest = rows_terms(grid, d_pre, w_up, (0,))
        state = grid.scatter_begin(top)
        if n < last:
            (state, rest), cross_state = meet((state, rest), grid.scatter_begin(cross_terms_late[0]))
        hidden_pairs = [
            weight_grads(after(k["full_three"], state), d_pre),
            weight_grads(after(dy_three, state), k["hidden_low"]),
        ]
        if n == last:
            late_state = tied(late_state, rest)
        grad_normed, hidden_pairs = grid.scatter_end(state, rest, hidden_pairs)
        grad_res, gain_three, shift_three = norm_backward(grad_normed, k["normed_three"], k["inv_three"], gains[n, 2])
        gradient = gradient + grad_res
        if n < last:
            gradient, hidden_sums[n + 1] = meet(gradient, hidden_sums[n + 1])
        before_cross = gradient
        if n == last:
            late_sum, _ = grid.scatter_end(tied(late_state, gradient), late_rest)
        dy_two = gradient.astype(BF)
        d_cross = product(dy_two, w_cross[n][1]).astype(BF)
        d_cquery, d_ckey, d_cvalue = cross_attention_grad(k["cross_queries"], *k["text"], d_cross)
        grad_normed = product_nt(d_cquery, w_cross[n][0])
        text_grads[n] = jnp.concatenate([d_ckey, d_cvalue], axis=1)
        grad_res, gain_two, shift_two = norm_backward(grad_normed, k["normed_two"], k["inv_two"], gains[n, 1])
        gradient = gradient + grad_res
        sent = gradient.astype(BF)
        if n == last:
            sent, late_sum = meet(sent, late_sum)
            fill = own_last(grid, (before_last + late_sum).astype(BF))
        else:
            sent, hidden_slots_grad = meet(sent, hidden_grad_slots(grid, hidden_pairs, grad_normed))
            hidden_sums[n] = col_sum(hidden_slots_grad)
            fill = ()
        dy_one, fill = meet(flat(grid.gather(sent)), fill)
        if n == last:
            output = grid.tokens_out_begin(fill)
        d_attn = columns_product(dy_one, w_self[n], (3,))
        d_qkv = self_attention_grad(grid, k["qkv"], d_attn, k["sums_self"])
        if n == 0:
            text_state, text_rest = text_begin(grid, after(jnp.concatenate(text_grads, axis=1), dy_one))
            d_qkv, (text_state, self_sums[1:]) = meet(d_qkv, (text_state, self_sums[1:]))
        if n == last:
            d_qkv, output = meet(d_qkv, output)
            output = grid.tokens_out_end(output)

        def cross_products(token):
            return [
                product_tn(after(k["low_two"], token), d_cquery).astype(BF),
                product_tn(after(dy_two, token), k["cross_low"]).astype(BF),
            ]

        if n > 0:
            top, rest = rows_terms(grid, d_qkv, w_self[n], (0, 1, 2))
            state = grid.scatter_begin(top)
            qkv_pair = weight_grads(after(k["full_one"], state), d_qkv)
            out_pair = weight_grads(after(dy_one, state), k["attn_low"])
            fill = [qkv_pair, out_pair, output, hidden_grad_slots(grid, hidden_pairs, state), cross_products(state)]
        else:
            qkv_pair = weight_grads(k["full_one"], d_qkv)
            out_pair = weight_grads(dy_one, after(k["attn_low"], d_qkv))
            text_mine = grid.scatter_end(text_state, text_rest)[0].astype(BF)
            own, _ = grid.scatter_end(tied(cross_state, dy_one), cross_terms_late[1])
            out_pair, (text_mine, own) = meet(out_pair, (text_mine, cross_blocks(grid, own, rows, width)))
            cross_sums[n + 1] = own
            top = rows_top(grid, after(d_qkv, [qkv_pair, out_pair]), w_self[n], (0, 1, 2))
            state = grid.scatter_begin(top)
            top, slots = meet(top, self_grad_slots(grid, [qkv_pair, out_pair], out_pair))
            self_sums[0] = col_sum(slots)
            rest = rows_rest(grid, after(d_qkv, slots), w_self[n], (0, 1, 2))
            fill = cross_terms(grid, cross_core_sum(grid, cross_products(state), state), rows, width)
        grad_normed, fill = grid.scatter_end(state, rest, fill)
        if n == 0:
            cross_state, cross_last = grid.scatter_begin(fill[0]), fill[1]
        if n > 0:
            qkv_pair, out_pair, output, hidden_slots_grad, cross_lows = fill
            hidden_sums[n] = col_sum(hidden_slots_grad)
            self_slots_grad = self_grad_slots(grid, [qkv_pair, out_pair], grad_normed)
        grad_res, gain_one, shift_one = norm_backward(grad_normed, k["normed_one"], k["inv_one"], gains[n, 0])
        gradient = gradient + grad_res
        norms[n] = jnp.stack([gain_one, gain_two, gain_three, shift_one, shift_two, shift_three])

    gradient, cross_state = meet(gradient.astype(BF), cross_state)
    input_grad = grid.tokens_out_begin(own_last(grid, gradient))
    text_full = text_backward(grid, after(text_mine, grad_normed), width)
    own, _ = grid.scatter_end(cross_state, cross_last)
    text_full, cross_sums[0] = meet(text_full, cross_blocks(grid, own, rows, width))
    cross_all, self_sums[0] = meet(jnp.concatenate(cross_sums, axis=1), self_sums[0])
    cross_all = col_sum(cross_all).astype(F32)
    cross_out_grads = [cross_all[2 * n : 2 * n + 2] for n in range(LAYERS)]
    text_weights = [[product_tn(text_cols, text_full[:, 2 * n + side]) for side in range(2)] for n in range(LAYERS)]
    text_part = 0.0
    for n in range(LAYERS):
        for side, mats in enumerate((cross_key, cross_value)):
            text_part = text_part + product_nt(text_full[:, 2 * n + side], mats[n])
    text_grad = text_out(grid, text_part)
    early = [hidden_sums[n] for n in range(1, LAYERS)] + [self_sums[n] for n in range(1, LAYERS)]
    widths = [value.shape[1] for value in early]
    moved = jnp.concatenate([value.reshape(grid.T, rows, value.shape[1]) for value in early], axis=2)
    moved = grid.plane_a2a(after(moved, grad_normed))
    input_grad, (moved, hidden_sums[0]) = meet(input_grad, (moved, hidden_sums[0]))
    input_grad = grid.tokens_out_end(input_grad).astype(F32)
    parts = [moved[:, :, sum(widths[:m]) : sum(widths[: m + 1])] for m in range(len(early))]
    first = [grid.plane_a2a(value[0].reshape(grid.T, rows, value[0].shape[1])) for value in (hidden_sums, self_sums)]
    hidden_out = [hidden_grad_blocks(grid, part, 2) for part in [first[0]] + parts[: LAYERS - 1]]
    self_out_grads = [self_grad_blocks(grid, part, units) for part in [first[1]] + parts[LAYERS - 1 :]]
    totals = grid.total(own_last(grid, jnp.concatenate(norms, axis=0))).reshape(LAYERS, 6, -1)
    gains_sum, shifts_sum = totals[:, :3], totals[:, 3:]

    def both(values, slot):
        return jnp.stack([values[n][slot] for n in range(LAYERS)])

    return (
        output.astype(F32),
        input_grad,
        text_grad,
        gains_sum,
        shifts_sum[:, 1:],
        shifts_sum[:, 0],
        both(self_out_grads, 0),
        both(self_out_grads, 1),
        both(self_out_grads, 2),
        both(self_out_grads, 3),
        both(cross_out_grads, 0),
        both(text_weights, 0),
        both(text_weights, 1),
        both(cross_out_grads, 1),
        both(hidden_out, 0),
        both(hidden_out, 1),
    )


def solution(mesh):
    grid = Grid(mesh)
    tokens = P(("row", "col"), None)
    text = P("row", "col", None)
    block = P(None, "row", "col")
    in_specs = (tokens, text, tokens, P(), P()) + (block,) * 10
    out_specs = (tokens, tokens, text, P(), P(), P()) + (block,) * 10

    def run(*args):
        return shards(grid, *args)

    return jax.shard_map(run, mesh=mesh, in_specs=in_specs, out_specs=out_specs, check_vma=False)
```

```python
import functools

import jax
import jax.numpy as jnp
from jax import lax
from jax.experimental import pallas as pl
from jax.experimental.pallas import tpu as pltpu
from jax.sharding import PartitionSpec as P

HEAD = 64
CLIP_LEN = 1024
LAYERS = 2
SCALE = 0.125
EPS = 1e-05
NEG = -1e30
BF = jnp.bfloat16
F32 = jnp.float32
VMEM_LIMIT = 48 * 2**20
COST = CLIP_LEN * CLIP_LEN * 8


def product(left, right):
    return jnp.dot(left, right, preferred_element_type=F32)


def product_tn(left, right):
    return lax.dot_general(left, right, (((0,), (0,)), ((), ())), preferred_element_type=F32)


def product_nt(left, right):
    return lax.dot_general(left, right, (((1,), (1,)), ((), ())), preferred_element_type=F32)


def after(value, token):
    return lax.optimization_barrier((value, token))[0]


def tied(values, others):
    leaves, tree = jax.tree.flatten(values)
    arrays = [leaf for leaf in leaves if not isinstance(leaf, int)]
    others = [leaf for leaf in jax.tree.leaves(others) if not isinstance(leaf, int)]
    done = iter(lax.optimization_barrier((arrays, others))[0])
    return jax.tree.unflatten(tree, [leaf if isinstance(leaf, int) else next(done) for leaf in leaves])


def meet(values, fill):
    return tied((values, fill), [])


def joined(pieces):
    return pieces[0] if len(pieces) == 1 else jnp.concatenate(pieces, axis=0)


def flat(pieces):
    return [array for piece in pieces for array in piece]


class Grid:
    def __init__(self, mesh):
        self.R = mesh.shape["row"]
        self.C = mesh.shape["col"]
        self.T = self.R // 2
        assert self.T == self.C
        self.groups = [[2 * i + core for i in range(self.T)] for core in range(2)]

    def at(self):
        row = lax.axis_index("row")
        self.i = row // 2
        self.core = row % 2
        self.z = lax.axis_index("col")

    def swap(self, value, d):
        return lax.ppermute(value, "row", [(r, r ^ (2 * d)) for r in range(self.R)])

    def core_swap(self, value):
        return lax.ppermute(value, "row", [(r, r ^ 1) for r in range(self.R)])

    def plane_a2a(self, value):
        return lax.all_to_all(value, "row", 0, 0, tiled=True, axis_index_groups=self.groups)

    def row_a2a(self, value):
        return lax.all_to_all(value, "row", 0, 0, tiled=True)

    def col_a2a(self, value):
        return lax.all_to_all(value, "col", 0, 0, tiled=True)

    def distances(self):
        return sorted(range(1, self.T), key=lambda d: (bin(d).count("1"), d))

    def order(self):
        return [0] + self.distances()

    def gather_begin(self, own):
        return [own] + [self.swap(own, d) for d in self.distances() if d & (d - 1) == 0]

    def gather_end(self, near):
        half = near[0].shape[0] // 2
        pieces = {d: [piece] for d, piece in zip([0] + [d for d in self.distances() if d & (d - 1) == 0], near)}

        def part(d, upper):
            if len(pieces[d]) == 2:
                return pieces[d][upper]
            return pieces[d][0][half:] if upper else pieces[d][0][:half]

        for d in self.distances():
            high = 1 << (d.bit_length() - 1)
            low = d & -d
            if high != low:
                pieces[d] = [self.swap(part(d ^ high, 0), high), self.swap(part(d ^ low, 1), low)]
        return [pieces[d] for d in self.order()]

    def gather(self, own):
        return self.gather_end(self.gather_begin(own))

    def scatter_begin(self, top):
        d = self.order()[-1]
        high = 1 << (d.bit_length() - 1)
        low = d & -d
        return [(d ^ high, 0, self.swap(top[0], high)), (d ^ low, 1, self.swap(top[1], low))]

    def scatter_end(self, state, rest, fill=()):
        held = []
        order = self.order()
        state = list(state)
        for n in reversed(range(1, self.T - 1)):
            d = order[n]
            high = 1 << (d.bit_length() - 1)
            low = d & -d
            half = rest[n].shape[0] // 2
            parts = [rest[n][:half], rest[n][half:]]
            for goal, upper, value in state:
                if goal == d:
                    parts[upper] = parts[upper] + value.astype(F32)
            parts = [part.astype(BF) for part in parts]
            if high == low:
                held.append(self.swap(joined(parts), d))
            else:
                state += [(d ^ high, 0, self.swap(parts[0], high)), (d ^ low, 1, self.swap(parts[1], low))]
        total = rest[0]
        held, fill = meet(held, fill)
        for value in held:
            total = total + value.astype(F32)
        return total, fill

    def scatter(self, top, rest, fill=()):
        return self.scatter_end(self.scatter_begin(top), rest, fill)

    def natural(self, pieces):
        by_distance = [None] * self.T
        for d, piece in zip(self.order(), pieces):
            by_distance[d] = joined(piece)
        return self.picked(by_distance, [self.i ^ m for m in range(self.T)])

    def picked(self, parts, indices):
        stacked = jnp.stack(parts)
        return [lax.dynamic_index_in_dim(stacked, index, 0, keepdims=False) for index in indices]

    def col_swap(self, value, d):
        if d == 0:
            return value
        return lax.ppermute(value, "col", [(c, c ^ d) for c in range(self.C)])

    def plane_swap(self, value, d):
        return self.swap(value, d) if d else value

    def tokens_in(self, block, mid=None):
        rows, width = block.shape
        parts = block.reshape(self.T, rows // self.T, width)
        sent = [lax.dynamic_index_in_dim(parts, self.i ^ d, 0, keepdims=False) for d in range(self.T)]
        got = [self.plane_swap(sent[d], d) for d in range(self.T)]
        got = got if mid is None else tied(got, mid)
        sent = self.picked(got, [self.i ^ self.z ^ e for e in range(self.C)])
        return joined([self.col_swap(sent[e], e) for e in range(self.C)])

    def tokens_out_begin(self, block):
        small = block.shape[0] // self.C
        return [self.col_swap(block[e * small : (e + 1) * small], e) for e in range(self.C)]

    def tokens_out_end(self, got):
        sent = self.picked(got, [self.i ^ self.z ^ d for d in range(self.T)])
        got = [self.plane_swap(sent[d], d) for d in range(self.T)]
        return joined(self.picked(got, [self.i ^ m for m in range(self.T)]))

    def tokens_out(self, block):
        return self.tokens_out_end(self.tokens_out_begin(block))

    def total(self, value):
        for d in range(self.R.bit_length() - 1):
            value = value + lax.ppermute(value, "row", [(r, r ^ (1 << d)) for r in range(self.R)])
        for d in range(self.C.bit_length() - 1):
            value = value + lax.ppermute(value, "col", [(c, c ^ (1 << d)) for c in range(self.C)])
        return value


def gelu_parts(u):
    cdf = 0.5 * (1.0 + lax.erf(u * (0.5**0.5)))
    pdf = jnp.exp(-0.5 * u * u) * (0.5 / jnp.pi) ** 0.5
    return u * cdf, cdf + u * pdf


def norm_forward(residual, gain, shift):
    row_mean = jnp.mean(residual, axis=1, keepdims=True)
    centered = residual - row_mean
    variance = jnp.mean(centered * centered, axis=1, keepdims=True)
    inv_std = lax.rsqrt(variance + EPS)
    normed = centered * inv_std
    return (normed, inv_std, (normed * gain + shift).astype(BF))


def norm_backward(grad_out, normed, inv_std, gain):
    scaled = grad_out * gain
    row_mean = jnp.mean(scaled, axis=1, keepdims=True)
    row_along = jnp.mean(scaled * normed, axis=1, keepdims=True)
    grad_in = inv_std * (scaled - row_mean - normed * row_along)
    return (grad_in, jnp.sum(grad_out * normed, axis=0), jnp.sum(grad_out, axis=0))


def to_clip(grid, at_ref, source, target):
    rows = CLIP_LEN // grid.T
    small = rows // grid.C
    for n, d in enumerate(grid.order()):
        for e in range(grid.C):
            start = pl.multiple_of((at_ref[0] ^ d) * small + (at_ref[1] ^ e) * rows, small)
            low = n * rows + e * small
            target[pl.ds(start, small), :] = source[low : low + small, :]


def from_clip(grid, at_ref, block, k, target):
    rows = CLIP_LEN // grid.T
    small = rows // grid.C
    for n, d in enumerate(grid.order()):
        start = pl.multiple_of((at_ref[0] ^ d) * small, small)
        goal = pl.multiple_of(n * rows + (at_ref[1] ^ k) * small, small)
        target[pl.ds(goal, small), :] = block[pl.ds(start, small), :]


def causal_block(scores_t, size):
    keys = lax.broadcasted_iota(jnp.int32, (size, size), 0)
    asks = lax.broadcasted_iota(jnp.int32, (size, size), 1)
    last = scores_t.shape[0] - size
    edge = jnp.where(keys <= asks, scores_t[last:], NEG)
    return edge if last == 0 else jnp.concatenate([scores_t[:last], edge], axis=0)


def dot_nt(left, right):
    return lax.dot_general(left, right, (((1,), (1,)), ((), ())), preferred_element_type=F32)


def dot_nn(left, right):
    return lax.dot_general(left, right, (((1,), (0,)), ((), ())), preferred_element_type=F32)


def flip(value):
    return value.astype(F32).T


def self_forward_kernel(grid, width, at_ref, x_ref, out_ref, sums_ref, clip, block):
    size = CLIP_LEN // grid.C
    to_clip(grid, at_ref, x_ref, clip)
    heads = range(width // HEAD)

    def lanes(which, h):
        return slice(which * width + h * HEAD, which * width + (h + 1) * HEAD)

    keys = [clip[:, lanes(1, h)] for h in heads]
    values_t = [flip(clip[:, lanes(2, h)]).astype(BF) for h in heads]
    for k in range(grid.C):
        low, high = k * size, (k + 1) * size
        outs = []
        for h in heads:
            asks = clip[low:high, lanes(0, h)] * BF(SCALE)
            scores = causal_block(dot_nt(keys[h][:high], asks), size)
            top = jnp.max(scores, axis=0, keepdims=True)
            weight = jnp.exp(scores - top)
            total = jnp.sum(weight, axis=0, keepdims=True)
            outs.append(dot_nn(values_t[h][:, :high], weight.astype(BF)) / total)
            sums_ref[h : h + 1, low:high] = top + jnp.log(total)
        both = outs[0] if len(outs) == 1 else jnp.concatenate(outs, axis=0)
        block[...] = both.T.astype(BF)
        from_clip(grid, at_ref, block, k, out_ref)


def self_backward_kernel(grid, width, at_ref, x_ref, da_ref, sums_ref, out_ref, clip, da_clip, block, acc):
    size = CLIP_LEN // grid.C
    to_clip(grid, at_ref, x_ref, clip)
    to_clip(grid, at_ref, da_ref, da_clip)
    heads = range(width // HEAD)

    def lanes(which, h):
        return slice(which * width + h * HEAD, which * width + (h + 1) * HEAD)

    keys = [clip[:, lanes(1, h)] for h in heads]
    values = [clip[:, lanes(2, h)] for h in heads]
    keys_t = [flip(keys[h]).astype(BF) for h in heads]
    for k in reversed(range(grid.C)):
        low, high = k * size, (k + 1) * size
        dq = []
        for h in heads:
            asks = clip[low:high, lanes(0, h)] * BF(SCALE)
            da = da_clip[low:high, lanes(0, h)]
            scores = causal_block(dot_nt(keys[h][:high], asks), size)
            probs = jnp.exp(scores - sums_ref[h : h + 1, low:high])
            d_probs = dot_nt(values[h][:high], da)
            inner = jnp.sum(probs * d_probs, axis=0, keepdims=True)
            d_scores = (probs * (d_probs - inner)).astype(BF)
            dk = dot_nn(d_scores, asks)
            dv = dot_nn(probs.astype(BF), da)
            if k == grid.C - 1:
                acc[:, lanes(0, h)] = dk
                acc[:, lanes(1, h)] = dv
            else:
                acc[:high, lanes(0, h)] += dk
                acc[:high, lanes(1, h)] += dv
            dq.append(dot_nn(keys_t[h][:, :high], d_scores) * SCALE)
        both = dq[0] if len(dq) == 1 else jnp.concatenate(dq, axis=0)
        block[:, :width] = both.T.astype(BF)
        block[:, width:] = acc[low:high, :].astype(BF)
        from_clip(grid, at_ref, block, k, out_ref)


def unit_spec(rows, lanes):
    return pl.BlockSpec((None, rows, lanes), lambda n, *at: (n, 0, 0))


def self_attention(grid, x):
    units, _, width = x.shape
    width //= 3
    size = CLIP_LEN // grid.C
    return pl.pallas_call(
        functools.partial(self_forward_kernel, grid, width),
        grid_spec=pltpu.PrefetchScalarGridSpec(
            num_scalar_prefetch=1,
            grid=(units,),
            in_specs=[unit_spec(CLIP_LEN, 3 * width)],
            out_specs=[unit_spec(CLIP_LEN, width), unit_spec(8, CLIP_LEN)],
            scratch_shapes=[pltpu.VMEM((CLIP_LEN, 3 * width), BF), pltpu.VMEM((size, width), BF)],
        ),
        out_shape=[
            jax.ShapeDtypeStruct((units, CLIP_LEN, width), BF),
            jax.ShapeDtypeStruct((units, 8, CLIP_LEN), F32),
        ],
        compiler_params=pltpu.CompilerParams(vmem_limit_bytes=VMEM_LIMIT),
        cost_estimate=pl.CostEstimate(
            flops=COST * units * width, bytes_accessed=CLIP_LEN * units * width * 8, transcendentals=0
        ),
        name="self_attention",
    )(jnp.stack([grid.i, grid.z]), x)


def self_attention_grad(grid, x, da, sums):
    units, _, width = da.shape
    size = CLIP_LEN // grid.C
    return pl.pallas_call(
        functools.partial(self_backward_kernel, grid, width),
        grid_spec=pltpu.PrefetchScalarGridSpec(
            num_scalar_prefetch=1,
            grid=(units,),
            in_specs=[unit_spec(CLIP_LEN, 3 * width), unit_spec(CLIP_LEN, width), unit_spec(8, CLIP_LEN)],
            out_specs=unit_spec(CLIP_LEN, 3 * width),
            scratch_shapes=[
                pltpu.VMEM((CLIP_LEN, 3 * width), BF),
                pltpu.VMEM((CLIP_LEN, width), BF),
                pltpu.VMEM((size, 3 * width), BF),
                pltpu.VMEM((CLIP_LEN, 2 * width), F32),
            ],
        ),
        out_shape=jax.ShapeDtypeStruct((units, CLIP_LEN, 3 * width), BF),
        compiler_params=pltpu.CompilerParams(vmem_limit_bytes=VMEM_LIMIT),
        cost_estimate=pl.CostEstimate(
            flops=3 * COST * units * width, bytes_accessed=CLIP_LEN * units * width * 16, transcendentals=0
        ),
        name="self_attention_grad",
    )(jnp.stack([grid.i, grid.z]), x, da, sums)


def reorder_kernel(spans, core_ref, x_ref, out_ref):
    for core in range(2):

        @pl.when(core_ref[0] == core)
        def _(core=core):
            out_ref[...] = jnp.concatenate([x_ref[:, low : low + size] for low, size in spans[core]], axis=1)


def reorder(grid, x, back):
    rows, width = x.shape
    size = width // grid.R
    half = width // 2
    if back:
        spans = [[((r % 2 != core) * half + r // 2 * size, size) for r in range(grid.R)] for core in range(2)]
    else:
        spans = [[((2 * i + (core + n) % 2) * size, size) for n in range(2) for i in range(grid.T)] for core in range(2)]
    return pl.pallas_call(
        functools.partial(reorder_kernel, spans),
        grid_spec=pltpu.PrefetchScalarGridSpec(
            num_scalar_prefetch=1,
            grid=(1,),
            in_specs=[pl.BlockSpec((rows, width), lambda n, core: (0, 0))],
            out_specs=pl.BlockSpec((rows, width), lambda n, core: (0, 0)),
        ),
        out_shape=jax.ShapeDtypeStruct((rows, width), x.dtype),
        name="reorder",
    )(grid.core.reshape(1), x)


def own_first(grid, x):
    return reorder(grid, x, False)


def own_last(grid, x):
    return reorder(grid, x, True)


def lanes_of(ref, mats):
    parts = [ref[m] for m in mats]
    return parts[0] if len(parts) == 1 else jnp.concatenate(parts, axis=1)


def columns_kernel(mats, count, kind, *refs):
    pieces, (own_ref, other_ref), rest = refs[:count], refs[count : count + 2], refs[count + 2 :]
    own, other = lanes_of(own_ref, mats), lanes_of(other_ref, mats)
    half = own.shape[0]
    low = 0
    for piece in pieces:
        high = low + piece.shape[0]
        out = dot_nn(piece[:, :half], own) + dot_nn(piece[:, half:], other)
        if kind == "gelu":
            value, slope = gelu_parts(out)
            rest[0][low:high] = value.astype(BF)
            rest[1][low:high] = slope.astype(BF)
        elif kind == "slope":
            rest[1][low:high] = (out * rest[0][low:high].astype(F32)).astype(BF)
        else:
            rest[0][low:high] = out.astype(BF)
        low = high


def whole(array):
    return pl.BlockSpec(array.shape, lambda n: (0,) * array.ndim)


def act_spec(rows, lanes):
    return pl.BlockSpec((None, rows, lanes), lambda n: (n, 0, 0))


def columns_product(pieces, weights, mats, kind="plain", slope=None):
    own, other = weights
    blocks, _, half, wide = own.shape
    lanes = len(mats) * wide
    rows = sum(p.shape[0] for p in pieces)
    extra = [] if slope is None else [slope]
    outs = 2 if kind == "gelu" else 1
    shape = jax.ShapeDtypeStruct((blocks, rows, lanes), BF)
    first, picked = (mats[0], 1) if len(mats) == 1 else (0, own.shape[1])
    spec = pl.BlockSpec((None, picked) + own.shape[2:], lambda n: (n, first, 0, 0))
    result = pl.pallas_call(
        functools.partial(columns_kernel, (0,) if len(mats) == 1 else mats, len(pieces), kind),
        grid=(blocks,),
        in_specs=[whole(p) for p in pieces] + [spec, spec] + [act_spec(rows, lanes)] * len(extra),
        out_specs=[act_spec(rows, lanes)] * outs,
        out_shape=[shape] * outs,
        compiler_params=pltpu.CompilerParams(vmem_limit_bytes=VMEM_LIMIT),
        cost_estimate=pl.CostEstimate(flops=4 * half * rows * lanes * blocks, bytes_accessed=4 * half * lanes * blocks, transcendentals=0),
        name="columns_" + kind,
    )(*pieces, own, other, *extra)
    return result if outs > 1 else result[0]


def rows_kernel(mats, low, high, act_ref, own_ref, other_ref, *outs):
    blocks = act_ref.shape[0]
    acts = [act_ref[n, low:high] for n in range(blocks)]
    half = own_ref.shape[2]
    for cols, ref in ((slice(0, half), own_ref), (slice(half, 2 * half), other_ref)):
        parts = [lanes_of(ref.at[n], mats) for n in range(blocks)]
        if parts[0].shape[1] < 256:
            total = dot_nt(jnp.concatenate(acts, axis=1), jnp.concatenate(parts, axis=1))
        else:
            total = dot_nt(acts[0], parts[0])
            for act, part in zip(acts[1:], parts[1:]):
                total = total + dot_nt(act, part)
        at = 0
        for out in outs:
            out[:, cols] = total[at : at + out.shape[0]].astype(out.dtype)
            at += out.shape[0]


def rows_product(act, weights, mats, low, high, shapes):
    own, other = weights
    blocks, _, half, _ = own.shape
    lanes = act.shape[2]
    first, count = (mats[0], 1) if len(mats) == 1 else (0, own.shape[1])
    spec = pl.BlockSpec((blocks, count) + own.shape[2:], lambda n: (0, first, 0, 0))
    return pl.pallas_call(
        functools.partial(rows_kernel, (0,) if len(mats) == 1 else mats, low, high),
        grid=(1,),
        in_specs=[whole(act), spec, spec],
        out_specs=[whole(s) for s in shapes],
        out_shape=shapes,
        compiler_params=pltpu.CompilerParams(vmem_limit_bytes=VMEM_LIMIT),
        cost_estimate=pl.CostEstimate(
            flops=4 * half * (high - low) * lanes * blocks, bytes_accessed=4 * half * lanes * blocks, transcendentals=0
        ),
        name="rows",
    )(act, own, other)


def rows_top(grid, act, weights, mats):
    rows = act.shape[1] // grid.T
    shapes = [jax.ShapeDtypeStruct((rows // 2, 2 * weights[0].shape[2]), BF)] * 2
    return list(rows_product(act, weights, mats, rows * (grid.T - 1), rows * grid.T, shapes))


def rows_rest(grid, act, weights, mats):
    rows = act.shape[1] // grid.T
    shapes = [jax.ShapeDtypeStruct((rows, 2 * weights[0].shape[2]), F32)] * (grid.T - 1)
    return list(rows_product(act, weights, mats, 0, rows * (grid.T - 1), shapes))


def rows_terms(grid, act, weights, mats):
    top = rows_top(grid, act, weights, mats)
    return top, rows_rest(grid, after(act, top), weights, mats)


def grads_kernel(count, *refs):
    pieces, y_ref, keep_ref, send_ref, turned = refs[:count], refs[count], refs[count + 1], refs[count + 2], refs[count + 3]
    half = keep_ref.shape[0]

    @pl.when(pl.program_id(0) == 0)
    def _():
        low = 0
        for piece in pieces:
            high = low + piece.shape[0]
            turned[:, low:high] = piece[...].T
            low = high

    y = y_ref[...]
    keep_ref[...] = dot_nn(turned[:half], y).astype(BF)
    send_ref[...] = dot_nn(turned[half:], y).astype(BF)


def weight_grads(pieces, y):
    blocks, rows, lanes = y.shape
    width = pieces[0].shape[1]
    half = width // 2
    shape = jax.ShapeDtypeStruct((blocks, half, lanes), BF)
    return pl.pallas_call(
        functools.partial(grads_kernel, len(pieces)),
        grid=(blocks,),
        in_specs=[whole(p) for p in pieces] + [act_spec(rows, lanes)],
        out_specs=[act_spec(half, lanes)] * 2,
        out_shape=[shape] * 2,
        scratch_shapes=[pltpu.VMEM((width, rows), BF)],
        compiler_params=pltpu.CompilerParams(vmem_limit_bytes=VMEM_LIMIT),
        cost_estimate=pl.CostEstimate(flops=4 * half * rows * lanes * blocks, bytes_accessed=4 * half * lanes * blocks, transcendentals=0),
        name="weight_grads",
    )(*pieces, y)


def cross_scores(keys, asks):
    scores = dot_nt(keys, asks)
    top = jnp.max(scores, axis=0, keepdims=True)
    weight = jnp.exp(scores - top)
    return weight / jnp.sum(weight, axis=0, keepdims=True)


def cross_forward_kernel(q_ref, k_ref, v_ref, out_ref):
    for low in range(0, q_ref.shape[1], 2 * HEAD):
        pair = []
        for at in (slice(low, low + HEAD), slice(low + HEAD, low + 2 * HEAD)):
            probs = cross_scores(k_ref[:, at], q_ref[:, at] * BF(SCALE)).astype(BF)
            pair.append(dot_nn(flip(v_ref[:, at]).astype(BF), probs))
        out_ref[:, low : low + 2 * HEAD] = jnp.concatenate(pair, axis=0).T.astype(BF)


def cross_backward_kernel(q_ref, k_ref, v_ref, dc_ref, dq_ref, dk_ref, dv_ref):
    for low in range(0, q_ref.shape[1], 2 * HEAD):
        pair, dk, dv = [], [], []
        for at in (slice(low, low + HEAD), slice(low + HEAD, low + 2 * HEAD)):
            asks = q_ref[:, at] * BF(SCALE)
            probs = cross_scores(k_ref[:, at], asks)
            d_probs = dot_nt(v_ref[:, at], dc_ref[:, at])
            inner = jnp.sum(probs * d_probs, axis=0, keepdims=True)
            d_scores = (probs * (d_probs - inner)).astype(BF)
            dk.append(dot_nn(d_scores, asks))
            dv.append(dot_nn(probs.astype(BF), dc_ref[:, at]))
            pair.append(dot_nn(flip(k_ref[:, at]).astype(BF), d_scores) * SCALE)
        at = slice(low, low + 2 * HEAD)
        dq_ref[:, at] = jnp.concatenate(pair, axis=0).T.astype(BF)
        dk_ref[:, at] = jnp.concatenate(dk, axis=1)
        dv_ref[:, at] = jnp.concatenate(dv, axis=1)


def cross_call(kernel, name, arrays, outs):
    width = arrays[0].shape[1]
    lanes = 512 if width % 512 == 0 else width

    def spec(rows):
        return pl.BlockSpec((rows, lanes), lambda n: (0, n))

    return pl.pallas_call(
        kernel,
        grid=(width // lanes,),
        in_specs=[spec(a.shape[0]) for a in arrays],
        out_specs=[spec(rows) for rows, _ in outs],
        out_shape=[jax.ShapeDtypeStruct((rows, width), kind) for rows, kind in outs],
        compiler_params=pltpu.CompilerParams(vmem_limit_bytes=VMEM_LIMIT),
        cost_estimate=pl.CostEstimate(
            flops=arrays[0].shape[0] * arrays[1].shape[0] * width * 20, bytes_accessed=2**22, transcendentals=0
        ),
        name=name,
    )(*arrays)


def cross_attention(queries, keys, values):
    return cross_call(cross_forward_kernel, "cross_attention", [queries, keys, values], [(queries.shape[0], BF)])[0]


def cross_attention_grad(queries, keys, values, grad_out):
    outs = [(queries.shape[0], BF), (keys.shape[0], F32), (keys.shape[0], F32)]
    return cross_call(cross_backward_kernel, "cross_attention_grad", [queries, keys, values, grad_out], outs)


def head_units(grid, width):
    heads = width // HEAD
    per_unit = -(-heads // grid.T)
    assert heads % per_unit == 0
    return heads // per_unit, per_unit * HEAD


def self_slots(grid, mats):
    units, wide = head_units(grid, mats[0].shape[1])
    both = jnp.stack(mats)
    lows = [jnp.minimum((s - grid.z - 1) % grid.T, units - 1) * wide for s in range(grid.T)]
    return jnp.stack([lax.dynamic_slice_in_dim(both, low, wide, axis=2) for low in lows])


def by_matrix(moved):
    sources, count, rows, wide = moved.shape
    return moved.transpose(1, 0, 2, 3).reshape(count, sources * rows, wide)


def self_weights(grid, slots, units):
    half = jnp.stack(
        [lax.dynamic_index_in_dim(slots, (grid.i - 1 - m) % grid.T, 0, keepdims=False) for m in range(units)]
    )
    return half, grid.core_swap(half)


def core_sum(grid, keep, send, mid):
    got = tied(grid.core_swap(send), mid)
    return (keep.astype(F32) + got.astype(F32)).astype(BF)


def self_grad_slots(grid, pairs, mid):
    half = jnp.concatenate([core_sum(grid, *pair, mid) for pair in pairs], axis=2)
    half = jnp.concatenate([half, jnp.zeros((grid.C - half.shape[0],) + half.shape[1:], BF)], axis=0)
    return jnp.stack(
        [lax.dynamic_index_in_dim(half, (grid.i - c - 1) % grid.T, 0, keepdims=False) for c in range(grid.C)]
    )


def self_grad_blocks(grid, moved, units):
    wide = moved.shape[2] // 4
    mine = [lax.dynamic_index_in_dim(moved, (grid.z + 1 + m) % grid.T, 0, keepdims=False) for m in range(units)]
    return [
        jnp.concatenate([part[:, n * wide : (n + 1) * wide] for part in mine], axis=1).astype(F32) for n in range(4)
    ]


def hidden_slots(grid, mats):
    rows, width = mats[0].shape
    count = len(mats)
    return jnp.stack(mats).reshape(count, rows, grid.T, width // grid.T).transpose(2, 0, 1, 3)


def hidden_gathered(moved, n, token):
    sources, _, rows, wide = moved.shape
    return lax.all_gather(after(moved[:, n].reshape(1, sources * rows, wide), token), "col", axis=0)


def with_other(grid, own):
    return own, grid.core_swap(own)


def hidden_grad_slots(grid, pairs, mid):
    return jnp.concatenate([core_sum(grid, *pair, mid) for pair in pairs], axis=2)


def col_sum(slots):
    return lax.psum_scatter(slots, "col", scatter_dimension=0)


def hidden_grad_blocks(grid, moved, count):
    rows, wide = moved.shape[1], moved.shape[2] // count
    return [
        moved[:, :, n * wide : (n + 1) * wide].transpose(1, 0, 2).reshape(rows, -1).astype(F32) for n in range(count)
    ]


def cross_columns(grid, blocks):
    _, count, rows, width = blocks.shape
    return blocks.transpose(1, 2, 0, 3).reshape(count * rows, grid.C * width)


def cross_weights(grid, pieces, count):
    half = jnp.stack(grid.natural(pieces))
    width = half.shape[2]
    half = half.reshape(grid.T, count, -1, width).transpose(1, 0, 2, 3).reshape(count, -1, width)
    other = grid.core_swap(half)
    return [joined([half[n], other[n]]) for n in range(count)]


def cross_core_sum(grid, lows, mid):
    edge = lows[0].shape[0] // 2
    return [core_sum(grid, low[:edge], low[edge:], mid) for low in lows]


def cross_terms(grid, halves, rows, width):
    halves = [half.reshape(grid.T, rows, grid.C * width) for half in halves]

    def term(d):
        return joined([lax.dynamic_index_in_dim(half, grid.i ^ d, 0, keepdims=False) for half in halves])

    order = grid.order()
    top = term(order[-1])
    size = top.shape[0] // 2
    return [top[:size], top[size:]], [term(d).astype(F32) for d in order[:-1]]


def cross_blocks(grid, own, rows, width):
    return own.astype(BF).reshape(-1, rows, grid.C, width).transpose(2, 0, 1, 3)


def text_columns(grid, text):
    _, own, width = text.shape
    parts = text.reshape(own, grid.R, width // grid.R).transpose(1, 0, 2)
    parts = grid.row_a2a(parts)
    pieces = [parts] + [
        lax.ppermute(parts, "col", [(c, c ^ d) for c in range(grid.C)]) for d in range(1, grid.C)
    ]
    stacked = jnp.stack(pieces)
    order = [lax.dynamic_index_in_dim(stacked, grid.z ^ c, 0, keepdims=False) for c in range(grid.C)]
    return jnp.stack(order, axis=1).reshape(-1, width // grid.R)


def text_parts(grid, columns, mats):
    count, rows, width = mats.shape
    own = columns.shape[0] // (grid.R * grid.C)
    part = product(columns, mats.transpose(1, 0, 2).reshape(rows, count * width)).astype(BF)
    part = part.reshape(grid.T, 2, grid.C, own, count * width).transpose(2, 1, 0, 3, 4)
    return grid.row_a2a(part.reshape(grid.R, grid.T * own, count * width))


def text_shared(grid, moved):
    own = moved.shape[1] // grid.T
    summed = jnp.sum(moved.astype(F32), axis=0).astype(BF).reshape(grid.T, own, moved.shape[2])
    sent = grid.picked(list(summed), [grid.z ^ e for e in range(grid.C)])
    return [grid.col_swap(sent[e], e) for e in range(grid.C)]


def text_states_of(grid, got, count):
    own, width = got[0].shape[0], got[0].shape[1] // count
    blocks = jnp.stack(grid.picked(got, [grid.z ^ c for c in range(grid.C)]))
    mine = blocks.reshape(grid.C, own, count, width).transpose(1, 2, 0, 3)
    mine = mine.reshape(own, count * grid.C * width)
    full = joined(flat(grid.gather(mine)))
    return full.reshape(-1, count, grid.C * width)


def text_begin(grid, grads):
    own = grads.shape[0] // grid.T
    pieces = grads.reshape(grid.T, own, -1)
    top = pieces[grid.T - 1].astype(BF)
    return grid.scatter_begin([top[: own // 2], top[own // 2 :]]), [pieces[n] for n in range(grid.T - 1)]


def text_backward(grid, mine, width):
    own = mine.shape[0]
    mine = mine.reshape(own, -1, grid.C, width).transpose(2, 0, 1, 3)
    moved = grid.col_a2a(mine)
    other = grid.core_swap(moved)
    pair = jnp.stack(
        [jnp.where(grid.core == 0, moved, other), jnp.where(grid.core == 0, other, moved)], axis=1
    )
    shape = pair.shape
    flat = pair.reshape(shape[0] * 2, -1)
    full = jnp.stack(grid.natural(grid.gather(flat)), axis=1)
    return full.reshape(-1, shape[3], width)


def text_out(grid, part):
    own = part.shape[0] // (grid.R * grid.C)
    cols = part.shape[1]
    parts = part.astype(BF).reshape(grid.R, grid.C, own, cols).transpose(1, 0, 2, 3)
    moved = grid.col_a2a(parts).astype(F32)
    summed = jnp.sum(moved, axis=0).astype(BF)
    moved = grid.row_a2a(summed)
    return moved.transpose(1, 0, 2).reshape(1, own, grid.R * cols).astype(F32)


def shards(
    grid,
    inputs,
    text_states,
    cotangent,
    norm_gains,
    norm_shifts,
    self_query,
    self_key,
    self_value,
    self_out,
    cross_query,
    cross_key,
    cross_value,
    cross_out,
    mlp_up,
    mlp_down,
):
    grid.at()
    last = LAYERS - 1
    rows, width = self_query.shape[1:]
    units, _ = head_units(grid, width)

    self_parts = [self_slots(grid, [w[n] for w in (self_query, self_key, self_value, self_out)]) for n in range(LAYERS)]
    hidden_parts = [hidden_slots(grid, [mlp_up[n], mlp_down[n]]) for n in range(LAYERS)]
    self_moved = [None] * LAYERS
    hidden_moved = [None] * LAYERS
    self_full = [None] * LAYERS
    self_moved[0] = grid.plane_a2a(self_parts[0])
    sent = by_matrix(self_moved[0])
    cross_parts = [jnp.stack([cross_query[n], cross_out[n]]) for n in range(LAYERS)]
    tokens = grid.tokens_in(jnp.concatenate([inputs, cotangent.astype(BF)], axis=1))
    tokens, sent = meet(tokens, sent)
    text_cols = text_columns(grid, after(text_states, tokens))
    gradient = tokens[:, inputs.shape[1] :]
    tokens = tokens[:, : inputs.shape[1]]
    self_full[0] = lax.all_gather(sent, "col", axis=0)
    residual = own_first(grid, tokens).astype(F32)
    norm_rows = after(jnp.concatenate([norm_gains, norm_shifts], axis=1), tokens)
    norm_rows = own_first(grid, norm_rows.reshape(-1, norm_rows.shape[2])).reshape(norm_rows.shape)
    gains, shifts = norm_rows[:, :3], norm_rows[:, 3:]
    text_mats = jnp.stack([mat for n in range(LAYERS) for mat in (cross_key[n], cross_value[n])])

    kept = [dict() for _ in range(LAYERS)]
    w_self = [None] * LAYERS
    w_cross = [None] * LAYERS
    w_hidden = [None] * LAYERS
    for n in range(LAYERS):
        k = kept[n]
        k["normed_one"], k["inv_one"], low_one = norm_forward(residual, gains[n, 0], shifts[n, 0])
        near_one = grid.gather_begin(low_one)
        if n == 0:
            hidden_moved[0] = grid.plane_a2a(after(hidden_parts[0], near_one))
            text_moved = text_parts(grid, after(text_cols, near_one), text_mats)
        full_one = flat(grid.gather_end(near_one))
        if n == 0:
            (self_full[0], full_one), (text_sent, hidden_moved[0]) = meet(
                (self_full[0], full_one), (text_shared(grid, text_moved), hidden_moved[0])
            )
            cross_full = lax.all_gather(after(cross_parts[0], sent), "col", axis=0)
        else:
            self_full[n] = after(self_full[n], residual)
        k["full_one"] = full_one
        w_self[n] = self_weights(grid, self_full[n], units)
        k["qkv"] = columns_product(full_one, w_self[n], (0, 1, 2))
        k["attn_low"], k["sums_self"] = self_attention(grid, k["qkv"])
        if n > 0:
            next_near = grid.gather_begin(cross_columns(grid, after(cross_full, full_one)))
            k["attn_low"], next_near = meet(k["attn_low"], next_near)
            w_cross[n] = cross_weights(grid, grid.gather_end(next_near), 2)
        up_full = hidden_gathered(hidden_moved[n], 0, full_one if n == 0 else hidden_moved[n])
        down_full = hidden_gathered(hidden_moved[n], 1, k["qkv"])
        top, rest = rows_terms(grid, k["attn_low"], w_self[n], (3,))
        fill = []
        if n == 0:
            next_near = grid.gather_begin(cross_columns(grid, after(cross_full, k["qkv"])))
            rest, next_near = meet(rest, next_near)
            w_cross[0] = cross_weights(grid, grid.gather_end(next_near), 2)
        if n == 0:
            text_all = text_states_of(grid, tied(text_sent, top), 2 * LAYERS)
        added, _ = grid.scatter(top, rest)
        residual = residual + added
        w_up = with_other(grid, after(up_full, residual))
        before_cross = residual
        k["text"] = [text_all[:, 2 * n + side] for side in range(2)]
        k["normed_two"], k["inv_two"], k["low_two"] = norm_forward(residual, gains[n, 1], shifts[n, 1])
        k["cross_queries"] = product(k["low_two"], w_cross[n][0]).astype(BF)
        k["cross_low"] = cross_attention(k["cross_queries"], *k["text"])
        residual = residual + product_nt(k["cross_low"], w_cross[n][1])
        k["normed_three"], k["inv_three"], low_three = norm_forward(residual, gains[n, 2], shifts[n, 2])
        if n < last:
            w_down = with_other(grid, after(down_full, before_cross))
            w_down, low_three = meet(w_down, low_three)
            sent = by_matrix(grid.plane_a2a(after(self_parts[n + 1], before_cross)))
            low_three, sent = meet(low_three, sent)
            self_full[n + 1] = lax.all_gather(sent, "col", axis=0)
            cross_full = lax.all_gather(after(cross_parts[n + 1], sent), "col", axis=0)
        if n == last:
            low_three, next_near = meet(low_three, grid.gather_begin(after(gradient, before_cross)))
        k["full_three"] = flat(grid.gather(low_three))
        if n < last:
            hidden_moved[n + 1] = grid.plane_a2a(after(hidden_parts[n + 1], low_three))
            k["full_three"], hidden_moved[n + 1] = meet(k["full_three"], hidden_moved[n + 1])
        k["hidden_low"], k["hidden_slope"] = columns_product(k["full_three"], w_up, (0,), "gelu")
        if n == last:
            w_down = with_other(grid, after(down_full, k["hidden_low"]))
        w_hidden[n] = (w_up, w_down)
        if n < last:
            top, rest = rows_terms(grid, k["hidden_low"], w_hidden[n][1], (0,))
            gradient = own_first(grid, after(gradient, rest)) if n == 0 else gradient
            added, gradient = grid.scatter(top, rest, gradient)
            residual = residual + added
        else:
            dy_three = flat(grid.gather_end(next_near))
            gradient = gradient.astype(F32)

    before_last = residual
    hidden_sums = [None] * LAYERS
    self_sums = [None] * LAYERS
    cross_sums = [None] * LAYERS
    text_grads = [None] * LAYERS
    norms = [None] * LAYERS
    fill = []
    for n in range(last, -1, -1):
        k = kept[n]
        w_up, w_down = w_hidden[n]
        if n < last:
            sent, slots = meet(gradient.astype(BF), self_slots_grad)
            self_sums[n + 1] = col_sum(slots)
            cross_terms_late = cross_terms(grid, cross_core_sum(grid, cross_lows, sent), rows, width)
            dy_three, cross_terms_late = meet(flat(grid.gather(sent)), cross_terms_late)
        if n == last:
            late_top, late_rest = rows_terms(grid, k["hidden_low"], w_down, (0,))
            late_state = grid.scatter_begin(late_top)
            dy_three, late_rest = meet(dy_three, late_rest)
        d_pre = columns_product(dy_three, w_down, (0,), "slope", k["hidden_slope"])
        top, rest = rows_terms(grid, d_pre, w_up, (0,))
        state = grid.scatter_begin(top)
        if n < last:
            (state, rest), cross_state = meet((state, rest), grid.scatter_begin(cross_terms_late[0]))
        hidden_pairs = [
            weight_grads(after(k["full_three"], state), d_pre),
            weight_grads(after(dy_three, state), k["hidden_low"]),
        ]
        if n == last:
            late_state = tied(late_state, rest)
        grad_normed, hidden_pairs = grid.scatter_end(state, rest, hidden_pairs)
        grad_res, gain_three, shift_three = norm_backward(grad_normed, k["normed_three"], k["inv_three"], gains[n, 2])
        gradient = gradient + grad_res
        if n < last:
            gradient, hidden_sums[n + 1] = meet(gradient, hidden_sums[n + 1])
        before_cross = gradient
        if n == last:
            late_sum, _ = grid.scatter_end(tied(late_state, gradient), late_rest)
        dy_two = gradient.astype(BF)
        d_cross = product(dy_two, w_cross[n][1]).astype(BF)
        d_cquery, d_ckey, d_cvalue = cross_attention_grad(k["cross_queries"], *k["text"], d_cross)
        grad_normed = product_nt(d_cquery, w_cross[n][0])
        text_grads[n] = jnp.concatenate([d_ckey, d_cvalue], axis=1)
        grad_res, gain_two, shift_two = norm_backward(grad_normed, k["normed_two"], k["inv_two"], gains[n, 1])
        gradient = gradient + grad_res
        sent = gradient.astype(BF)
        if n == last:
            sent, late_sum = meet(sent, late_sum)
            fill = own_last(grid, (before_last + late_sum).astype(BF))
        else:
            sent, hidden_slots_grad = meet(sent, hidden_grad_slots(grid, hidden_pairs, grad_normed))
            hidden_sums[n] = col_sum(hidden_slots_grad)
            fill = ()
        dy_one, fill = meet(flat(grid.gather(sent)), fill)
        if n == last:
            output = grid.tokens_out_begin(fill)
        d_attn = columns_product(dy_one, w_self[n], (3,))
        d_qkv = self_attention_grad(grid, k["qkv"], d_attn, k["sums_self"])
        if n == 0:
            text_state, text_rest = text_begin(grid, after(jnp.concatenate(text_grads, axis=1), dy_one))
            d_qkv, (text_state, self_sums[1:]) = meet(d_qkv, (text_state, self_sums[1:]))
        if n == last:
            d_qkv, output = meet(d_qkv, output)
            output = grid.tokens_out_end(output)

        def cross_products(token):
            return [
                product_tn(after(k["low_two"], token), d_cquery).astype(BF),
                product_tn(after(dy_two, token), k["cross_low"]).astype(BF),
            ]

        if n > 0:
            top, rest = rows_terms(grid, d_qkv, w_self[n], (0, 1, 2))
            state = grid.scatter_begin(top)
            qkv_pair = weight_grads(after(k["full_one"], state), d_qkv)
            out_pair = weight_grads(after(dy_one, state), k["attn_low"])
            fill = [qkv_pair, out_pair, output, hidden_grad_slots(grid, hidden_pairs, state)]
        else:
            qkv_pair = weight_grads(k["full_one"], d_qkv)
            out_pair = weight_grads(dy_one, after(k["attn_low"], d_qkv))
            text_mine = grid.scatter_end(text_state, text_rest)[0].astype(BF)
            own, _ = grid.scatter_end(tied(cross_state, dy_one), cross_terms_late[1])
            out_pair, (text_mine, own) = meet(out_pair, (text_mine, cross_blocks(grid, own, rows, width)))
            cross_sums[n + 1] = own
            top = rows_top(grid, after(d_qkv, [qkv_pair, out_pair]), w_self[n], (0, 1, 2))
            state = grid.scatter_begin(top)
            top, slots = meet(top, self_grad_slots(grid, [qkv_pair, out_pair], out_pair))
            self_sums[0] = col_sum(slots)
            rest = rows_rest(grid, after(d_qkv, slots), w_self[n], (0, 1, 2))
            fill = cross_terms(grid, cross_core_sum(grid, cross_products(state), state), rows, width)
        grad_normed, fill = grid.scatter_end(state, rest, fill)
        if n == 0:
            cross_state, cross_last = grid.scatter_begin(fill[0]), fill[1]
        if n > 0:
            qkv_pair, out_pair, output, hidden_slots_grad = fill
            cross_lows = cross_products(grad_normed)
            hidden_sums[n] = col_sum(hidden_slots_grad)
            self_slots_grad = self_grad_slots(grid, [qkv_pair, out_pair], grad_normed)
        grad_res, gain_one, shift_one = norm_backward(grad_normed, k["normed_one"], k["inv_one"], gains[n, 0])
        gradient = gradient + grad_res
        norms[n] = jnp.stack([gain_one, gain_two, gain_three, shift_one, shift_two, shift_three])

    gradient, cross_state = meet(gradient.astype(BF), cross_state)
    input_grad = grid.tokens_out_begin(own_last(grid, gradient))
    text_full = text_backward(grid, after(text_mine, grad_normed), width)
    own, _ = grid.scatter_end(cross_state, cross_last)
    text_full, cross_sums[0] = meet(text_full, cross_blocks(grid, own, rows, width))
    cross_all, self_sums[0] = meet(jnp.concatenate(cross_sums, axis=1), self_sums[0])
    cross_all = col_sum(cross_all).astype(F32)
    cross_out_grads = [cross_all[2 * n : 2 * n + 2] for n in range(LAYERS)]
    text_weights = [[product_tn(text_cols, text_full[:, 2 * n + side]) for side in range(2)] for n in range(LAYERS)]
    text_part = 0.0
    for n in range(LAYERS):
        for side, mats in enumerate((cross_key, cross_value)):
            text_part = text_part + product_nt(text_full[:, 2 * n + side], mats[n])
    early = [hidden_sums[n] for n in range(1, LAYERS)] + [self_sums[n] for n in range(1, LAYERS)]
    widths = [value.shape[1] for value in early]
    moved = jnp.concatenate([value.reshape(grid.T, rows, value.shape[1]) for value in early], axis=2)
    moved = grid.plane_a2a(after(moved, grad_normed))
    input_grad, (moved, hidden_sums[0]) = meet(input_grad, (moved, hidden_sums[0]))
    input_grad = grid.tokens_out_end(input_grad).astype(F32)
    parts = [moved[:, :, sum(widths[:m]) : sum(widths[: m + 1])] for m in range(len(early))]
    first = [grid.plane_a2a(value[0].reshape(grid.T, rows, value[0].shape[1])) for value in (hidden_sums, self_sums)]
    text_part, first = meet(text_part, first)
    text_grad = text_out(grid, text_part)
    hidden_out = [hidden_grad_blocks(grid, part, 2) for part in [first[0]] + parts[: LAYERS - 1]]
    self_out_grads = [self_grad_blocks(grid, part, units) for part in [first[1]] + parts[LAYERS - 1 :]]
    totals = grid.total(own_last(grid, jnp.concatenate(norms, axis=0))).reshape(LAYERS, 6, -1)
    gains_sum, shifts_sum = totals[:, :3], totals[:, 3:]

    def both(values, slot):
        return jnp.stack([values[n][slot] for n in range(LAYERS)])

    return (
        output.astype(F32),
        input_grad,
        text_grad,
        gains_sum,
        shifts_sum[:, 1:],
        shifts_sum[:, 0],
        both(self_out_grads, 0),
        both(self_out_grads, 1),
        both(self_out_grads, 2),
        both(self_out_grads, 3),
        both(cross_out_grads, 0),
        both(text_weights, 0),
        both(text_weights, 1),
        both(cross_out_grads, 1),
        both(hidden_out, 0),
        both(hidden_out, 1),
    )


def solution(mesh):
    grid = Grid(mesh)
    tokens = P(("row", "col"), None)
    text = P("row", "col", None)
    block = P(None, "row", "col")
    in_specs = (tokens, text, tokens, P(), P()) + (block,) * 10
    out_specs = (tokens, tokens, text, P(), P(), P()) + (block,) * 10

    def run(*args):
        return shards(grid, *args)

    return jax.shard_map(run, mesh=mesh, in_specs=in_specs, out_specs=out_specs, check_vma=False)
```

```python
import functools

import jax
import jax.numpy as jnp
from jax import lax
from jax.experimental import pallas as pl
from jax.experimental.pallas import tpu as pltpu
from jax.sharding import PartitionSpec as P

HEAD = 64
CLIP_LEN = 1024
LAYERS = 2
SCALE = 0.125
EPS = 1e-05
NEG = -1e30
BF = jnp.bfloat16
F32 = jnp.float32
VMEM_LIMIT = 48 * 2**20
COST = CLIP_LEN * CLIP_LEN * 8


def product(left, right):
    return jnp.dot(left, right, preferred_element_type=F32)


def product_tn(left, right):
    return lax.dot_general(left, right, (((0,), (0,)), ((), ())), preferred_element_type=F32)


def product_nt(left, right):
    return lax.dot_general(left, right, (((1,), (1,)), ((), ())), preferred_element_type=F32)


def after(value, token):
    return lax.optimization_barrier((value, token))[0]


def tied(values, others):
    leaves, tree = jax.tree.flatten(values)
    arrays = [leaf for leaf in leaves if not isinstance(leaf, int)]
    others = [leaf for leaf in jax.tree.leaves(others) if not isinstance(leaf, int)]
    done = iter(lax.optimization_barrier((arrays, others))[0])
    return jax.tree.unflatten(tree, [leaf if isinstance(leaf, int) else next(done) for leaf in leaves])


def meet(values, fill):
    return tied((values, fill), [])


def joined(pieces):
    return pieces[0] if len(pieces) == 1 else jnp.concatenate(pieces, axis=0)


def flat(pieces):
    return [array for piece in pieces for array in piece]


class Grid:
    def __init__(self, mesh):
        self.R = mesh.shape["row"]
        self.C = mesh.shape["col"]
        self.T = self.R // 2
        assert self.T == self.C
        self.groups = [[2 * i + core for i in range(self.T)] for core in range(2)]

    def at(self):
        row = lax.axis_index("row")
        self.i = row // 2
        self.core = row % 2
        self.z = lax.axis_index("col")

    def swap(self, value, d):
        return lax.ppermute(value, "row", [(r, r ^ (2 * d)) for r in range(self.R)])

    def core_swap(self, value):
        return lax.ppermute(value, "row", [(r, r ^ 1) for r in range(self.R)])

    def plane_a2a(self, value):
        return lax.all_to_all(value, "row", 0, 0, tiled=True, axis_index_groups=self.groups)

    def row_a2a(self, value):
        return lax.all_to_all(value, "row", 0, 0, tiled=True)

    def col_a2a(self, value):
        return lax.all_to_all(value, "col", 0, 0, tiled=True)

    def distances(self):
        return sorted(range(1, self.T), key=lambda d: (bin(d).count("1"), d))

    def order(self):
        return [0] + self.distances()

    def gather_begin(self, own):
        return [own] + [self.swap(own, d) for d in self.distances() if d & (d - 1) == 0]

    def gather_end(self, near):
        half = near[0].shape[0] // 2
        pieces = {d: [piece] for d, piece in zip([0] + [d for d in self.distances() if d & (d - 1) == 0], near)}

        def part(d, upper):
            if len(pieces[d]) == 2:
                return pieces[d][upper]
            return pieces[d][0][half:] if upper else pieces[d][0][:half]

        for d in self.distances():
            high = 1 << (d.bit_length() - 1)
            low = d & -d
            if high != low:
                pieces[d] = [self.swap(part(d ^ high, 0), high), self.swap(part(d ^ low, 1), low)]
        return [pieces[d] for d in self.order()]

    def gather(self, own):
        return self.gather_end(self.gather_begin(own))

    def scatter_begin(self, top):
        d = self.order()[-1]
        high = 1 << (d.bit_length() - 1)
        low = d & -d
        return [(d ^ high, 0, self.swap(top[0], high)), (d ^ low, 1, self.swap(top[1], low))]

    def scatter_end(self, state, rest, fill=()):
        held = []
        order = self.order()
        state = list(state)
        for n in reversed(range(1, self.T - 1)):
            d = order[n]
            high = 1 << (d.bit_length() - 1)
            low = d & -d
            half = rest[n].shape[0] // 2
            parts = [rest[n][:half], rest[n][half:]]
            for goal, upper, value in state:
                if goal == d:
                    parts[upper] = parts[upper] + value.astype(F32)
            parts = [part.astype(BF) for part in parts]
            if high == low:
                held.append(self.swap(joined(parts), d))
            else:
                state += [(d ^ high, 0, self.swap(parts[0], high)), (d ^ low, 1, self.swap(parts[1], low))]
        total = rest[0]
        held, fill = meet(held, fill)
        for value in held:
            total = total + value.astype(F32)
        return total, fill

    def scatter(self, top, rest, fill=()):
        return self.scatter_end(self.scatter_begin(top), rest, fill)

    def natural(self, pieces):
        by_distance = [None] * self.T
        for d, piece in zip(self.order(), pieces):
            by_distance[d] = joined(piece)
        return self.picked(by_distance, [self.i ^ m for m in range(self.T)])

    def picked(self, parts, indices):
        stacked = jnp.stack(parts)
        return [lax.dynamic_index_in_dim(stacked, index, 0, keepdims=False) for index in indices]

    def col_swap(self, value, d):
        if d == 0:
            return value
        return lax.ppermute(value, "col", [(c, c ^ d) for c in range(self.C)])

    def plane_swap(self, value, d):
        return self.swap(value, d) if d else value

    def tokens_in(self, block, mid=None):
        rows, width = block.shape
        parts = block.reshape(self.T, rows // self.T, width)
        sent = [lax.dynamic_index_in_dim(parts, self.i ^ d, 0, keepdims=False) for d in range(self.T)]
        got = [self.plane_swap(sent[d], d) for d in range(self.T)]
        got = got if mid is None else tied(got, mid)
        sent = self.picked(got, [self.i ^ self.z ^ e for e in range(self.C)])
        return joined([self.col_swap(sent[e], e) for e in range(self.C)])

    def tokens_out_begin(self, block):
        small = block.shape[0] // self.C
        return [self.col_swap(block[e * small : (e + 1) * small], e) for e in range(self.C)]

    def tokens_out_end(self, got):
        sent = self.picked(got, [self.i ^ self.z ^ d for d in range(self.T)])
        got = [self.plane_swap(sent[d], d) for d in range(self.T)]
        return joined(self.picked(got, [self.i ^ m for m in range(self.T)]))

    def tokens_out(self, block):
        return self.tokens_out_end(self.tokens_out_begin(block))

    def total(self, value):
        for d in range(self.R.bit_length() - 1):
            value = value + lax.ppermute(value, "row", [(r, r ^ (1 << d)) for r in range(self.R)])
        for d in range(self.C.bit_length() - 1):
            value = value + lax.ppermute(value, "col", [(c, c ^ (1 << d)) for c in range(self.C)])
        return value


def gelu_parts(u):
    cdf = 0.5 * (1.0 + lax.erf(u * (0.5**0.5)))
    pdf = jnp.exp(-0.5 * u * u) * (0.5 / jnp.pi) ** 0.5
    return u * cdf, cdf + u * pdf


def norm_forward(residual, gain, shift):
    row_mean = jnp.mean(residual, axis=1, keepdims=True)
    centered = residual - row_mean
    variance = jnp.mean(centered * centered, axis=1, keepdims=True)
    inv_std = lax.rsqrt(variance + EPS)
    normed = centered * inv_std
    return (normed, inv_std, (normed * gain + shift).astype(BF))


def norm_backward(grad_out, normed, inv_std, gain):
    scaled = grad_out * gain
    row_mean = jnp.mean(scaled, axis=1, keepdims=True)
    row_along = jnp.mean(scaled * normed, axis=1, keepdims=True)
    grad_in = inv_std * (scaled - row_mean - normed * row_along)
    return (grad_in, jnp.sum(grad_out * normed, axis=0), jnp.sum(grad_out, axis=0))


def to_clip(grid, at_ref, source, target):
    rows = CLIP_LEN // grid.T
    small = rows // grid.C
    for n, d in enumerate(grid.order()):
        for e in range(grid.C):
            start = pl.multiple_of((at_ref[0] ^ d) * small + (at_ref[1] ^ e) * rows, small)
            low = n * rows + e * small
            target[pl.ds(start, small), :] = source[low : low + small, :]


def from_clip(grid, at_ref, block, k, target):
    rows = CLIP_LEN // grid.T
    small = rows // grid.C
    for n, d in enumerate(grid.order()):
        start = pl.multiple_of((at_ref[0] ^ d) * small, small)
        goal = pl.multiple_of(n * rows + (at_ref[1] ^ k) * small, small)
        target[pl.ds(goal, small), :] = block[pl.ds(start, small), :]


def causal_spans(low, high):
    return ([(0, low, False)] if low else []) + [(low, high, True)]


def causal_scores(keys, asks, masked):
    scores = dot_nt(keys, asks)
    if not masked:
        return scores
    key_ids = lax.broadcasted_iota(jnp.int32, scores.shape, 0)
    ask_ids = lax.broadcasted_iota(jnp.int32, scores.shape, 1)
    return jnp.where(key_ids <= ask_ids, scores, NEG)


def summed(terms):
    return functools.reduce(lambda left, right: left + right, terms)


def dot_nt(left, right):
    return lax.dot_general(left, right, (((1,), (1,)), ((), ())), preferred_element_type=F32)


def dot_nn(left, right):
    return lax.dot_general(left, right, (((1,), (0,)), ((), ())), preferred_element_type=F32)


def flip(value):
    return value.astype(F32).T


def self_forward_kernel(grid, width, at_ref, x_ref, out_ref, sums_ref, clip, block):
    size = CLIP_LEN // grid.C
    to_clip(grid, at_ref, x_ref, clip)
    heads = range(width // HEAD)

    def lanes(which, h):
        return slice(which * width + h * HEAD, which * width + (h + 1) * HEAD)

    keys = [clip[:, lanes(1, h)] for h in heads]
    values_t = [flip(clip[:, lanes(2, h)]).astype(BF) for h in heads]
    for k in range(grid.C):
        low, high = k * size, (k + 1) * size
        outs = []
        for h in heads:
            asks = clip[low:high, lanes(0, h)] * BF(SCALE)
            spans = causal_spans(low, high)
            scores = [causal_scores(keys[h][start:end], asks, masked) for start, end, masked in spans]
            top = functools.reduce(jnp.maximum, [jnp.max(part, axis=0, keepdims=True) for part in scores])
            weights = [jnp.exp(part - top) for part in scores]
            total = summed([jnp.sum(part, axis=0, keepdims=True) for part in weights])
            out = summed(
                [dot_nn(values_t[h][:, start:end], part.astype(BF)) for (start, end, _), part in zip(spans, weights)]
            )
            outs.append(out / total)
            sums_ref[h : h + 1, low:high] = top + jnp.log(total)
        both = outs[0] if len(outs) == 1 else jnp.concatenate(outs, axis=0)
        block[...] = both.T.astype(BF)
        from_clip(grid, at_ref, block, k, out_ref)


def self_backward_kernel(grid, width, at_ref, x_ref, da_ref, sums_ref, out_ref, clip, da_clip, block, acc):
    size = CLIP_LEN // grid.C
    to_clip(grid, at_ref, x_ref, clip)
    to_clip(grid, at_ref, da_ref, da_clip)
    heads = range(width // HEAD)

    def lanes(which, h):
        return slice(which * width + h * HEAD, which * width + (h + 1) * HEAD)

    keys = [clip[:, lanes(1, h)] for h in heads]
    values = [clip[:, lanes(2, h)] for h in heads]
    keys_t = [flip(keys[h]).astype(BF) for h in heads]
    for k in reversed(range(grid.C)):
        low, high = k * size, (k + 1) * size
        dq = []
        for h in heads:
            asks = clip[low:high, lanes(0, h)] * BF(SCALE)
            da = da_clip[low:high, lanes(0, h)]
            spans = causal_spans(low, high)
            sums = sums_ref[h : h + 1, low:high]
            probs = [jnp.exp(causal_scores(keys[h][start:end], asks, masked) - sums) for start, end, masked in spans]
            d_probs = [dot_nt(values[h][start:end], da) for start, end, _ in spans]
            inner = summed([jnp.sum(p * d, axis=0, keepdims=True) for p, d in zip(probs, d_probs)])
            terms = []
            for (start, end, _), p, d in zip(spans, probs, d_probs):
                d_scores = (p * (d - inner)).astype(BF)
                dk = dot_nn(d_scores, asks)
                dv = dot_nn(p.astype(BF), da)
                if k == grid.C - 1:
                    acc[start:end, lanes(0, h)] = dk
                    acc[start:end, lanes(1, h)] = dv
                else:
                    acc[start:end, lanes(0, h)] += dk
                    acc[start:end, lanes(1, h)] += dv
                terms.append(dot_nn(keys_t[h][:, start:end], d_scores))
            dq.append(summed(terms) * SCALE)
        both = dq[0] if len(dq) == 1 else jnp.concatenate(dq, axis=0)
        block[:, :width] = both.T.astype(BF)
        block[:, width:] = acc[low:high, :].astype(BF)
        from_clip(grid, at_ref, block, k, out_ref)


def unit_spec(rows, lanes):
    return pl.BlockSpec((None, rows, lanes), lambda n, *at: (n, 0, 0))


def self_attention(grid, x):
    units, _, width = x.shape
    width //= 3
    size = CLIP_LEN // grid.C
    return pl.pallas_call(
        functools.partial(self_forward_kernel, grid, width),
        grid_spec=pltpu.PrefetchScalarGridSpec(
            num_scalar_prefetch=1,
            grid=(units,),
            in_specs=[unit_spec(CLIP_LEN, 3 * width)],
            out_specs=[unit_spec(CLIP_LEN, width), unit_spec(8, CLIP_LEN)],
            scratch_shapes=[pltpu.VMEM((CLIP_LEN, 3 * width), BF), pltpu.VMEM((size, width), BF)],
        ),
        out_shape=[
            jax.ShapeDtypeStruct((units, CLIP_LEN, width), BF),
            jax.ShapeDtypeStruct((units, 8, CLIP_LEN), F32),
        ],
        compiler_params=pltpu.CompilerParams(vmem_limit_bytes=VMEM_LIMIT),
        cost_estimate=pl.CostEstimate(
            flops=COST * units * width, bytes_accessed=CLIP_LEN * units * width * 8, transcendentals=0
        ),
        name="self_attention",
    )(jnp.stack([grid.i, grid.z]), x)


def self_attention_grad(grid, x, da, sums):
    units, _, width = da.shape
    size = CLIP_LEN // grid.C
    return pl.pallas_call(
        functools.partial(self_backward_kernel, grid, width),
        grid_spec=pltpu.PrefetchScalarGridSpec(
            num_scalar_prefetch=1,
            grid=(units,),
            in_specs=[unit_spec(CLIP_LEN, 3 * width), unit_spec(CLIP_LEN, width), unit_spec(8, CLIP_LEN)],
            out_specs=unit_spec(CLIP_LEN, 3 * width),
            scratch_shapes=[
                pltpu.VMEM((CLIP_LEN, 3 * width), BF),
                pltpu.VMEM((CLIP_LEN, width), BF),
                pltpu.VMEM((size, 3 * width), BF),
                pltpu.VMEM((CLIP_LEN, 2 * width), F32),
            ],
        ),
        out_shape=jax.ShapeDtypeStruct((units, CLIP_LEN, 3 * width), BF),
        compiler_params=pltpu.CompilerParams(vmem_limit_bytes=VMEM_LIMIT),
        cost_estimate=pl.CostEstimate(
            flops=3 * COST * units * width, bytes_accessed=CLIP_LEN * units * width * 16, transcendentals=0
        ),
        name="self_attention_grad",
    )(jnp.stack([grid.i, grid.z]), x, da, sums)


def reorder_kernel(spans, core_ref, x_ref, out_ref):
    for core in range(2):

        @pl.when(core_ref[0] == core)
        def _(core=core):
            out_ref[...] = jnp.concatenate([x_ref[:, low : low + size] for low, size in spans[core]], axis=1)


def reorder(grid, x, back):
    rows, width = x.shape
    size = width // grid.R
    half = width // 2
    if back:
        spans = [[((r % 2 != core) * half + r // 2 * size, size) for r in range(grid.R)] for core in range(2)]
    else:
        spans = [[((2 * i + (core + n) % 2) * size, size) for n in range(2) for i in range(grid.T)] for core in range(2)]
    return pl.pallas_call(
        functools.partial(reorder_kernel, spans),
        grid_spec=pltpu.PrefetchScalarGridSpec(
            num_scalar_prefetch=1,
            grid=(1,),
            in_specs=[pl.BlockSpec((rows, width), lambda n, core: (0, 0))],
            out_specs=pl.BlockSpec((rows, width), lambda n, core: (0, 0)),
        ),
        out_shape=jax.ShapeDtypeStruct((rows, width), x.dtype),
        name="reorder",
    )(grid.core.reshape(1), x)


def own_first(grid, x):
    return reorder(grid, x, False)


def own_last(grid, x):
    return reorder(grid, x, True)


def lanes_of(ref, mats):
    parts = [ref[m] for m in mats]
    return parts[0] if len(parts) == 1 else jnp.concatenate(parts, axis=1)


def columns_kernel(mats, count, kind, *refs):
    pieces, (own_ref, other_ref), rest = refs[:count], refs[count : count + 2], refs[count + 2 :]
    own, other = lanes_of(own_ref, mats), lanes_of(other_ref, mats)
    half = own.shape[0]
    low = 0
    for piece in pieces:
        high = low + piece.shape[0]
        out = dot_nn(piece[:, :half], own) + dot_nn(piece[:, half:], other)
        if kind == "gelu":
            value, slope = gelu_parts(out)
            rest[0][low:high] = value.astype(BF)
            rest[1][low:high] = slope.astype(BF)
        elif kind == "slope":
            rest[1][low:high] = (out * rest[0][low:high].astype(F32)).astype(BF)
        else:
            rest[0][low:high] = out.astype(BF)
        low = high


def whole(array):
    return pl.BlockSpec(array.shape, lambda n: (0,) * array.ndim)


def act_spec(rows, lanes):
    return pl.BlockSpec((None, rows, lanes), lambda n: (n, 0, 0))


def columns_product(pieces, weights, mats, kind="plain", slope=None):
    own, other = weights
    blocks, _, half, wide = own.shape
    lanes = len(mats) * wide
    rows = sum(p.shape[0] for p in pieces)
    extra = [] if slope is None else [slope]
    outs = 2 if kind == "gelu" else 1
    shape = jax.ShapeDtypeStruct((blocks, rows, lanes), BF)
    first, picked = (mats[0], 1) if len(mats) == 1 else (0, own.shape[1])
    spec = pl.BlockSpec((None, picked) + own.shape[2:], lambda n: (n, first, 0, 0))
    result = pl.pallas_call(
        functools.partial(columns_kernel, (0,) if len(mats) == 1 else mats, len(pieces), kind),
        grid=(blocks,),
        in_specs=[whole(p) for p in pieces] + [spec, spec] + [act_spec(rows, lanes)] * len(extra),
        out_specs=[act_spec(rows, lanes)] * outs,
        out_shape=[shape] * outs,
        compiler_params=pltpu.CompilerParams(vmem_limit_bytes=VMEM_LIMIT),
        cost_estimate=pl.CostEstimate(flops=4 * half * rows * lanes * blocks, bytes_accessed=4 * half * lanes * blocks, transcendentals=0),
        name="columns_" + kind,
    )(*pieces, own, other, *extra)
    return result if outs > 1 else result[0]


def rows_kernel(mats, low, high, act_ref, own_ref, other_ref, *outs):
    blocks = act_ref.shape[0]
    acts = [act_ref[n, low:high] for n in range(blocks)]
    half = own_ref.shape[2]
    for cols, ref in ((slice(0, half), own_ref), (slice(half, 2 * half), other_ref)):
        parts = [lanes_of(ref.at[n], mats) for n in range(blocks)]
        if parts[0].shape[1] < 256:
            total = dot_nt(jnp.concatenate(acts, axis=1), jnp.concatenate(parts, axis=1))
        else:
            total = dot_nt(acts[0], parts[0])
            for act, part in zip(acts[1:], parts[1:]):
                total = total + dot_nt(act, part)
        at = 0
        for out in outs:
            out[:, cols] = total[at : at + out.shape[0]].astype(out.dtype)
            at += out.shape[0]


def rows_product(act, weights, mats, low, high, shapes):
    own, other = weights
    blocks, _, half, _ = own.shape
    lanes = act.shape[2]
    first, count = (mats[0], 1) if len(mats) == 1 else (0, own.shape[1])
    spec = pl.BlockSpec((blocks, count) + own.shape[2:], lambda n: (0, first, 0, 0))
    return pl.pallas_call(
        functools.partial(rows_kernel, (0,) if len(mats) == 1 else mats, low, high),
        grid=(1,),
        in_specs=[whole(act), spec, spec],
        out_specs=[whole(s) for s in shapes],
        out_shape=shapes,
        compiler_params=pltpu.CompilerParams(vmem_limit_bytes=VMEM_LIMIT),
        cost_estimate=pl.CostEstimate(
            flops=4 * half * (high - low) * lanes * blocks, bytes_accessed=4 * half * lanes * blocks, transcendentals=0
        ),
        name="rows",
    )(act, own, other)


def rows_top(grid, act, weights, mats):
    rows = act.shape[1] // grid.T
    shapes = [jax.ShapeDtypeStruct((rows // 2, 2 * weights[0].shape[2]), BF)] * 2
    return list(rows_product(act, weights, mats, rows * (grid.T - 1), rows * grid.T, shapes))


def rows_rest(grid, act, weights, mats):
    rows = act.shape[1] // grid.T
    shapes = [jax.ShapeDtypeStruct((rows, 2 * weights[0].shape[2]), F32)] * (grid.T - 1)
    return list(rows_product(act, weights, mats, 0, rows * (grid.T - 1), shapes))


def rows_terms(grid, act, weights, mats):
    top = rows_top(grid, act, weights, mats)
    return top, rows_rest(grid, after(act, top), weights, mats)


def grads_kernel(count, *refs):
    pieces, y_ref, keep_ref, send_ref, turned = refs[:count], refs[count], refs[count + 1], refs[count + 2], refs[count + 3]
    half = keep_ref.shape[0]

    @pl.when(pl.program_id(0) == 0)
    def _():
        low = 0
        for piece in pieces:
            high = low + piece.shape[0]
            turned[:, low:high] = piece[...].T
            low = high

    y = y_ref[...]
    keep_ref[...] = dot_nn(turned[:half], y).astype(BF)
    send_ref[...] = dot_nn(turned[half:], y).astype(BF)


def weight_grads(pieces, y):
    blocks, rows, lanes = y.shape
    width = pieces[0].shape[1]
    half = width // 2
    shape = jax.ShapeDtypeStruct((blocks, half, lanes), BF)
    return pl.pallas_call(
        functools.partial(grads_kernel, len(pieces)),
        grid=(blocks,),
        in_specs=[whole(p) for p in pieces] + [act_spec(rows, lanes)],
        out_specs=[act_spec(half, lanes)] * 2,
        out_shape=[shape] * 2,
        scratch_shapes=[pltpu.VMEM((width, rows), BF)],
        compiler_params=pltpu.CompilerParams(vmem_limit_bytes=VMEM_LIMIT),
        cost_estimate=pl.CostEstimate(flops=4 * half * rows * lanes * blocks, bytes_accessed=4 * half * lanes * blocks, transcendentals=0),
        name="weight_grads",
    )(*pieces, y)


def cross_scores(keys, asks):
    scores = dot_nt(keys, asks)
    top = jnp.max(scores, axis=0, keepdims=True)
    weight = jnp.exp(scores - top)
    return weight / jnp.sum(weight, axis=0, keepdims=True)


def cross_forward_kernel(q_ref, k_ref, v_ref, out_ref):
    for low in range(0, q_ref.shape[1], 2 * HEAD):
        pair = []
        for at in (slice(low, low + HEAD), slice(low + HEAD, low + 2 * HEAD)):
            probs = cross_scores(k_ref[:, at], q_ref[:, at] * BF(SCALE)).astype(BF)
            pair.append(dot_nn(flip(v_ref[:, at]).astype(BF), probs))
        out_ref[:, low : low + 2 * HEAD] = jnp.concatenate(pair, axis=0).T.astype(BF)


def cross_backward_kernel(q_ref, k_ref, v_ref, dc_ref, dq_ref, dk_ref, dv_ref):
    for low in range(0, q_ref.shape[1], 2 * HEAD):
        pair, dk, dv = [], [], []
        for at in (slice(low, low + HEAD), slice(low + HEAD, low + 2 * HEAD)):
            asks = q_ref[:, at] * BF(SCALE)
            probs = cross_scores(k_ref[:, at], asks)
            d_probs = dot_nt(v_ref[:, at], dc_ref[:, at])
            inner = jnp.sum(probs * d_probs, axis=0, keepdims=True)
            d_scores = (probs * (d_probs - inner)).astype(BF)
            dk.append(dot_nn(d_scores, asks))
            dv.append(dot_nn(probs.astype(BF), dc_ref[:, at]))
            pair.append(dot_nn(flip(k_ref[:, at]).astype(BF), d_scores) * SCALE)
        at = slice(low, low + 2 * HEAD)
        dq_ref[:, at] = jnp.concatenate(pair, axis=0).T.astype(BF)
        dk_ref[:, at] = jnp.concatenate(dk, axis=1)
        dv_ref[:, at] = jnp.concatenate(dv, axis=1)


def cross_call(kernel, name, arrays, outs):
    width = arrays[0].shape[1]
    lanes = 512 if width % 512 == 0 else width

    def spec(rows):
        return pl.BlockSpec((rows, lanes), lambda n: (0, n))

    return pl.pallas_call(
        kernel,
        grid=(width // lanes,),
        in_specs=[spec(a.shape[0]) for a in arrays],
        out_specs=[spec(rows) for rows, _ in outs],
        out_shape=[jax.ShapeDtypeStruct((rows, width), kind) for rows, kind in outs],
        compiler_params=pltpu.CompilerParams(vmem_limit_bytes=VMEM_LIMIT),
        cost_estimate=pl.CostEstimate(
            flops=arrays[0].shape[0] * arrays[1].shape[0] * width * 20, bytes_accessed=2**22, transcendentals=0
        ),
        name=name,
    )(*arrays)


def cross_attention(queries, keys, values):
    return cross_call(cross_forward_kernel, "cross_attention", [queries, keys, values], [(queries.shape[0], BF)])[0]


def cross_attention_grad(queries, keys, values, grad_out):
    outs = [(queries.shape[0], BF), (keys.shape[0], F32), (keys.shape[0], F32)]
    return cross_call(cross_backward_kernel, "cross_attention_grad", [queries, keys, values, grad_out], outs)


def head_units(grid, width):
    heads = width // HEAD
    per_unit = -(-heads // grid.T)
    assert heads % per_unit == 0
    return heads // per_unit, per_unit * HEAD


def self_slots(grid, mats):
    units, wide = head_units(grid, mats[0].shape[1])
    both = jnp.stack(mats)
    lows = [jnp.minimum((s - grid.z - 1) % grid.T, units - 1) * wide for s in range(grid.T)]
    return jnp.stack([lax.dynamic_slice_in_dim(both, low, wide, axis=2) for low in lows])


def by_matrix(moved):
    sources, count, rows, wide = moved.shape
    return moved.transpose(1, 0, 2, 3).reshape(count, sources * rows, wide)


def self_weights(grid, slots, units):
    half = jnp.stack(
        [lax.dynamic_index_in_dim(slots, (grid.i - 1 - m) % grid.T, 0, keepdims=False) for m in range(units)]
    )
    return half, grid.core_swap(half)


def core_sum(grid, keep, send, mid):
    got = tied(grid.core_swap(send), mid)
    return (keep.astype(F32) + got.astype(F32)).astype(BF)


def self_grad_slots(grid, pairs, mid):
    half = jnp.concatenate([core_sum(grid, *pair, mid) for pair in pairs], axis=2)
    half = jnp.concatenate([half, jnp.zeros((grid.C - half.shape[0],) + half.shape[1:], BF)], axis=0)
    return jnp.stack(
        [lax.dynamic_index_in_dim(half, (grid.i - c - 1) % grid.T, 0, keepdims=False) for c in range(grid.C)]
    )


def self_grad_blocks(grid, moved, units):
    wide = moved.shape[2] // 4
    mine = [lax.dynamic_index_in_dim(moved, (grid.z + 1 + m) % grid.T, 0, keepdims=False) for m in range(units)]
    return [
        jnp.concatenate([part[:, n * wide : (n + 1) * wide] for part in mine], axis=1).astype(F32) for n in range(4)
    ]


def hidden_slots(grid, mats):
    rows, width = mats[0].shape
    count = len(mats)
    return jnp.stack(mats).reshape(count, rows, grid.T, width // grid.T).transpose(2, 0, 1, 3)


def hidden_gathered(moved, n, token):
    sources, _, rows, wide = moved.shape
    return lax.all_gather(after(moved[:, n].reshape(1, sources * rows, wide), token), "col", axis=0)


def with_other(grid, own):
    return own, grid.core_swap(own)


def hidden_grad_slots(grid, pairs, mid):
    return jnp.concatenate([core_sum(grid, *pair, mid) for pair in pairs], axis=2)


def col_sum(slots):
    return lax.psum_scatter(slots, "col", scatter_dimension=0)


def hidden_grad_blocks(grid, moved, count):
    rows, wide = moved.shape[1], moved.shape[2] // count
    return [
        moved[:, :, n * wide : (n + 1) * wide].transpose(1, 0, 2).reshape(rows, -1).astype(F32) for n in range(count)
    ]


def cross_columns(grid, blocks):
    _, count, rows, width = blocks.shape
    return blocks.transpose(1, 2, 0, 3).reshape(count * rows, grid.C * width)


def cross_weights(grid, pieces, count):
    half = jnp.stack(grid.natural(pieces))
    width = half.shape[2]
    half = half.reshape(grid.T, count, -1, width).transpose(1, 0, 2, 3).reshape(count, -1, width)
    other = grid.core_swap(half)
    return [joined([half[n], other[n]]) for n in range(count)]


def cross_core_sum(grid, lows, mid):
    edge = lows[0].shape[0] // 2
    return [core_sum(grid, low[:edge], low[edge:], mid) for low in lows]


def cross_terms(grid, halves, rows, width):
    halves = [half.reshape(grid.T, rows, grid.C * width) for half in halves]

    def term(d):
        return joined([lax.dynamic_index_in_dim(half, grid.i ^ d, 0, keepdims=False) for half in halves])

    order = grid.order()
    top = term(order[-1])
    size = top.shape[0] // 2
    return [top[:size], top[size:]], [term(d).astype(F32) for d in order[:-1]]


def cross_blocks(grid, own, rows, width):
    return own.astype(BF).reshape(-1, rows, grid.C, width).transpose(2, 0, 1, 3)


def text_columns(grid, text):
    _, own, width = text.shape
    parts = text.reshape(own, grid.R, width // grid.R).transpose(1, 0, 2)
    parts = grid.row_a2a(parts)
    pieces = [parts] + [
        lax.ppermute(parts, "col", [(c, c ^ d) for c in range(grid.C)]) for d in range(1, grid.C)
    ]
    stacked = jnp.stack(pieces)
    order = [lax.dynamic_index_in_dim(stacked, grid.z ^ c, 0, keepdims=False) for c in range(grid.C)]
    return jnp.stack(order, axis=1).reshape(-1, width // grid.R)


def text_parts(grid, columns, mats):
    count, rows, width = mats.shape
    own = columns.shape[0] // (grid.R * grid.C)
    part = product(columns, mats.transpose(1, 0, 2).reshape(rows, count * width)).astype(BF)
    part = part.reshape(grid.T, 2, grid.C, own, count * width).transpose(2, 1, 0, 3, 4)
    return grid.row_a2a(part.reshape(grid.R, grid.T * own, count * width))


def text_shared(grid, moved):
    own = moved.shape[1] // grid.T
    summed = jnp.sum(moved.astype(F32), axis=0).astype(BF).reshape(grid.T, own, moved.shape[2])
    sent = grid.picked(list(summed), [grid.z ^ e for e in range(grid.C)])
    return [grid.col_swap(sent[e], e) for e in range(grid.C)]


def text_states_of(grid, got, count):
    own, width = got[0].shape[0], got[0].shape[1] // count
    blocks = jnp.stack(grid.picked(got, [grid.z ^ c for c in range(grid.C)]))
    mine = blocks.reshape(grid.C, own, count, width).transpose(1, 2, 0, 3)
    mine = mine.reshape(own, count * grid.C * width)
    full = joined(flat(grid.gather(mine)))
    return full.reshape(-1, count, grid.C * width)


def text_begin(grid, grads):
    own = grads.shape[0] // grid.T
    pieces = grads.reshape(grid.T, own, -1)
    top = pieces[grid.T - 1].astype(BF)
    return grid.scatter_begin([top[: own // 2], top[own // 2 :]]), [pieces[n] for n in range(grid.T - 1)]


def text_backward(grid, mine, width):
    own = mine.shape[0]
    mine = mine.reshape(own, -1, grid.C, width).transpose(2, 0, 1, 3)
    moved = grid.col_a2a(mine)
    other = grid.core_swap(moved)
    pair = jnp.stack(
        [jnp.where(grid.core == 0, moved, other), jnp.where(grid.core == 0, other, moved)], axis=1
    )
    shape = pair.shape
    flat = pair.reshape(shape[0] * 2, -1)
    full = jnp.stack(grid.natural(grid.gather(flat)), axis=1)
    return full.reshape(-1, shape[3], width)


def text_out(grid, part):
    own = part.shape[0] // (grid.R * grid.C)
    cols = part.shape[1]
    parts = part.astype(BF).reshape(grid.R, grid.C, own, cols).transpose(1, 0, 2, 3)
    moved = grid.col_a2a(parts).astype(F32)
    summed = jnp.sum(moved, axis=0).astype(BF)
    moved = grid.row_a2a(summed)
    return moved.transpose(1, 0, 2).reshape(1, own, grid.R * cols).astype(F32)


def shards(
    grid,
    inputs,
    text_states,
    cotangent,
    norm_gains,
    norm_shifts,
    self_query,
    self_key,
    self_value,
    self_out,
    cross_query,
    cross_key,
    cross_value,
    cross_out,
    mlp_up,
    mlp_down,
):
    grid.at()
    last = LAYERS - 1
    rows, width = self_query.shape[1:]
    units, _ = head_units(grid, width)

    self_parts = [self_slots(grid, [w[n] for w in (self_query, self_key, self_value, self_out)]) for n in range(LAYERS)]
    hidden_parts = [hidden_slots(grid, [mlp_up[n], mlp_down[n]]) for n in range(LAYERS)]
    self_moved = [None] * LAYERS
    hidden_moved = [None] * LAYERS
    self_full = [None] * LAYERS
    self_moved[0] = grid.plane_a2a(self_parts[0])
    sent = by_matrix(self_moved[0])
    cross_parts = [jnp.stack([cross_query[n], cross_out[n]]) for n in range(LAYERS)]
    tokens = grid.tokens_in(jnp.concatenate([inputs, cotangent.astype(BF)], axis=1))
    tokens, sent = meet(tokens, sent)
    text_cols = text_columns(grid, after(text_states, tokens))
    gradient = tokens[:, inputs.shape[1] :]
    tokens = tokens[:, : inputs.shape[1]]
    self_full[0] = lax.all_gather(sent, "col", axis=0)
    residual = own_first(grid, tokens).astype(F32)
    norm_rows = after(jnp.concatenate([norm_gains, norm_shifts], axis=1), tokens)
    norm_rows = own_first(grid, norm_rows.reshape(-1, norm_rows.shape[2])).reshape(norm_rows.shape)
    gains, shifts = norm_rows[:, :3], norm_rows[:, 3:]
    text_mats = jnp.stack([mat for n in range(LAYERS) for mat in (cross_key[n], cross_value[n])])

    kept = [dict() for _ in range(LAYERS)]
    w_self = [None] * LAYERS
    w_cross = [None] * LAYERS
    w_hidden = [None] * LAYERS
    for n in range(LAYERS):
        k = kept[n]
        k["normed_one"], k["inv_one"], low_one = norm_forward(residual, gains[n, 0], shifts[n, 0])
        near_one = grid.gather_begin(low_one)
        if n == 0:
            hidden_moved[0] = grid.plane_a2a(after(hidden_parts[0], near_one))
            text_moved = text_parts(grid, after(text_cols, near_one), text_mats)
        full_one = flat(grid.gather_end(near_one))
        if n == 0:
            (self_full[0], full_one), (text_sent, hidden_moved[0]) = meet(
                (self_full[0], full_one), (text_shared(grid, text_moved), hidden_moved[0])
            )
            cross_full = lax.all_gather(after(cross_parts[0], sent), "col", axis=0)
        else:
            self_full[n] = after(self_full[n], residual)
        k["full_one"] = full_one
        w_self[n] = self_weights(grid, self_full[n], units)
        k["qkv"] = columns_product(full_one, w_self[n], (0, 1, 2))
        k["attn_low"], k["sums_self"] = self_attention(grid, k["qkv"])
        if n > 0:
            next_near = grid.gather_begin(cross_columns(grid, after(cross_full, full_one)))
            k["attn_low"], next_near = meet(k["attn_low"], next_near)
            w_cross[n] = cross_weights(grid, grid.gather_end(next_near), 2)
        up_full = hidden_gathered(hidden_moved[n], 0, full_one if n == 0 else hidden_moved[n])
        down_full = hidden_gathered(hidden_moved[n], 1, k["qkv"])
        top, rest = rows_terms(grid, k["attn_low"], w_self[n], (3,))
        fill = []
        if n == 0:
            next_near = grid.gather_begin(cross_columns(grid, after(cross_full, k["qkv"])))
            rest, next_near = meet(rest, next_near)
            w_cross[0] = cross_weights(grid, grid.gather_end(next_near), 2)
        if n == 0:
            text_all = text_states_of(grid, tied(text_sent, top), 2 * LAYERS)
        added, _ = grid.scatter(top, rest)
        residual = residual + added
        w_up = with_other(grid, after(up_full, residual))
        before_cross = residual
        k["text"] = [text_all[:, 2 * n + side] for side in range(2)]
        k["normed_two"], k["inv_two"], k["low_two"] = norm_forward(residual, gains[n, 1], shifts[n, 1])
        k["cross_queries"] = product(k["low_two"], w_cross[n][0]).astype(BF)
        k["cross_low"] = cross_attention(k["cross_queries"], *k["text"])
        residual = residual + product_nt(k["cross_low"], w_cross[n][1])
        k["normed_three"], k["inv_three"], low_three = norm_forward(residual, gains[n, 2], shifts[n, 2])
        if n < last:
            w_down = with_other(grid, after(down_full, before_cross))
            w_down, low_three = meet(w_down, low_three)
            sent = by_matrix(grid.plane_a2a(after(self_parts[n + 1], before_cross)))
            low_three, sent = meet(low_three, sent)
            self_full[n + 1] = lax.all_gather(sent, "col", axis=0)
            cross_full = lax.all_gather(after(cross_parts[n + 1], sent), "col", axis=0)
        if n == last:
            low_three, next_near = meet(low_three, grid.gather_begin(after(gradient, before_cross)))
        k["full_three"] = flat(grid.gather(low_three))
        if n < last:
            hidden_moved[n + 1] = grid.plane_a2a(after(hidden_parts[n + 1], low_three))
            k["full_three"], hidden_moved[n + 1] = meet(k["full_three"], hidden_moved[n + 1])
        k["hidden_low"], k["hidden_slope"] = columns_product(k["full_three"], w_up, (0,), "gelu")
        if n == last:
            w_down = with_other(grid, after(down_full, k["hidden_low"]))
        w_hidden[n] = (w_up, w_down)
        if n < last:
            top, rest = rows_terms(grid, k["hidden_low"], w_hidden[n][1], (0,))
            gradient = own_first(grid, after(gradient, rest)) if n == 0 else gradient
            added, gradient = grid.scatter(top, rest, gradient)
            residual = residual + added
        else:
            dy_three = flat(grid.gather_end(next_near))
            gradient = gradient.astype(F32)

    before_last = residual
    hidden_sums = [None] * LAYERS
    self_sums = [None] * LAYERS
    cross_sums = [None] * LAYERS
    text_grads = [None] * LAYERS
    norms = [None] * LAYERS
    fill = []
    for n in range(last, -1, -1):
        k = kept[n]
        w_up, w_down = w_hidden[n]
        if n < last:
            sent, slots = meet(gradient.astype(BF), self_slots_grad)
            self_sums[n + 1] = col_sum(slots)
            cross_terms_late = cross_terms(grid, cross_core_sum(grid, cross_lows, sent), rows, width)
            dy_three, cross_terms_late = meet(flat(grid.gather(sent)), cross_terms_late)
        if n == last:
            late_top, late_rest = rows_terms(grid, k["hidden_low"], w_down, (0,))
            late_state = grid.scatter_begin(late_top)
            dy_three, late_rest = meet(dy_three, late_rest)
        d_pre = columns_product(dy_three, w_down, (0,), "slope", k["hidden_slope"])
        top, rest = rows_terms(grid, d_pre, w_up, (0,))
        state = grid.scatter_begin(top)
        if n < last:
            (state, rest), cross_state = meet((state, rest), grid.scatter_begin(cross_terms_late[0]))
        hidden_pairs = [
            weight_grads(after(k["full_three"], state), d_pre),
            weight_grads(after(dy_three, state), k["hidden_low"]),
        ]
        if n == last:
            late_state = tied(late_state, rest)
        grad_normed, hidden_pairs = grid.scatter_end(state, rest, hidden_pairs)
        grad_res, gain_three, shift_three = norm_backward(grad_normed, k["normed_three"], k["inv_three"], gains[n, 2])
        gradient = gradient + grad_res
        if n < last:
            gradient, hidden_sums[n + 1] = meet(gradient, hidden_sums[n + 1])
        before_cross = gradient
        if n == last:
            late_sum, _ = grid.scatter_end(tied(late_state, gradient), late_rest)
        dy_two = gradient.astype(BF)
        d_cross = product(dy_two, w_cross[n][1]).astype(BF)
        d_cquery, d_ckey, d_cvalue = cross_attention_grad(k["cross_queries"], *k["text"], d_cross)
        grad_normed = product_nt(d_cquery, w_cross[n][0])
        text_grads[n] = jnp.concatenate([d_ckey, d_cvalue], axis=1)
        grad_res, gain_two, shift_two = norm_backward(grad_normed, k["normed_two"], k["inv_two"], gains[n, 1])
        gradient = gradient + grad_res
        sent = gradient.astype(BF)
        if n == last:
            sent, late_sum = meet(sent, late_sum)
            fill = own_last(grid, (before_last + late_sum).astype(BF))
        else:
            sent, hidden_slots_grad = meet(sent, hidden_grad_slots(grid, hidden_pairs, grad_normed))
            hidden_sums[n] = col_sum(hidden_slots_grad)
            fill = ()
        dy_one, fill = meet(flat(grid.gather(sent)), fill)
        if n == last:
            output = grid.tokens_out_begin(fill)
        d_attn = columns_product(dy_one, w_self[n], (3,))
        d_qkv = self_attention_grad(grid, k["qkv"], d_attn, k["sums_self"])
        if n == 0:
            text_state, text_rest = text_begin(grid, after(jnp.concatenate(text_grads, axis=1), dy_one))
            d_qkv, (text_state, self_sums[1:]) = meet(d_qkv, (text_state, self_sums[1:]))
        if n == last:
            d_qkv, output = meet(d_qkv, output)
            output = grid.tokens_out_end(output)

        def cross_products(token):
            return [
                product_tn(after(k["low_two"], token), d_cquery).astype(BF),
                product_tn(after(dy_two, token), k["cross_low"]).astype(BF),
            ]

        if n > 0:
            top, rest = rows_terms(grid, d_qkv, w_self[n], (0, 1, 2))
            state = grid.scatter_begin(top)
            qkv_pair = weight_grads(after(k["full_one"], state), d_qkv)
            out_pair = weight_grads(after(dy_one, state), k["attn_low"])
            fill = [qkv_pair, out_pair, output, hidden_grad_slots(grid, hidden_pairs, state)]
        else:
            qkv_pair = weight_grads(k["full_one"], d_qkv)
            out_pair = weight_grads(dy_one, after(k["attn_low"], d_qkv))
            text_mine = grid.scatter_end(text_state, text_rest)[0].astype(BF)
            own, _ = grid.scatter_end(tied(cross_state, dy_one), cross_terms_late[1])
            out_pair, (text_mine, own) = meet(out_pair, (text_mine, cross_blocks(grid, own, rows, width)))
            cross_sums[n + 1] = own
            top = rows_top(grid, after(d_qkv, [qkv_pair, out_pair]), w_self[n], (0, 1, 2))
            state = grid.scatter_begin(top)
            top, slots = meet(top, self_grad_slots(grid, [qkv_pair, out_pair], out_pair))
            self_sums[0] = col_sum(slots)
            rest = rows_rest(grid, after(d_qkv, slots), w_self[n], (0, 1, 2))
            fill = cross_terms(grid, cross_core_sum(grid, cross_products(state), state), rows, width)
        grad_normed, fill = grid.scatter_end(state, rest, fill)
        if n == 0:
            cross_state, cross_last = grid.scatter_begin(fill[0]), fill[1]
        if n > 0:
            qkv_pair, out_pair, output, hidden_slots_grad = fill
            cross_lows = cross_products(grad_normed)
            hidden_sums[n] = col_sum(hidden_slots_grad)
            self_slots_grad = self_grad_slots(grid, [qkv_pair, out_pair], grad_normed)
        grad_res, gain_one, shift_one = norm_backward(grad_normed, k["normed_one"], k["inv_one"], gains[n, 0])
        gradient = gradient + grad_res
        norms[n] = jnp.stack([gain_one, gain_two, gain_three, shift_one, shift_two, shift_three])

    gradient, cross_state = meet(gradient.astype(BF), cross_state)
    input_grad = grid.tokens_out_begin(own_last(grid, gradient))
    text_full = text_backward(grid, after(text_mine, grad_normed), width)
    own, _ = grid.scatter_end(cross_state, cross_last)
    text_full, cross_sums[0] = meet(text_full, cross_blocks(grid, own, rows, width))
    cross_all, self_sums[0] = meet(jnp.concatenate(cross_sums, axis=1), self_sums[0])
    cross_all = col_sum(cross_all).astype(F32)
    cross_out_grads = [cross_all[2 * n : 2 * n + 2] for n in range(LAYERS)]
    text_weights = [[product_tn(text_cols, text_full[:, 2 * n + side]) for side in range(2)] for n in range(LAYERS)]
    text_part = 0.0
    for n in range(LAYERS):
        for side, mats in enumerate((cross_key, cross_value)):
            text_part = text_part + product_nt(text_full[:, 2 * n + side], mats[n])
    early = [hidden_sums[n] for n in range(1, LAYERS)] + [self_sums[n] for n in range(1, LAYERS)]
    widths = [value.shape[1] for value in early]
    moved = jnp.concatenate([value.reshape(grid.T, rows, value.shape[1]) for value in early], axis=2)
    moved = grid.plane_a2a(after(moved, grad_normed))
    input_grad, (moved, hidden_sums[0]) = meet(input_grad, (moved, hidden_sums[0]))
    input_grad = grid.tokens_out_end(input_grad).astype(F32)
    parts = [moved[:, :, sum(widths[:m]) : sum(widths[: m + 1])] for m in range(len(early))]
    first = [grid.plane_a2a(value[0].reshape(grid.T, rows, value[0].shape[1])) for value in (hidden_sums, self_sums)]
    text_part, first = meet(text_part, first)
    text_grad = text_out(grid, text_part)
    hidden_out = [hidden_grad_blocks(grid, part, 2) for part in [first[0]] + parts[: LAYERS - 1]]
    self_out_grads = [self_grad_blocks(grid, part, units) for part in [first[1]] + parts[LAYERS - 1 :]]
    totals = grid.total(own_last(grid, jnp.concatenate(norms, axis=0))).reshape(LAYERS, 6, -1)
    gains_sum, shifts_sum = totals[:, :3], totals[:, 3:]

    def both(values, slot):
        return jnp.stack([values[n][slot] for n in range(LAYERS)])

    return (
        output.astype(F32),
        input_grad,
        text_grad,
        gains_sum,
        shifts_sum[:, 1:],
        shifts_sum[:, 0],
        both(self_out_grads, 0),
        both(self_out_grads, 1),
        both(self_out_grads, 2),
        both(self_out_grads, 3),
        both(cross_out_grads, 0),
        both(text_weights, 0),
        both(text_weights, 1),
        both(cross_out_grads, 1),
        both(hidden_out, 0),
        both(hidden_out, 1),
    )


def solution(mesh):
    grid = Grid(mesh)
    tokens = P(("row", "col"), None)
    text = P("row", "col", None)
    block = P(None, "row", "col")
    in_specs = (tokens, text, tokens, P(), P()) + (block,) * 10
    out_specs = (tokens, tokens, text, P(), P(), P()) + (block,) * 10

    def run(*args):
        return shards(grid, *args)

    return jax.shard_map(run, mesh=mesh, in_specs=in_specs, out_specs=out_specs, check_vma=False)
```
